128 devices in a mesh: expert: 64 (over z_hi, x, y, core), tensor: 2 (over z_lo).
Axes of the slice: x: 4, y: 4, z: 4 (z_hi: 2, z_lo: 2; z = z_hi * 2 + z_lo), core: 2. Of those that a mesh axis runs over, the one named last changes fastest.
Arguments:
- tokens: bfloat16 [32768, 768], P('expert'), may hold values from -6 to 6
- routes: int32 [32768, 2], P('expert'), may hold values from 0 to 15, all different within a row; in each aligned block of 512 rows (0 to 511, 512 to 1023, ...) at most 80 rows name the same one
- gain_one: float32 [768], replicated, may hold values from 0.5 to 1.5
- w_query: bfloat16 [768, 768], P(None, 'tensor'), may hold values from -0.21875 to 0.21875
- w_key: bfloat16 [768, 768], P(None, 'tensor'), may hold values from -0.21875 to 0.21875
- w_value: bfloat16 [768, 768], P(None, 'tensor'), may hold values from -0.21875 to 0.21875
- w_output: bfloat16 [768, 768], P('tensor'), may hold values from -3 to 3
- gain_two: float32 [768], replicated, may hold values from 0.5 to 1.5
- w_router: bfloat16 [768, 16], replicated, may hold values from -0.15625 to 0.15625
- shared_gate: bfloat16 [768, 2048], P(None, 'tensor'), may hold values from -0.21875 to 0.21875
- shared_up: bfloat16 [768, 2048], P(None, 'tensor'), may hold values from -0.21875 to 0.21875
- shared_down: bfloat16 [2048, 768], P('tensor'), may hold values from -0.125 to 0.125
- expert_gate: bfloat16 [64, 768, 512], P('expert', None, 'tensor'), may hold values from -0.21875 to 0.21875
- expert_up: bfloat16 [64, 768, 512], P('expert', None, 'tensor'), may hold values from -0.21875 to 0.21875
- expert_down: bfloat16 [64, 512, 768], P('expert', 'tensor'), may hold values from -0.125 to 0.125
- cotangent: bfloat16 [32768, 768], P('expert'), may hold values from -6 to 6
Outputs:
- block_out: bfloat16 [32768, 768], P('expert')
- grad_tokens: float32 [32768, 768], P('expert')
- grad_gain_one: float32 [768], replicated
- grad_w_query: float32 [768, 768], P(None, 'tensor')
- grad_w_key: float32 [768, 768], P(None, 'tensor')
- grad_w_value: float32 [768, 768], P(None, 'tensor')
- grad_w_output: float32 [768, 768], P('tensor')
- grad_gain_two: float32 [768], replicated
- grad_router: float32 [768, 16], replicated
- grad_shared_gate: float32 [768, 2048], P(None, 'tensor')
- grad_shared_up: float32 [768, 2048], P(None, 'tensor')
- grad_shared_down: float32 [2048, 768], P('tensor')
- grad_expert_gate: float32 [64, 768, 512], P('expert', None, 'tensor')
- grad_expert_up: float32 [64, 768, 512], P('expert', None, 'tensor')
- grad_expert_down: float32 [64, 512, 768], P('expert', 'tensor')
The draws below stay inside these ranges and needn't reach their ends.
Inputs may be any that keep to these rules, and one draw needn't show every extreme that they name: `routes`: in each device's block of 512 rows no expert is named by more than 80 rows, a bound that some block reaches; the 2 entries of a row differ, and every expert is named somewhere.
All inputs are finite; a program needn't handle non-finite values.
Results may differ from the reference program's by a relative error of at most 0.02.
Values may be sent and summed in bfloat16 or wider, within the bound.
No kernel may reach another device: no remote copies, remote signals or barrier semaphores. Data moves between devices by JAX's collectives and lax.ppermute only.
A program may use at most 256 MiB of HBM per device.

```python
import math
import jax
import jax.numpy as jnp
import numpy as np
from jax import lax

D = 768
HEADS = 12
HEAD_DIM = 64
FF = 2048
TOP = 2
EXPERTS = 16
SHARED_FF = 2048
BLOCK = 256
TOK_DEV = 512
TOKENS = 32768
SPLIT = 4
SEQ_LEN = 2048
CAP = 80
N_EXPERT = 64


def shard_levels(rng, extent, cuts, smallest, largest):
    def one(position, shards_of):
        steps = jax.random.uniform(jax.random.fold_in(jax.random.fold_in(rng, 6), position), (shards_of,), jnp.float32, smallest / len(cuts), largest / len(cuts))
        return jnp.repeat(jnp.exp(steps), extent[position] // shards_of).reshape((-1,) + (1,) * (len(extent) - position - 1))

    factor_of = one(*cuts[0])
    for cut in cuts[1:]:
        factor_of = factor_of * one(*cut)
    return factor_of


def assign_block(rng, own, number, rows, number_of, top, most, lean):
    ranking = jax.random.permutation(rng, number_of)
    crowded, ordinary = portions_of(number_of, rows * top, most, lean, True), portions_of(number_of, rows * top, most, lean, False)
    places = jnp.arange(number_of)

    def named(sizes, rotation):
        used = int((sizes > 0).sum())
        fixed = max(1, used // 4)
        passed = fixed + (places - fixed + rotation * (used - fixed)) % max(1, number_of - fixed)
        return jnp.zeros((number_of,), jnp.int32).at[ranking[jnp.where(places < fixed, places, passed)]].set(jnp.asarray(sizes, jnp.int32))

    sizes = jnp.where(number % 4 == 0, named(crowded, number // 4), named(ordinary, number - number // 4 - 1))
    mixed = jax.random.permutation(jax.random.fold_in(own, 3), number_of)
    source_of, taker = mixed[0:number_of // 2 * 2:2], mixed[1:number_of // 2 * 2:2]
    margin = jnp.minimum(sizes[source_of] - 1, most - sizes[taker]) // 2
    margin = jnp.where((source_of == ranking[0]) | (taker == ranking[0]) | (sizes[taker] == 0), 0, jnp.maximum(margin, 0))
    passed = jax.random.randint(jax.random.fold_in(own, 4), (number_of // 2,), 0, 1 << 20) % (margin + 1)
    sizes = sizes.at[source_of].add(-passed).at[taker].add(passed)
    items = jnp.searchsorted(jnp.cumsum(sizes), jnp.arange(rows * top), side="right").astype(jnp.int32)
    grid = items.reshape(top, rows).T
    grid = grid[jax.random.permutation(jax.random.fold_in(own, 1), rows)]
    rotation = jax.random.randint(jax.random.fold_in(own, 2), (rows, 1), 0, top)
    return jnp.take_along_axis(grid, (jnp.arange(top)[None, :] + rotation) % top, axis=1)


def portions_of(number_of, total, most, slope, full):
    loads = [(1 << 20) // math.isqrt(rank ** slope) + 1 for rank in range(1, number_of + 1)]
    largest = most if full else min(most, max(-(-total // number_of), total * loads[0] // sum(loads)))
    least = 1 if total - largest >= number_of - 1 else 0
    counts, spare = [largest] + [least] * (number_of - 1), total - largest - least * (number_of - 1)
    while spare > 0:
        free = [i for i in range(1, number_of) if counts[i] < largest] or [i for i in range(1, number_of) if counts[i] < most]
        mass, remaining = sum([loads[i] for i in free]), spare
        for i in free:
            extra = min(most - counts[i], max(1, remaining * loads[i] // mass), spare)
            counts[i] = counts[i] + extra
            spare = spare - extra
    return np.array(counts)


def centred(key, dims, deviation, most, shards=(), kind=jnp.bfloat16):
    values = jax.random.normal(key, dims, jnp.float32) * deviation
    if len(shards) > 0:
        values = shard_levels(key, dims, shards, -0.22, 0.18) * values
    return jnp.clip(values, min=-most, max=most).astype(kind)


def setup_inputs(seed: int = 0) -> dict:
    splits = jax.random.split(jax.random.key(seed), 17)
    tokens = centred(splits[0], (TOKENS, D), 1.0, 6.0, ((0, 64),))
    routes_keys = jax.random.split(jax.random.fold_in(splits[1], 1), TOKENS // TOK_DEV)
    routes_turns = jax.random.permutation(jax.random.fold_in(splits[1], 3), TOKENS // TOK_DEV)
    routes = jax.vmap(lambda own, number: assign_block(jax.random.fold_in(splits[1], 2), own, number, TOK_DEV, EXPERTS, TOP, CAP, 1))(routes_keys, routes_turns).reshape((TOKENS, TOP))
    gain_one = jnp.clip(1.0 + 0.1 * jax.random.normal(splits[2], (D,), jnp.float32), 0.5, 1.5)
    w_query = centred(splits[3], (D, HEADS * HEAD_DIM), D ** -0.5, 0.21875, ((1, 2),))
    w_key = centred(splits[4], (D, HEADS * HEAD_DIM), D ** -0.5, 0.21875, ((1, 2),))
    w_value = centred(splits[5], (D, HEADS * HEAD_DIM), D ** -0.5, 0.21875, ((1, 2),))
    w_output = centred(splits[6], (HEADS * HEAD_DIM, D), 4 ** -0.5, 3.0, ((0, 2),))
    gain_two = jnp.clip(1.0 + 0.1 * jax.random.normal(splits[7], (D,), jnp.float32), 0.5, 1.5)
    w_router = centred(splits[8], (D, EXPERTS), (2 * D) ** -0.5, 0.15625)
    shared_gate = centred(splits[9], (D, SHARED_FF), D ** -0.5, 0.21875, ((1, 2),))
    shared_up = centred(splits[10], (D, SHARED_FF), D ** -0.5, 0.21875, ((1, 2),))
    shared_down = centred(splits[11], (SHARED_FF, D), SHARED_FF ** -0.5, 0.125, ((0, 2),))
    expert_gate = centred(splits[12], (EXPERTS * SPLIT, D, FF // SPLIT), D ** -0.5, 0.21875, ((0, 64), (2, 2)))
    expert_up = centred(splits[13], (EXPERTS * SPLIT, D, FF // SPLIT), D ** -0.5, 0.21875, ((0, 64), (2, 2)))
    expert_down = centred(splits[14], (EXPERTS * SPLIT, FF // SPLIT, D), FF ** -0.5, 0.125, ((0, 64), (1, 2)))
    cotangent = centred(splits[15], (TOKENS, D), 1.0, 6.0, ((0, 64),))
    return dict(tokens=tokens, routes=routes, gain_one=gain_one, w_query=w_query, w_key=w_key, w_value=w_value, w_output=w_output, gain_two=gain_two, w_router=w_router, shared_gate=shared_gate, shared_up=shared_up, shared_down=shared_down, expert_gate=expert_gate, expert_up=expert_up, expert_down=expert_down, cotangent=cotangent)


@jax.custom_vjp
def low(v):
    return lax.optimization_barrier(v.astype(jnp.bfloat16)).astype(jnp.float32)

@jax.custom_vjp
def low_back(v):
    return v

def low_keep(v):
    return (low(v), None)

def low_pass(kept, grad):
    return (grad,)

def back_keep(v):
    return (v, None)

def back_low(kept, grad):
    return (low(grad),)
low.defvjp(low_keep, low_pass)
low_back.defvjp(back_keep, back_low)
epsilon = 1e-06
rope_base = 10000.0
masked_out = -1e+30
precise = lax.Precision.HIGHEST

def matmul(left_side, right_side):
    return jnp.dot(left_side, right_side, precision=precise, preferred_element_type=jnp.float32)

def rms_scale(values):
    return lax.rsqrt(lax.optimization_barrier(jnp.mean(values * values, axis=-1, keepdims=True)) + epsilon)

def swish_unit(values):
    return values * jax.nn.sigmoid(values)

def rotary(values, places):
    midpoint = HEAD_DIM // 2
    frequency = rope_base ** (-jnp.arange(midpoint, dtype=jnp.float32) * 2.0 / HEAD_DIM)
    angles = places.astype(jnp.float32)[:, None] * frequency[None, :]
    cosine = jnp.cos(angles)[:, None, :]
    sine_part = jnp.sin(angles)[:, None, :]
    leading = values[..., :midpoint]
    trailing = values[..., midpoint:]
    return jnp.concatenate([leading * cosine - trailing * sine_part, trailing * cosine + leading * sine_part], axis=-1)

def attend(pieces):
    query_seq, key_seq, value_seq = pieces
    raw_scores = low_back(jnp.einsum('qhd,khd->hqk', query_seq, key_seq, precision=precise))
    places = jnp.arange(SEQ_LEN, dtype=jnp.int32)
    allowed = places[None, :] // BLOCK <= places[:, None] // BLOCK
    scores = jnp.where(allowed[None], raw_scores * HEAD_DIM ** (-0.5), masked_out)
    highest = lax.optimization_barrier(jnp.max(scores, axis=-1, keepdims=True))
    weights = jnp.exp(scores - highest)
    attention = weights / lax.optimization_barrier(jnp.sum(weights, axis=-1, keepdims=True))
    mixed_heads = jnp.einsum('hqk,khd->qhd', low(attention), value_seq, precision=precise)
    return low(low_back(mixed_heads))

def route_slots(routes):
    flat_routes = routes.reshape(N_EXPERT, TOK_DEV * TOP).astype(jnp.int32)
    matches = (flat_routes[:, :, None] == jnp.arange(EXPERTS, dtype=jnp.int32)[None, None, :]).astype(jnp.int32)
    before = jnp.cumsum(matches, axis=1).astype(jnp.int32) - matches
    slot_index = lax.optimization_barrier(jnp.sum(before * matches, axis=-1)).astype(jnp.int32)
    source = jnp.arange(N_EXPERT, dtype=jnp.int32)[:, None]
    return (flat_routes * (N_EXPERT * CAP) + source * CAP + slot_index).reshape(-1).astype(jnp.int32)

def expert_rows(pieces):
    rows_in, gate_weight, up_weight, down_weight = pieces
    copies = low_back(jnp.broadcast_to(rows_in[None], (SPLIT,) + rows_in.shape))
    gate_value = low_back(jnp.einsum('grd,gdf->grf', copies, gate_weight, precision=precise))
    up_value = low_back(jnp.einsum('grd,gdf->grf', copies, up_weight, precision=precise))
    hidden = low(swish_unit(gate_value) * up_value)
    partial_value = low(low_back(jnp.einsum('grf,gfd->grd', hidden, down_weight, precision=precise)))
    return lax.optimization_barrier(jnp.sum(partial_value, axis=0))

def forward(stream, gain_one, w_query, w_key, w_value, w_output, gain_two, w_router, shared_gate, shared_up, shared_down, expert_gate, expert_up, expert_down, routes):
    normed = low(stream * rms_scale(stream) * gain_one)
    places = jnp.arange(TOKENS, dtype=jnp.int32) % SEQ_LEN
    head_shape = (TOKENS, HEADS, HEAD_DIM)
    query_rot = low(rotary(low_back(matmul(normed, w_query)).reshape(head_shape), places))
    key_rot = low(rotary(low_back(matmul(normed, w_key)).reshape(head_shape), places))
    value_low = low(low_back(matmul(normed, w_value))).reshape(head_shape)
    sequences = TOKENS // SEQ_LEN
    seq_shape = (sequences, SEQ_LEN, HEADS, HEAD_DIM)
    mixed_heads = lax.map(jax.checkpoint(attend), (query_rot.reshape(seq_shape), key_rot.reshape(seq_shape), value_low.reshape(seq_shape)))
    middle = stream + low_back(matmul(mixed_heads.reshape(TOKENS, HEADS * HEAD_DIM), w_output))
    normed_two = low(middle * rms_scale(middle) * gain_two)
    logits = low_back(matmul(normed_two, w_router))
    chosen = jnp.take_along_axis(logits, routes, axis=1)
    weights = jnp.exp(chosen - lax.optimization_barrier(jnp.max(chosen, axis=1, keepdims=True)))
    gate_share = weights / lax.optimization_barrier(jnp.sum(weights, axis=1, keepdims=True))
    gate_shared = low_back(matmul(normed_two, shared_gate))
    up_shared = low_back(matmul(normed_two, shared_up))
    hidden_shared = low(swish_unit(gate_shared) * up_shared)
    shared_out = low_back(matmul(hidden_shared, shared_down))
    targets = route_slots(routes)
    sent_rows = jnp.repeat(normed_two, TOP, axis=0)
    buffer = jnp.zeros((EXPERTS * N_EXPERT * CAP, D), jnp.float32).at[targets].set(sent_rows)
    slice_width = FF // SPLIT
    outputs = lax.map(jax.checkpoint(expert_rows), (buffer.reshape(EXPERTS, N_EXPERT * CAP, D), expert_gate.reshape(EXPERTS, SPLIT, D, slice_width), expert_up.reshape(EXPERTS, SPLIT, D, slice_width), expert_down.reshape(EXPERTS, SPLIT, slice_width, D)))
    picked = outputs.reshape(EXPERTS * N_EXPERT * CAP, D)[targets].reshape(TOKENS, TOP, D)
    return middle + shared_out + lax.optimization_barrier(jnp.sum(gate_share[:, :, None] * picked, axis=1))

def reference(tokens, routes, gain_one, w_query, w_key, w_value, w_output, gain_two, w_router, shared_gate, shared_up, shared_down, expert_gate, expert_up, expert_down, cotangent):
    params = tuple((array_in.astype(jnp.float32) for array_in in (tokens, gain_one, w_query, w_key, w_value, w_output, gain_two, w_router, shared_gate, shared_up, shared_down, expert_gate, expert_up, expert_down)))

    def wrapped(*inputs):
        return forward(*inputs, routes)
    result, pullback = jax.vjp(wrapped, *params)
    gradients = pullback(cotangent.astype(jnp.float32))
    return (result.astype(jnp.bfloat16), gradients[0], gradients[1], gradients[2], gradients[3], gradients[4], gradients[5], gradients[6], gradients[7], gradients[8], gradients[9], gradients[10], gradients[11], gradients[12], gradients[13])
```

```python
import jax
import jax.numpy as jnp
import numpy as np
from jax import lax
from jax.sharding import Mesh
from jax.sharding import PartitionSpec as P

HEAD_DIM = 64
BLOCK = 256
SLOTS = 40
AXES = ("zh", "x", "yh", "yl", "c", "t")
EXPERT = AXES[:5]
ROUTE = ("zh", "x", "yh")
PLANE = ("x", "yh", "yl")

epsilon = 1e-06
rope_base = 10000.0
masked_out = -1e30
bf16 = jnp.bfloat16
f32 = jnp.float32


def swap(x, axis):
    return lax.ppermute(x, axis, [(0, 1), (1, 0)])


def exchange(x, axis):
    return lax.all_to_all(x, axis, split_axis=0, concat_axis=0, tiled=True)


def dot(a, b, dims=((1,), (0,))):
    return lax.dot_general(a, b, (dims, ((), ())), preferred_element_type=f32)


def dot_nt(a, b):
    return dot(a, b, ((1,), (1,)))


def dot_tn(a, b):
    return dot(a, b, ((0,), (0,)))


def swish_unit(values):
    return values * jax.nn.sigmoid(values)


def swish_slope(values):
    sigmoid = jax.nn.sigmoid(values)
    return sigmoid * (1.0 + values * (1.0 - sigmoid))


def rms_scale(values):
    return lax.rsqrt(jnp.mean(values * values, axis=-1, keepdims=True) + epsilon)


def pair_sum(values, axis):
    low = values.astype(bf16)
    return low.astype(f32) + swap(low, axis).astype(f32)


def norm_back(inputs, row_scale, gain_row, upstream):
    unit_rows = inputs * row_scale
    scaled_grad = upstream * gain_row
    return row_scale * (
        scaled_grad - unit_rows * jnp.mean(scaled_grad * unit_rows, axis=-1, keepdims=True)
    )


def half_by(values, bit):
    rows = values.shape[0] // 2
    first, second = values[:rows], values[rows:]
    return jnp.where(bit == 0, first, second), jnp.where(bit == 0, second, first)


def sum_over_expert(values, core):
    rows, width = values.shape
    kept, given = half_by(values, core)
    kept = kept + swap(given.astype(bf16), "c").astype(f32)
    parts = exchange(kept.astype(bf16).reshape(16, rows // 32, width), PLANE)
    part = jnp.sum(parts.astype(f32), axis=0)
    part = pair_sum(part, "zh").astype(bf16)
    copies = jnp.broadcast_to(part[None], (16, rows // 32, width))
    mine = exchange(copies, PLANE).reshape(rows // 2, width)
    theirs = swap(mine, "c")
    return jnp.concatenate(
        [jnp.where(core == 0, mine, theirs), jnp.where(core == 0, theirs, mine)], axis=0
    ).astype(f32)


def local(
    tokens,
    routes,
    gain_one,
    w_query,
    w_key,
    w_value,
    w_output,
    gain_two,
    w_router,
    shared_gate,
    shared_up,
    shared_down,
    expert_gate,
    expert_up,
    expert_down,
    cotangent,
):
    rows, width = tokens.shape
    wide = w_query.shape[1]
    heads_here = wide // HEAD_DIM
    experts = w_router.shape[1]
    seats = experts * SLOTS
    tensor = lax.axis_index("t")
    core = lax.axis_index("c")
    high = lax.axis_index("yl")
    expert_here = lax.axis_index(ROUTE)
    score_scale = HEAD_DIM ** (-0.5)
    place_of = [
        (high ^ my) * 2 + (core ^ mc) for my, mc in ((0, 0), (0, 1), (1, 0), (1, 1))
    ]
    own_place = place_of[0]

    tokens_y = swap(tokens, "yl")
    tokens_c = swap(tokens, "c")
    tokens_yc = swap(tokens_y, "c")
    all_tokens = jnp.concatenate([tokens, tokens_c, tokens_y, tokens_yc], axis=0)

    own_weights = jnp.concatenate([expert_gate[0], expert_up[0], expert_down[0].T], axis=1)[None]
    weights = jnp.concatenate([own_weights, swap(own_weights, "t")], axis=0)
    weights = jnp.concatenate([weights, swap(weights, "yl")], axis=0)
    weights = jnp.concatenate([weights, swap(weights, "c")], axis=0)

    flat_routes = routes.reshape(-1)
    expert_ids = jnp.arange(experts, dtype=jnp.int32)
    matches = (flat_routes[:, None] == expert_ids[None, :]).astype(jnp.int32)
    before = jnp.cumsum(matches, axis=0) - matches
    slot_index = jnp.sum(before * matches, axis=-1) - tensor * SLOTS
    seat = jnp.where(
        (slot_index >= 0) & (slot_index < SLOTS), flat_routes * SLOTS + slot_index, -1
    ).reshape(rows, -1)
    seat_ids = jnp.arange(seats, dtype=jnp.int32)
    placer = jnp.sum((seat[:, :, None] == seat_ids[None, None, :]).astype(f32), axis=1).astype(bf16)
    extra = jnp.where(
        jnp.arange(128)[None, :] == 0, jnp.sum(routes, axis=1, keepdims=True).astype(f32), 0.0
    ).astype(bf16)
    sent_cot = dot_tn(placer, jnp.concatenate([cotangent, extra], axis=1)).astype(bf16)
    cot_ext = exchange(sent_cot.reshape(experts, SLOTS, -1), ROUTE).reshape(seats, -1)
    cot_rows = cot_ext[:, :width]
    other_expert = cot_ext[:, width : width + 1].astype(jnp.int32) - expert_here

    all_stream = all_tokens.astype(f32)
    all_unit = all_stream * rms_scale(all_stream)
    all_normed = (all_unit * gain_one).astype(bf16)
    stream = tokens.astype(f32)
    scale_one = rms_scale(stream)
    normed = all_normed[:rows]
    frequency = rope_base ** (-np.arange(HEAD_DIM // 2) * 2.0 / HEAD_DIM)
    key_places = jnp.concatenate(
        [place * rows + jnp.arange(rows, dtype=jnp.int32) for place in place_of]
    )
    angles = key_places.astype(f32)[:, None] * frequency.astype(np.float32)[None, :]
    cosine, sine = jnp.cos(angles)[:, None, :], jnp.sin(angles)[:, None, :]

    def rotary(values, direction):
        count = values.shape[0]
        cos, sin = cosine[:count], direction * sine[:count]
        leading, trailing = values[..., : HEAD_DIM // 2], values[..., HEAD_DIM // 2 :]
        return jnp.concatenate(
            [leading * cos - trailing * sin, trailing * cos + leading * sin], axis=-1
        )

    query_rot = rotary(dot(normed, w_query).reshape(rows, heads_here, HEAD_DIM), 1.0).astype(bf16)
    all_keys = rotary(dot(all_normed, w_key).reshape(4 * rows, heads_here, HEAD_DIM), 1.0).astype(
        bf16
    )
    all_values = dot(all_normed, w_value).astype(bf16).reshape(4 * rows, heads_here, HEAD_DIM)
    query_places = key_places[:rows]
    allowed = key_places[None, :] // BLOCK <= query_places[:, None] // BLOCK

    def scores_of():
        raw = jnp.einsum("qhd,khd->hqk", query_rot, all_keys, preferred_element_type=f32)
        return jnp.where(allowed[None], raw * score_scale, masked_out)

    scores = scores_of()
    highest = jnp.max(scores, axis=-1, keepdims=True)
    weigh = jnp.exp(scores - highest)
    weight_sum = jnp.sum(weigh, axis=-1, keepdims=True)
    attention = weigh / weight_sum
    log_total = highest + jnp.log(weight_sum)
    mixed_heads = (
        jnp.einsum("hqk,khd->qhd", attention.astype(bf16), all_values, preferred_element_type=f32)
        .astype(bf16)
        .reshape(rows, -1)
    )
    middle = stream + pair_sum(dot(mixed_heads, w_output), "t")
    scale_two = rms_scale(middle)
    unit_two = middle * scale_two
    normed_two = (unit_two * gain_two).astype(bf16)

    sent_rows = dot_tn(placer, normed_two).astype(bf16)
    rows_in = exchange(sent_rows.reshape(experts, SLOTS, width), ROUTE).reshape(seats, width)
    row_logits = dot(rows_in, w_router)
    own_logit = jnp.sum(jnp.where(expert_ids[None, :] == expert_here, row_logits, 0.0), axis=1, keepdims=True)
    other_logit = jnp.sum(jnp.where(expert_ids[None, :] == other_expert, row_logits, 0.0), axis=1, keepdims=True)
    top_logit = jnp.maximum(own_logit, other_logit)
    own_weight = jnp.exp(own_logit - top_logit)
    row_share = own_weight / (own_weight + jnp.exp(other_logit - top_logit))
    part = wide_part = expert_gate.shape[2]
    gates, ups = weights[:, :, :part], weights[:, :, part : 2 * part]
    downs = weights[:, :, 2 * part :]
    gate_expert = jnp.einsum("rd,kdf->krf", rows_in, gates, preferred_element_type=f32)
    up_expert = jnp.einsum("rd,kdf->krf", rows_in, ups, preferred_element_type=f32)
    hidden_grads = jnp.einsum("rd,kdf->krf", cot_rows, downs, preferred_element_type=f32)
    hidden_expert = (swish_unit(gate_expert) * up_expert).astype(bf16)
    gate_dots = jnp.sum(hidden_expert.astype(f32) * hidden_grads, axis=(0, 2))[:, None]
    expert_gate_grads = (hidden_grads * up_expert * swish_slope(gate_expert)).astype(bf16)
    expert_up_grads = (hidden_grads * swish_unit(gate_expert)).astype(bf16)
    rows_part = jnp.einsum("krf,kdf->rd", expert_gate_grads, gates, preferred_element_type=f32)
    rows_part = rows_part + jnp.einsum(
        "krf,kdf->rd", expert_up_grads, ups, preferred_element_type=f32
    )
    dots_high = gate_dots.astype(bf16).astype(f32)
    lanes = jnp.arange(128)[None, :]
    dots_ext = jnp.where(lanes == expert_here, dots_high, 0.0) + jnp.where(
        lanes == experts + expert_here, gate_dots - dots_high, 0.0
    )
    back = jnp.concatenate([row_share * rows_part, dots_ext], axis=1).astype(bf16)
    back = exchange(back.reshape(experts, SLOTS, -1), ROUTE).reshape(seats, -1)
    expert_out = jnp.einsum("krf,kdf->rd", hidden_expert, downs, preferred_element_type=f32)
    picked = exchange(
        (row_share * expert_out).astype(bf16).reshape(experts, SLOTS, width), ROUTE
    ).reshape(seats, width)

    scaled_rows = (row_share * rows_in.astype(f32)).astype(bf16)
    out_grads = (row_share * cot_rows.astype(f32)).astype(bf16)
    grad_gates = jnp.einsum("rd,krf->kdf", scaled_rows, expert_gate_grads, preferred_element_type=f32)
    grad_ups = jnp.einsum("rd,krf->kdf", scaled_rows, expert_up_grads, preferred_element_type=f32)
    grad_downs = jnp.einsum("rd,krf->kdf", out_grads, hidden_expert, preferred_element_type=f32)
    grads = jnp.concatenate([grad_gates, grad_ups, grad_downs], axis=2).astype(bf16)
    grads = grads[:4].astype(f32) + swap(grads[4:], "c").astype(f32)
    grads = grads.astype(bf16)
    grads = grads[:2].astype(f32) + swap(grads[2:], "yl").astype(f32)
    grads = grads.astype(bf16)
    grads = grads[0].astype(f32) + swap(grads[1], "t").astype(f32)
    grad_expert_gate = grads[None, :, :part]
    grad_expert_up = grads[None, :, part : 2 * part]
    grad_expert_down = grads[:, 2 * part :].T[None]

    gate_shared = dot(normed_two, shared_gate)
    up_shared = dot(normed_two, shared_up)
    hidden_shared = (swish_unit(gate_shared) * up_shared).astype(bf16)
    shared_hidden_grads = dot_nt(cotangent, shared_down)
    shared_gate_grads = (shared_hidden_grads * up_shared * swish_slope(gate_shared)).astype(bf16)
    shared_up_grads = (shared_hidden_grads * swish_unit(gate_shared)).astype(bf16)
    shared_back = dot_nt(shared_gate_grads, shared_gate) + dot_nt(shared_up_grads, shared_up)
    shared_out = dot(hidden_shared, shared_down)
    grad_shared_down = dot_tn(hidden_shared, cotangent)
    grad_shared_gu = dot_tn(normed_two, jnp.concatenate([shared_gate_grads, shared_up_grads], axis=1))

    logits = dot(normed_two, w_router)
    choose = routes[:, :, None] == expert_ids[None, None, :]
    chosen = jnp.sum(jnp.where(choose, logits[:, None, :], 0.0), axis=-1)
    gate_weights = jnp.exp(chosen - jnp.max(chosen, axis=1, keepdims=True))
    gate_share = gate_weights / jnp.sum(gate_weights, axis=1, keepdims=True)
    share = jnp.sum(jnp.where(choose, gate_share[:, :, None], 0.0), axis=1)
    combined = dot(placer, back)
    routed_grads = combined[:, :width]
    gate_grads = combined[:, width : width + experts] + combined[:, width + experts : width + 2 * experts]
    logits_grads = (
        share * (gate_grads - jnp.sum(share * gate_grads, axis=1, keepdims=True))
    ).astype(bf16)
    grad_router = dot_tn(normed_two, logits_grads)
    router_back = dot_nt(logits_grads, w_router)
    normed_two_grads = pair_sum(shared_back + router_back + routed_grads, "t")
    grad_gain_two = jnp.sum(normed_two_grads * unit_two, axis=0)
    grad_result = cotangent.astype(f32)
    middle_grads = grad_result + norm_back(middle, scale_two, gain_two, normed_two_grads)
    middle_low = middle_grads.astype(bf16)
    block_out = (middle + pair_sum(shared_out + dot(placer, picked), "t")).astype(bf16)

    mixed_grads = dot_nt(middle_low, w_output).astype(bf16).reshape(rows, heads_here, HEAD_DIM)
    attention = jnp.exp(scores_of() - log_total)
    prob_grads = jnp.einsum("qhd,khd->hqk", mixed_grads, all_values, preferred_element_type=f32)
    value_full = jnp.einsum("hqk,qhd->khd", attention.astype(bf16), mixed_grads, preferred_element_type=f32)
    score_grads = (
        attention
        * (prob_grads - jnp.sum(prob_grads * attention, axis=-1, keepdims=True))
        * score_scale
    ).astype(bf16)
    query_full = jnp.einsum("hqk,khd->qhd", score_grads, all_keys, preferred_element_type=f32)
    key_full = jnp.einsum("hqk,qhd->khd", score_grads, query_rot, preferred_element_type=f32)
    query_grads = rotary(query_full, -1.0).reshape(rows, -1).astype(bf16)
    key_grads = rotary(key_full, -1.0).reshape(4 * rows, -1).astype(bf16)
    value_grads = value_full.reshape(4 * rows, -1).astype(bf16)
    normed_part = dot_nt(key_grads, w_key) + dot_nt(value_grads, w_value)
    own_part = normed_part[:rows] + dot_nt(query_grads, w_query)
    y_part = normed_part[2 * rows : 3 * rows]
    given = jnp.stack([normed_part[rows : 2 * rows], normed_part[3 * rows :]]).astype(bf16)
    taken = swap(given, "c").astype(f32)
    own_part = own_part + taken[0]
    own_part = own_part + swap((y_part + taken[1]).astype(bf16), "yl").astype(f32)
    normed_grads = pair_sum(own_part, "t")
    grad_tokens = middle_grads + norm_back(stream, scale_one, gain_one, normed_grads)

    grad_query = dot_tn(normed, query_grads)
    grad_key = dot_tn(all_normed, key_grads)
    grad_value = dot_tn(all_normed, value_grads)
    gain_part = (
        jnp.sum(
            grad_query * w_query.astype(f32)
            + grad_key * w_key.astype(f32)
            + grad_value * w_value.astype(f32),
            axis=1,
        )
        / gain_one
    )
    grad_output = dot_tn(middle_low, mixed_heads)
    small = jnp.concatenate(
        [
            grad_router,
            gain_part[:, None],
            grad_gain_two[:, None],
            jnp.zeros((width, 128 - experts - 2), f32),
        ],
        axis=1,
    )
    shared_gu = sum_over_expert(grad_shared_gu, core)
    grad_shared_down = sum_over_expert(grad_shared_down, core)
    packed = sum_over_expert(
        jnp.concatenate([grad_query, grad_key, grad_value, grad_output, small], axis=1), core
    )
    small = packed[:, 4 * wide :]
    both = small + swap(small, "t")
    return (
        block_out,
        grad_tokens,
        both[:, experts],
        packed[:, :wide],
        packed[:, wide : 2 * wide],
        packed[:, 2 * wide : 3 * wide],
        packed[:, 3 * wide : 4 * wide].T,
        small[:, experts + 1],
        both[:, :experts],
        shared_gu[:, : shared_gate.shape[1]],
        shared_gu[:, shared_gate.shape[1] :],
        grad_shared_down,
        grad_expert_gate,
        grad_expert_up,
        grad_expert_down,
    )


def solution(mesh):
    fine = Mesh(mesh.devices.reshape(2, 4, 2, 2, 2, 2), AXES)
    placed = (
        P(EXPERT, None),
        P(EXPERT, None),
        P(),
        P(None, "t"),
        P(None, "t"),
        P(None, "t"),
        P("t", None),
        P(),
        P(),
        P(None, "t"),
        P(None, "t"),
        P("t", None),
        P(EXPERT, None, "t"),
        P(EXPERT, None, "t"),
        P(EXPERT, "t", None),
        P(EXPERT, None),
    )
    return jax.shard_map(
        local,
        mesh=fine,
        in_specs=placed,
        out_specs=(
            P(EXPERT, None),
            P(EXPERT, None),
            P(),
            P(None, "t"),
            P(None, "t"),
            P(None, "t"),
            P("t", None),
            P(),
            P(),
            P(None, "t"),
            P(None, "t"),
            P("t", None),
            P(EXPERT, None, "t"),
            P(EXPERT, None, "t"),
            P(EXPERT, "t", None),
        ),
        check_vma=False,
    )
```

```python
import functools

import jax
import jax.numpy as jnp
import numpy as np
from jax import lax
from jax.experimental import pallas as pl
from jax.experimental.pallas import tpu as pltpu
from jax.sharding import Mesh
from jax.sharding import PartitionSpec as P

HEAD_DIM = 64
BLOCK = 256
SLOTS = 40
PAIR = 128
AXES = ("zh", "x", "yh", "yl", "c", "t")
EXPERT = AXES[:5]
ROUTE = ("zh", "x", "yh")
PLANE = ("x", "yh", "yl")

epsilon = 1e-06
rope_base = 10000.0
bf16 = jnp.bfloat16
f32 = jnp.float32
params = pltpu.CompilerParams(vmem_limit_bytes=52 << 20)


def swap(x, axis):
    return lax.ppermute(x, axis, [(0, 1), (1, 0)])


def exchange(x, axis):
    return lax.all_to_all(x, axis, split_axis=0, concat_axis=0, tiled=True)


def after(x, first):
    return lax.optimization_barrier((x, first))[0]


def dot(a, b, dims=((1,), (0,))):
    return lax.dot_general(a, b, (dims, ((), ())), preferred_element_type=f32)


def dot_nt(a, b):
    return dot(a, b, ((1,), (1,)))


def dot_tn(a, b):
    return dot(a, b, ((0,), (0,)))


def rms_scale(values):
    return lax.rsqrt(jnp.mean(values * values, axis=-1, keepdims=True) + epsilon)


def pair_sum(values, axis):
    low = values.astype(bf16)
    return low.astype(f32) + swap(low, axis).astype(f32)


def norm_back(inputs, row_scale, gain_row, upstream):
    unit_rows = inputs * row_scale
    scaled_grad = upstream * gain_row
    return row_scale * (
        scaled_grad - unit_rows * jnp.mean(scaled_grad * unit_rows, axis=-1, keepdims=True)
    )


def half_by(values, bit):
    rows = values.shape[0] // 2
    first, second = values[:rows], values[rows:]
    return jnp.where(bit == 0, first, second), jnp.where(bit == 0, second, first)


RATE = 1150000000
TIMES = dict(
    route=4,
    project=5,
    attend=14,
    attend_back=23,
    second=4,
    shared=12,
    expert_rows=20,
    expert_weights=17,
    combine=4,
    back_two=4,
    normed_back=8,
    first=4,
    shared_weights=6,
    late_weights=8,
)


def turn(values, cos, sin):
    half = HEAD_DIM // 2
    lanes = lax.broadcasted_iota(jnp.int32, values.shape, 1)
    first = (lanes // half) % 2 == 0
    size = values.shape[1]
    other = jnp.where(first, -pltpu.roll(values, size - half, 1), pltpu.roll(values, half, 1))
    return values * cos + other * sin


def whole(shape):
    return pl.BlockSpec(shape, lambda *_: (0,) * len(shape))


def call(kernel, name, args, outs, smem=(), grid=None, in_specs=None, out_specs=None, scratch=()):
    in_specs = dict(in_specs or {})
    out_specs = dict(out_specs or {})
    for i in smem:
        in_specs[i] = pl.BlockSpec(memory_space=pltpu.SMEM)
    return pl.pallas_call(
        kernel,
        **({} if grid is None else {"grid": grid}),
        in_specs=[in_specs.get(i, whole(a.shape)) for i, a in enumerate(args)],
        out_specs=[out_specs.get(i, whole(s)) for i, (s, _) in enumerate(outs)],
        out_shape=[jax.ShapeDtypeStruct(s, d) for s, d in outs],
        scratch_shapes=scratch,
        compiler_params=params,
        cost_estimate=pl.CostEstimate(flops=TIMES[name] * RATE, bytes_accessed=1 << 20, transcendentals=0),
        name=name,
    )(*args)


def lanes_of(rows=1, count=128):
    return lax.broadcasted_iota(jnp.int32, (rows, count), 1)


def route_kernel(tensor_ref, routes_ref, cot_ref, expand_ref, seat_ref, placer_ref, turned_ref, sent_ref):
    routes = routes_ref[...]
    rows, width = cot_ref.shape
    lanes = lanes_of(rows)
    member = (routes[:, 0:1] == lanes) | (routes[:, 1:2] == lanes)
    earlier = lax.broadcasted_iota(jnp.int32, (rows, rows), 0) > lanes_of(rows, rows)
    count = dot(
        jnp.where(earlier, 1.0, 0.0).astype(bf16), jnp.where(member, 1.0, 0.0).astype(bf16)
    )
    offset = (tensor_ref[0] * SLOTS).astype(f32)
    place = jnp.where(member, count - offset, -1.0).astype(bf16)
    placer = jnp.where(dot(place, expand_ref[...]) == seat_ref[...], 1.0, 0.0).astype(bf16)
    placer_ref[...] = placer
    turned = placer.T
    turned_ref[...] = turned
    sent_ref[:, :width] = dot(turned, cot_ref[...]).astype(bf16)
    sums = (routes[:, 0:1] + routes[:, 1:2]).astype(f32)
    sent_ref[:, width:] = dot(turned, jnp.where(lanes == 0, sums, 0.0).astype(bf16)).astype(bf16)


def route(tensor, routes, cotangent, experts):
    rows, width = cotangent.shape
    seats = experts * SLOTS
    columns = np.arange(seats)
    expand = jnp.asarray(np.arange(128)[:, None] == columns[None, :] // SLOTS, bf16)
    seat = jnp.asarray((columns % SLOTS)[None], f32)
    return call(
        route_kernel,
        "route",
        (tensor[None], routes, cotangent, expand, seat),
        [((rows, seats), bf16), ((seats, rows), bf16), ((seats, width + 128), bf16)],
        smem=(0,),
    )


def project_kernel(x0_ref, x1_ref, gain_ref, wk_ref, wv_ref, cos_ref, sin_ref, *rest):
    wq_ref = rest[0] if len(rest) == 5 else None
    n_ref, k_ref, v_ref = rest[-4:-1] if wq_ref is not None else rest
    for chunk, x_ref in enumerate((x0_ref, x1_ref)):
        rows = x_ref.shape[0]
        at_rows = slice(chunk * rows, (chunk + 1) * rows)
        x = x_ref[...].astype(f32)
        normed = (x * rms_scale(x) * gain_ref[...]).astype(bf16)
        n_ref[at_rows, :] = normed
        cos, sin = cos_ref[at_rows, :], sin_ref[at_rows, :]
        key = dot(normed, wk_ref[...])
        for at in range(0, key.shape[1], PAIR):
            lanes = slice(at, at + PAIR)
            k_ref[at_rows, lanes] = turn(key[:, lanes], cos, sin).astype(bf16)
        v_ref[at_rows, :] = dot(normed, wv_ref[...]).astype(bf16)
        if chunk == 0 and wq_ref is not None:
            q_ref = rest[-1]
            query = dot(normed, wq_ref[...])
            for at in range(0, query.shape[1], PAIR):
                lanes = slice(at, at + PAIR)
                turned = turn(query[:, lanes], cos, sin).astype(bf16)
                q_ref[:, lanes] = turned * (HEAD_DIM**-0.5)


def project(first, second, gain, w_key, w_value, cos, sin, w_query=None):
    rows, width = first.shape
    wide = w_key.shape[1]
    outs = [((2 * rows, width), bf16), ((2 * rows, wide), bf16), ((2 * rows, wide), bf16)]
    args = (first, second, gain, w_key, w_value, cos, sin)
    if w_query is not None:
        args += (w_query,)
        outs.append(((rows, wide), bf16))
    return call(project_kernel, "project", args, outs)


def attend_kernel(hide_ref, q_ref, ka_ref, va_ref, kb_ref, vb_ref, wo_ref, o_ref, lse_ref, part_ref, acc_ref):
    lanes = lanes_of()
    span = 2 * BLOCK
    step = pl.program_id(0)
    for half in range(2):
        rows = slice(half * BLOCK, (half + 1) * BLOCK)
        q = q_ref[rows, :]
        outs, logs = [], []
        for head in range(2):
            query = jnp.where(lanes // HEAD_DIM == head, q, jnp.zeros_like(q))
            spans = [(ka_ref, va_ref, 0, BLOCK * (half + 1), 0.0), (ka_ref, va_ref, span, span, hide_ref[1])]
            spans += [(kb_ref, vb_ref, 0, span, hide_ref[2]), (kb_ref, vb_ref, span, span, hide_ref[3])]
            scores = [dot_nt(query, k[a : a + n, :]) for k, _, a, n, _ in spans]
            tops = [jnp.max(s, axis=1, keepdims=True) - x[4] for s, x in zip(scores, spans)]
            top = functools.reduce(jnp.maximum, tops)
            total, acc = 0.0, 0.0
            for s, (_, v, a, n, off) in zip(scores, spans):
                p = jnp.exp(s - (top + off))
                total = total + jnp.sum(p, axis=1, keepdims=True)
                acc = acc + dot(p.astype(bf16), v[a : a + n, :])
            outs.append(acc / total)
            logs.append(top + jnp.log(total))
        mixed = jnp.where(lanes < HEAD_DIM, outs[0], outs[1]).astype(bf16)
        o_ref[rows, :] = mixed
        lse_ref[rows, :] = jnp.where(lanes < HEAD_DIM, logs[0], logs[1])
    part = dot(o_ref[...], wo_ref[...])

    @pl.when(step == 0)
    def _():
        acc_ref[...] = part

    @pl.when(step > 0)
    def _():
        acc_ref[...] += part

    @pl.when(step == pl.num_programs(0) - 1)
    def _():
        part_ref[...] = acc_ref[...].astype(bf16)


def attend(hide, q, ka, va, kb, vb, w_output):
    rows, keys = q.shape[0], ka.shape[0]
    width = w_output.shape[1]
    of_q = pl.BlockSpec((rows, PAIR), lambda p: (0, p))
    of_k = pl.BlockSpec((keys, PAIR), lambda p: (0, p))
    return call(
        attend_kernel,
        "attend",
        (hide, q, ka, va, kb, vb, w_output),
        [(q.shape, bf16), (q.shape, f32), ((rows, width), bf16)],
        smem=(0,),
        grid=(q.shape[1] // PAIR,),
        in_specs={1: of_q, 2: of_k, 3: of_k, 4: of_k, 5: of_k, 6: pl.BlockSpec((PAIR, width), lambda p: (p, 0))},
        out_specs={0: of_q, 1: of_q},
        scratch=[pltpu.VMEM((rows, width), f32)],
    )


def attend_back_kernel(
    hide_ref, q_ref, ka_ref, va_ref, kb_ref, vb_ref, o_ref, lse_ref, g_ref, ca_ref, sa_ref, cb_ref, sb_ref,
    dq_ref, dka_ref, dva_ref, dkb_ref, dvb_ref,
):
    lanes = lanes_of()
    q, g = q_ref[...], g_ref[...]
    rows = q.shape[0]
    deltas = (g.astype(f32) * o_ref[...].astype(f32)).T
    logs = lse_ref[...].T
    dq = 0.0
    near = (ka_ref, va_ref, ca_ref, sa_ref, dka_ref, dva_ref)
    far = (kb_ref, vb_ref, cb_ref, sb_ref, dkb_ref, dvb_ref)
    for block in range(8):
        k_ref, v_ref, cos_ref, sin_ref, dk_ref, dv_ref = near if block < 4 else far
        off = 0.0 if block < 2 else hide_ref[block // 2]
        first = BLOCK if block == 1 else 0
        keys = slice((block % 4) * BLOCK, (block % 4 + 1) * BLOCK)
        k, v = k_ref[keys, :], v_ref[keys, :]
        dk, dv = 0.0, 0.0
        for head in range(2):
            mine = lanes // HEAD_DIM == head
            low = head * HEAD_DIM
            query = jnp.where(mine, q[first:, :], jnp.zeros_like(q[first:, :]))
            grads = jnp.where(mine, g[first:, :], jnp.zeros_like(g[first:, :]))
            key = jnp.where(mine, k, jnp.zeros_like(k))
            log = logs[low : low + 1, first:] + off
            delta = jnp.sum(deltas[low : low + HEAD_DIM, first:], axis=0, keepdims=True)
            p = jnp.exp(dot_nt(k, query) - log)
            ds = (p * (dot_nt(v, grads) - delta)).astype(bf16)
            dv = dv + dot(p.astype(bf16), grads)
            dk = dk + dot(ds, query)
            part = dot_tn(ds, key)
            if first:
                part = jnp.concatenate([jnp.zeros((first, PAIR), f32), part], axis=0)
            dq = dq + part
        dv_ref[keys, :] = dv.astype(bf16)
        dk_ref[keys, :] = turn(dk, cos_ref[keys, :], -sin_ref[keys, :]).astype(bf16)
    dq = dq * (HEAD_DIM**-0.5)
    dq_ref[...] = turn(dq, ca_ref[:rows, :], -sa_ref[:rows, :]).astype(bf16)


def attend_back(hide, q, ka, va, kb, vb, o, lse, g, ca, sa, cb, sb):
    rows, keys = q.shape[0], ka.shape[0]
    of_q = pl.BlockSpec((rows, PAIR), lambda p: (0, p))
    of_k = pl.BlockSpec((keys, PAIR), lambda p: (0, p))
    return call(
        attend_back_kernel,
        "attend_back",
        (hide, q, ka, va, kb, vb, o, lse, g, ca, sa, cb, sb),
        [(q.shape, bf16)] + [(ka.shape, bf16)] * 4,
        smem=(0,),
        grid=(q.shape[1] // PAIR,),
        in_specs={1: of_q, 2: of_k, 3: of_k, 4: of_k, 5: of_k, 6: of_q, 7: of_q, 8: of_q},
        out_specs={0: of_q, 1: of_k, 2: of_k, 3: of_k, 4: of_k},
    )


def second_kernel(x_ref, mine_ref, theirs_ref, gain_ref, turned_ref, middle_ref, n_ref, sent_ref):
    middle = x_ref[...].astype(f32) + (mine_ref[...].astype(f32) + theirs_ref[...].astype(f32))
    middle_ref[...] = middle
    normed = (middle * rms_scale(middle) * gain_ref[...]).astype(bf16)
    n_ref[...] = normed
    sent_ref[...] = dot(turned_ref[...], normed).astype(bf16)


def swish(gate, up, grads):
    sigmoid = jax.nn.sigmoid(gate)
    unit = gate * sigmoid
    slope = sigmoid + unit * (1.0 - sigmoid)
    return (unit * up).astype(bf16), (grads * up * slope).astype(bf16), (grads * unit).astype(bf16)


def shared_kernel(
    n_ref, cot_ref, sg_ref, su_ref, sd_ref, router_ref, routes_ref, h_ref, gg_ref, gu_ref, back_ref, out_ref, share_ref
):
    normed, cot = n_ref[...], cot_ref[...]
    sg, su, sd = sg_ref[...], su_ref[...], sd_ref[...]
    hidden, gg, gu = swish(dot(normed, sg), dot(normed, su), dot_nt(cot, sd))
    h_ref[...], gg_ref[...], gu_ref[...] = hidden, gg, gu
    back = dot_nt(gg, sg) + dot_nt(gu, su)
    out = dot(hidden, sd)

    @pl.when(pl.program_id(0) == 0)
    def _():
        back_ref[...] = back
        out_ref[...] = out
        logits = dot(normed, router_ref[...])
        routes = routes_ref[...]
        lanes = lanes_of()
        first, second = lanes == routes[:, 0:1], lanes == routes[:, 1:2]
        one = jnp.sum(jnp.where(first, logits, 0.0), axis=1, keepdims=True)
        two = jnp.sum(jnp.where(second, logits, 0.0), axis=1, keepdims=True)
        top = jnp.maximum(one, two)
        one, two = jnp.exp(one - top), jnp.exp(two - top)
        share_ref[...] = (jnp.where(first, one, 0.0) + jnp.where(second, two, 0.0)) / (one + two)

    @pl.when(pl.program_id(0) > 0)
    def _():
        back_ref[...] += back
        out_ref[...] += out


def shared(normed, cot, shared_gate, shared_up, shared_down, router, routes):
    rows, width = normed.shape
    hidden = shared_gate.shape[1]
    block = 256
    columns = pl.BlockSpec((width, block), lambda k: (0, k))
    of_hidden = pl.BlockSpec((rows, block), lambda k: (0, k))
    return call(
        shared_kernel,
        "shared",
        (normed, cot, shared_gate, shared_up, shared_down, router, routes),
        [((rows, hidden), bf16)] * 3 + [((rows, width), f32)] * 2 + [((rows, 128), f32)],
        grid=(hidden // block,),
        in_specs={2: columns, 3: columns, 4: pl.BlockSpec((block, width), lambda k: (k, 0))},
        out_specs={0: of_hidden, 1: of_hidden, 2: of_hidden},
    )


def shared_weights_kernel(core_ref, n_ref, cot_ref, gg_ref, gu_ref, h_ref, d_ref):
    part = h_ref.shape[1]
    turned = n_ref[...].T
    d_ref[0, :, :part] = dot(turned, gg_ref[...]).astype(bf16)
    d_ref[0, :, part : 2 * part] = dot(turned, gu_ref[...]).astype(bf16)
    d_ref[0, :, 2 * part :] = dot(cot_ref[...].T, h_ref[...]).astype(bf16)


def half_call(kernel, name, core, halved, full, columns):
    half = halved[0].shape[1] // 2
    specs = [pl.BlockSpec((a.shape[0], half), lambda s, c: (0, jnp.where(s == 0, 1 - c[0], c[0]))) for a in halved]
    specs += [pl.BlockSpec(a.shape, lambda s, c: (0, 0)) for a in full]
    return pl.pallas_call(
        kernel,
        grid_spec=pltpu.PrefetchScalarGridSpec(
            num_scalar_prefetch=1,
            grid=(2,),
            in_specs=specs,
            out_specs=pl.BlockSpec((1, half, columns), lambda s, c: (s, 0, 0)),
        ),
        out_shape=jax.ShapeDtypeStruct((2, half, columns), bf16),
        compiler_params=params,
        cost_estimate=pl.CostEstimate(flops=TIMES[name] * RATE, bytes_accessed=1 << 20, transcendentals=0),
        name=name,
    )(core[None], *halved, *full)


def late_weights_kernel(
    core_ref, na_ref, nb_ref, n2_ref, low_ref, gain_ref, dq_ref, dka_ref, dkb_ref, dva_ref, dvb_ref, lg_ref, o_ref, d_ref, *, experts
):
    wide = dq_ref.shape[1]
    rows = dq_ref.shape[0]
    ta, tb = na_ref[...].T, nb_ref[...].T
    d_ref[0, :, :wide] = dot(ta[:, :rows], dq_ref[...]).astype(bf16)
    d_ref[0, :, wide : 2 * wide] = (dot(ta, dka_ref[...]) + dot(tb, dkb_ref[...])).astype(bf16)
    d_ref[0, :, 2 * wide : 3 * wide] = (dot(ta, dva_ref[...]) + dot(tb, dvb_ref[...])).astype(bf16)
    d_ref[0, :, 3 * wide : 4 * wide] = dot(low_ref[...].T, o_ref[...]).astype(bf16)
    small = dot(n2_ref[...].T, lg_ref[...])
    gain = jnp.broadcast_to(gain_ref[...], (128, gain_ref.shape[1])).T
    d_ref[0, :, 4 * wide :] = jnp.where(lanes_of() == experts, gain, small).astype(bf16)


def expert_kernel(
    here_ref, rows_ref, cot_ref, router_ref, *refs, experts, shards
):
    w_refs = refs[:shards]
    hidden_ref, grads_ref, back_ref, scaled_ref, out_ref, share_ref, acc_ref, dots_ref, slots_ref, sems = refs[shards:]
    step = pl.program_id(0)
    width = rows_ref.shape[1]

    def fetch(i, slot):
        return pltpu.make_async_copy(w_refs[i], slots_ref.at[slot], sems.at[slot])

    @pl.when(step == 0)
    def _():
        fetch(0, 0).start()

    for i in range(1, shards):
        @pl.when(step == i - 1)
        def _(i=i):
            fetch(i, i % 2).start()

    slot = lax.rem(step, 2)
    fetch(0, slot).wait()
    w = slots_ref.at[slot]
    part = w.shape[1] // 3
    half = rows_ref.shape[0] // 2
    w_in, w_down = w[:, : 2 * part], w[:, 2 * part :]
    for at in (0, half):
        these = slice(at, at + half)
        rows, cot = rows_ref[these, :], cot_ref[these, :width]
        both = dot(rows, w_in)
        hidden_grads = dot(cot, w_down)
        hidden, gg, gu = swish(both[:, :part], both[:, part:], hidden_grads)
        hidden_ref[0, these, :] = hidden
        grads_ref[0, these, :part] = gg
        grads_ref[0, these, part:] = gu
        product = hidden.astype(f32) * hidden_grads
        product = functools.reduce(jnp.add, [product[:, a : a + 128] for a in range(0, part, 128)])
        back = dot_nt(gg, w[:, :part]) + dot_nt(gu, w[:, part : 2 * part])
        acc_ref[these, :] = jnp.where(step == 0, 0.0, acc_ref[these, :]) + back
        dots_ref[these, :] = jnp.where(step == 0, 0.0, dots_ref[these, :]) + product

    @pl.when(step == pl.num_programs(0) - 1)
    def _():
        rows, cot = rows_ref[...], cot_ref[:, :width]
        here = here_ref[0]
        lanes = lanes_of()
        logits = dot(rows, router_ref[...])
        other = cot_ref[:, width:].astype(f32)[:, :1].astype(jnp.int32) - here
        own_logit = jnp.sum(jnp.where(lanes == here, logits, 0.0), axis=1, keepdims=True)
        other_logit = jnp.sum(jnp.where(lanes == other, logits, 0.0), axis=1, keepdims=True)
        top = jnp.maximum(own_logit, other_logit)
        own = jnp.exp(own_logit - top)
        share = own / (own + jnp.exp(other_logit - top))
        share_ref[...] = jnp.broadcast_to(share, share_ref.shape)
        scaled_ref[...] = (share * rows.astype(f32)).astype(bf16)
        out_ref[...] = (share * cot.astype(f32)).astype(bf16)
        back_ref[:, :width] = (share * acc_ref[...]).astype(bf16)
        dots = jnp.sum(dots_ref[...], axis=1, keepdims=True)
        high = dots.astype(bf16).astype(f32)
        back_ref[:, width:] = (
            jnp.where(lanes == here, high, 0.0)
            + jnp.where(lanes == experts + here, dots - high, 0.0)
        ).astype(bf16)


def expert_rows(here, rows_in, cot_ext, router, weights, experts):
    rows, width = rows_in.shape
    shards, packed = len(weights), weights[0].shape[1]
    part = packed // 3
    return call(
        functools.partial(expert_kernel, experts=experts, shards=shards),
        "expert_rows",
        (here[None], rows_in, cot_ext, router, *weights),
        [
            ((shards, rows, part), bf16),
            ((shards, rows, 2 * part), bf16),
            ((rows, width + 128), bf16),
            ((rows, width), bf16),
            ((rows, width), bf16),
            ((rows, 128), f32),
        ],
        smem=(0,),
        grid=(shards,),
        in_specs={4 + i: pl.BlockSpec(memory_space=pl.ANY) for i in range(shards)},
        out_specs={
            0: pl.BlockSpec((1, rows, part), lambda k: (k, 0, 0)),
            1: pl.BlockSpec((1, rows, 2 * part), lambda k: (k, 0, 0)),
        },
        scratch=[
            pltpu.VMEM((rows, width), f32),
            pltpu.VMEM((rows, 128), f32),
            pltpu.VMEM((2, width, packed), bf16),
            pltpu.SemaphoreType.DMA((2,)),
        ],
    )


def expert_weights_kernel(scaled_ref, out_ref, share_ref, hidden_ref, grads_ref, *refs, shards):
    w_refs = refs[:shards]
    given_ref, kept_ref, picked_ref, st_ref, ot_ref, acc_ref, slots_ref, sems = refs[shards:]
    step = pl.program_id(0)
    part = hidden_ref.shape[2]

    def fetch(i, slot):
        return pltpu.make_async_copy(w_refs[i].at[:, 2 * part :], slots_ref.at[slot], sems.at[slot])

    @pl.when(step == 0)
    def _():
        fetch(0, 0).start()
        st_ref[...] = scaled_ref[...].T
        ot_ref[...] = out_ref[...].T
        acc_ref[...] = jnp.zeros_like(acc_ref)

    for i in range(1, shards):
        @pl.when(step == i - 1)
        def _(i=i):
            fetch(i, i % 2).start()

    slot = lax.rem(step, 2)
    fetch(0, slot).wait()

    def write(d_ref):
        d_ref[0, :, : 2 * part] = dot(st_ref[...], grads_ref[0]).astype(bf16)
        d_ref[0, :, 2 * part :] = dot(ot_ref[...], hidden_ref[0]).astype(bf16)

    @pl.when(step < shards // 2)
    def _():
        write(given_ref)

    @pl.when(step >= shards // 2)
    def _():
        write(kept_ref)

    acc_ref[...] += dot_nt(hidden_ref[0], slots_ref[slot])

    @pl.when(step == pl.num_programs(0) - 1)
    def _():
        picked_ref[...] = (share_ref[:, :1] * acc_ref[...]).astype(bf16)


def expert_weights(scaled, out_grads, share, hidden, grads, weights):
    rows, width = scaled.shape
    shards, packed = len(weights), weights[0].shape[1]
    part = packed // 3
    half = shards // 2
    return call(
        functools.partial(expert_weights_kernel, shards=shards),
        "expert_weights",
        (scaled, out_grads, share, hidden, grads, *weights),
        [((half, width, packed), bf16), ((half, width, packed), bf16), ((rows, width), bf16)],
        grid=(shards,),
        in_specs={
            3: pl.BlockSpec((1, rows, part), lambda k: (k, 0, 0)),
            4: pl.BlockSpec((1, rows, 2 * part), lambda k: (k, 0, 0)),
            **{5 + i: pl.BlockSpec(memory_space=pl.ANY) for i in range(shards)},
        },
        out_specs={
            0: pl.BlockSpec((1, width, packed), lambda k: (jnp.minimum(k, half - 1), 0, 0)),
            1: pl.BlockSpec((1, width, packed), lambda k: (jnp.maximum(k - half, 0), 0, 0)),
        },
        scratch=[
            pltpu.VMEM((width, rows), bf16),
            pltpu.VMEM((width, rows), bf16),
            pltpu.VMEM((rows, width), f32),
            pltpu.VMEM((2, width, part), bf16),
            pltpu.SemaphoreType.DMA((2,)),
        ],
    )


def combine_kernel(placer_ref, back_ref, share_ref, router_ref, shared_ref, part_ref, lg_ref, *, experts):
    width = shared_ref.shape[1]
    placer = placer_ref[...]
    lanes = lanes_of()
    dots = dot(placer, back_ref[:, width:])
    dots = jnp.where(lanes < experts, dots + pltpu.roll(dots, 128 - experts, 1), 0.0)
    share = share_ref[...]
    grads = (share * (dots - jnp.sum(share * dots, axis=1, keepdims=True))).astype(bf16)
    lg_ref[...] = grads
    total = shared_ref[...] + dot_nt(grads, router_ref[...]) + dot(placer, back_ref[:, :width])
    part_ref[...] = total.astype(bf16)


def back_two_kernel(middle_ref, mine_ref, theirs_ref, cot_ref, gain_ref, wo_ref, grads_ref, low_ref, mixed_ref, sum_ref):
    middle = middle_ref[...]
    scale = rms_scale(middle)
    upstream = mine_ref[...].astype(f32) + theirs_ref[...].astype(f32)
    sum_ref[...] = jnp.sum(upstream * (middle * scale), axis=0, keepdims=True)
    grads = cot_ref[...].astype(f32) + norm_back(middle, scale, gain_ref[...], upstream)
    grads_ref[...] = grads
    low = grads.astype(bf16)
    low_ref[...] = low
    mixed_ref[...] = dot_nt(low, wo_ref[...]).astype(bf16)


def normed_back_kernel(dq_ref, dka_ref, dva_ref, dkb_ref, dvb_ref, wq_ref, wk_ref, wv_ref, given_ref, y_ref, own_ref):
    rows = dq_ref.shape[0]
    wk, wv = wk_ref[...], wv_ref[...]

    def back(dk_ref, dv_ref, chunk):
        these = slice(chunk * rows, (chunk + 1) * rows)
        return dot_nt(dk_ref[these, :], wk) + dot_nt(dv_ref[these, :], wv)

    given_ref[0] = back(dka_ref, dva_ref, 1).astype(bf16)
    given_ref[1] = back(dkb_ref, dvb_ref, 1).astype(bf16)
    y_ref[...] = back(dkb_ref, dvb_ref, 0)
    own_ref[...] = back(dka_ref, dva_ref, 0) + dot_nt(dq_ref[...], wq_ref[...])


def first_kernel(x_ref, mine_ref, theirs_ref, grads_ref, gain_ref, out_ref):
    x = x_ref[...].astype(f32)
    upstream = mine_ref[...].astype(f32) + theirs_ref[...].astype(f32)
    out_ref[...] = grads_ref[...] + norm_back(x, rms_scale(x), gain_ref[...], upstream)


def sum_over_expert(halves):
    _, rows, columns = halves.shape
    kept = (halves[1].astype(f32) + swap(halves[0], "c").astype(f32)).astype(bf16)
    parts = exchange(kept.reshape(16, rows // 16, columns), PLANE)
    part = jnp.sum(parts.astype(f32), axis=0)
    part = pair_sum(part, "zh").astype(bf16)
    copies = jnp.broadcast_to(part[None], (16, rows // 16, columns))
    return exchange(copies, PLANE).reshape(rows, columns)


RING = 4
NEAR = [(0, 1), (1, 0), (2, 3), (3, 2)]
FAR = [(0, 3), (3, 0), (1, 2), (2, 1)]


def ring_steps():
    steps = []
    for axis in ("x", ("yh", "yl")):
        at = lax.axis_index(axis)
        steps.append((axis, NEAR, jnp.where((at == 1) | (at == 2), 1, 0)))
        steps.append((axis, FAR, jnp.where(at >= 2, 1, 0)))
    return steps


def half_sum(halves):
    return (halves[1].astype(f32) + swap(halves[0], "c").astype(f32)).astype(bf16)


def sum_by_neighbours(values, hold):
    steps = ring_steps()
    for at, (axis, pairs, bit) in enumerate(steps):
        kept, given = half_by(values, bit)
        taken = lax.ppermute(given, axis, pairs)
        if at < len(hold):
            taken = after(taken, hold[at])
        values = (kept.astype(f32) + taken.astype(f32)).astype(bf16)
    values = pair_sum(values, "zh").astype(bf16)
    for axis, pairs, bit in reversed(steps):
        theirs = lax.ppermute(values, axis, pairs)
        values = jnp.concatenate(
            [jnp.where(bit == 0, values, theirs), jnp.where(bit == 0, theirs, values)], axis=0
        )
    return values


def both_halves(mine, core):
    theirs = swap(mine, "c")
    return jnp.concatenate(
        [jnp.where(core == 0, mine, theirs), jnp.where(core == 0, theirs, mine)], axis=0
    ).astype(f32)


def local(
    tokens,
    routes,
    gain_one,
    w_query,
    w_key,
    w_value,
    w_output,
    gain_two,
    w_router,
    shared_gate,
    shared_up,
    shared_down,
    expert_gate,
    expert_up,
    expert_down,
    cotangent,
):
    rows, width = tokens.shape
    wide = w_query.shape[1]
    experts = w_router.shape[1]
    seats = experts * SLOTS
    part = expert_gate.shape[2]
    shared_part = shared_gate.shape[1]
    tensor = lax.axis_index("t")
    core = lax.axis_index("c")
    high = lax.axis_index("yl")
    expert_here = lax.axis_index(ROUTE)
    router = jnp.pad(w_router, ((0, 0), (0, 128 - experts)))
    of_rows = ((rows, width), f32)
    of_rows_low = ((rows, width), bf16)

    tokens_y = swap(tokens, "yl")
    tokens_c = swap(tokens, "c")
    tokens_yc = swap(tokens_y, "c")
    hide = jnp.stack([core < 0, core == 0, high == 0, high == 0])
    hide = jnp.where(hide, 1e30, 0.0).astype(f32)

    frequency = rope_base ** (-np.arange(HEAD_DIM // 2) * 2.0 / HEAD_DIM)
    frequency = np.tile(frequency, PAIR // (HEAD_DIM // 2))
    inner = np.arange(rows)[:, None] * frequency[None, :]
    starts = jnp.stack(
        [((high ^ my) * 2 + (core ^ mc)) * rows for my, mc in ((0, 0), (0, 1), (1, 0), (1, 1))]
    )
    outer = starts.astype(f32)[:, None, None] * frequency.astype(np.float32)[None, None, :]
    cos_in, sin_in = np.cos(inner).astype(np.float32), np.sin(inner).astype(np.float32)
    cos_out, sin_out = jnp.cos(outer), jnp.sin(outer)
    cosine = (cos_out * cos_in - sin_out * sin_in).reshape(2, 2 * rows, PAIR)
    sine = (sin_out * cos_in + cos_out * sin_in).reshape(2, 2 * rows, PAIR)

    placer, placer_turned, sent_cot = route(tensor, routes, cotangent, experts)
    normed_a, keys_a, values_a, query = project(
        tokens, tokens_c, gain_one[None], w_key, w_value, cosine[0], sine[0], w_query
    )
    cot_ext = exchange(sent_cot.reshape(experts, SLOTS, -1), ROUTE).reshape(seats, -1)
    normed_b, keys_b, values_b = project(
        after(tokens_y, (keys_a, sent_cot)), tokens_yc, gain_one[None], w_key, w_value, cosine[1], sine[1]
    )
    mixed_heads, logs, attended = attend(
        hide, query, keys_a, values_a, keys_b, values_b, w_output
    )

    own = jnp.concatenate([after(expert_gate[0], placer), expert_up[0], expert_down[0].T], axis=1)
    own_t = swap(own, "t")
    own_y = swap(after(own, keys_b), "yl")
    own_ty = swap(after(own_t, keys_b), "yl")
    own, own_t, own_y, own_ty = lax.optimization_barrier((own, own_t, own_y, own_ty, attended))[:4]
    weights = [own, own_t, own_y, own_ty]
    weights = [swap(w, "c") for w in weights] + weights

    middle, normed_two, sent_rows = call(
        second_kernel,
        "second",
        (tokens, attended, swap(attended, "t"), gain_two[None], placer_turned),
        [of_rows, of_rows_low, ((seats, width), bf16)],
    )

    rows_in = exchange(sent_rows.reshape(experts, SLOTS, width), ROUTE).reshape(seats, width)
    hidden_shared, shared_gg, shared_gu, shared_back, shared_out, share = shared(
        normed_two, cotangent, shared_gate, shared_up, shared_down, router, routes
    )
    hidden_expert, expert_grads, back, scaled_rows, out_grads, row_share = expert_rows(
        expert_here, after(rows_in, shared_back), cot_ext, router, weights, experts
    )
    back = exchange(back.reshape(experts, SLOTS, -1), ROUTE).reshape(seats, -1)
    given, kept, picked = expert_weights(
        scaled_rows, out_grads, row_share, hidden_expert, expert_grads, weights
    )

    back = after(back, given)
    mine, logits_grads = call(
        functools.partial(combine_kernel, experts=experts),
        "combine",
        (placer, back, share, router, shared_back),
        [of_rows_low, ((rows, 128), bf16)],
    )
    grads = half_sum((given, kept))
    upper, lower = grads[:, : width // 2], grads[:, width // 2 :]
    to_high, to_tensor = upper[2:], jnp.stack([lower[1], lower[3]])
    shared_gg = after(shared_gg, mine)
    early = half_call(
        shared_weights_kernel,
        "shared_weights",
        core,
        (normed_two, cotangent),
        (shared_gg, shared_gu, hidden_shared),
        3 * shared_part,
    )
    early = half_sum(early)
    theirs = after(swap(mine, "t"), (to_high, to_tensor))
    middle_grads, middle_low, mixed_grads, gain_sum = call(
        back_two_kernel,
        "back_two",
        (middle, mine, theirs, cotangent, gain_two[None], w_output),
        [of_rows, of_rows_low, ((rows, wide), bf16), ((1, width), f32)],
    )

    dq, dka, dva, dkb, dvb = attend_back(
        hide, query, keys_a, values_a, keys_b, values_b, mixed_heads, logs, mixed_grads,
        cosine[0], sine[0], cosine[1], sine[1],
    )
    from_high, from_tensor = swap(to_high, "yl"), swap(to_tensor, "t")
    dq, from_high, from_tensor = lax.optimization_barrier((dq, from_high, from_tensor))
    late = half_call(
        functools.partial(late_weights_kernel, experts=experts),
        "late_weights",
        core,
        (normed_a, normed_b, normed_two, middle_low, gain_sum),
        (dq, dka, dkb, dva, dvb, logits_grads, mixed_heads),
        4 * wide + 128,
    )
    dq = after(dq, late)
    to_core, to_y, own_part = call(
        normed_back_kernel,
        "normed_back",
        (dq, dka, dva, dkb, dvb, w_query, w_key, w_value),
        [((2, rows, width), bf16), of_rows, of_rows],
    )
    from_core = swap(to_core, "c").astype(f32)
    from_y = swap((to_y + from_core[1]).astype(bf16), "yl").astype(f32)
    own_part = (own_part + from_core[0] + from_y).astype(bf16)
    (grad_tokens,) = call(
        first_kernel,
        "first",
        (tokens, own_part, swap(own_part, "t"), middle_grads, gain_one[None]),
        [of_rows],
    )

    upper = (upper[:2].astype(f32) + from_high.astype(f32)).astype(bf16)
    lower = (jnp.stack([lower[0], lower[2]]).astype(f32) + from_tensor.astype(f32)).astype(bf16)
    upper = upper[0].astype(f32) + swap(upper[1], "t").astype(f32)
    lower = lower[0].astype(f32) + swap(lower[1], "yl").astype(f32)
    grads = jnp.concatenate([upper, lower], axis=0)
    grad_expert_gate = grads[None, :, :part]
    grad_expert_up = grads[None, :, part : 2 * part]
    grad_expert_down = grads[:, 2 * part :].T[None]

    early = both_halves(sum_by_neighbours(early, (dq, late, to_core)), core)

    picked = after(picked, mine)
    picked = exchange(picked.reshape(experts, SLOTS, width), ROUTE).reshape(seats, width)
    block_out = (middle + pair_sum(shared_out + dot(placer, picked), "t")).astype(bf16)

    late = both_halves(sum_over_expert(late), core)
    small = late[:, 4 * wide :]
    grad_router = small[:, :experts] + swap(small, "t")[:, :experts]
    gain_part = jnp.sum(
        late[:, : 3 * wide] * jnp.concatenate([w_query, w_key, w_value], axis=1).astype(f32), axis=1
    )
    grad_gain_one = (gain_part + swap(gain_part, "t")) / gain_one
    return (
        block_out,
        grad_tokens,
        grad_gain_one,
        late[:, :wide],
        late[:, wide : 2 * wide],
        late[:, 2 * wide : 3 * wide],
        late[:, 3 * wide : 4 * wide].T,
        small[:, experts],
        grad_router,
        early[:, :shared_part],
        early[:, shared_part : 2 * shared_part],
        early[:, 2 * shared_part :].T,
        grad_expert_gate,
        grad_expert_up,
        grad_expert_down,
    )


def solution(mesh):
    fine = Mesh(mesh.devices.reshape(2, 4, 2, 2, 2, 2), AXES)
    placed = (
        P(EXPERT, None),
        P(EXPERT, None),
        P(),
        P(None, "t"),
        P(None, "t"),
        P(None, "t"),
        P("t", None),
        P(),
        P(),
        P(None, "t"),
        P(None, "t"),
        P("t", None),
        P(EXPERT, None, "t"),
        P(EXPERT, None, "t"),
        P(EXPERT, "t", None),
        P(EXPERT, None),
    )
    return jax.shard_map(
        local,
        mesh=fine,
        in_specs=placed,
        out_specs=(
            P(EXPERT, None),
            P(EXPERT, None),
            P(),
            P(None, "t"),
            P(None, "t"),
            P(None, "t"),
            P("t", None),
            P(),
            P(),
            P(None, "t"),
            P(None, "t"),
            P("t", None),
            P(EXPERT, None, "t"),
            P(EXPERT, None, "t"),
            P(EXPERT, "t", None),
        ),
        check_vma=False,
    )
```

```python
import functools

import jax
import jax.numpy as jnp
import numpy as np
from jax import lax
from jax.experimental import pallas as pl
from jax.experimental.pallas import tpu as pltpu
from jax.sharding import Mesh
from jax.sharding import PartitionSpec as P

HEAD_DIM = 64
BLOCK = 256
SLOTS = 40
PAIR = 128
AXES = ("zh", "x", "yh", "yl", "c", "t")
EXPERT = AXES[:5]
ROUTE = ("zh", "x", "yh")
PLANE = ("x", "yh", "yl")

epsilon = 1e-06
rope_base = 10000.0
bf16 = jnp.bfloat16
f32 = jnp.float32
params = pltpu.CompilerParams(vmem_limit_bytes=52 << 20)


def swap(x, axis):
    return lax.ppermute(x, axis, [(0, 1), (1, 0)])


def exchange(x, axis):
    return lax.all_to_all(x, axis, split_axis=0, concat_axis=0, tiled=True)


def after(x, first):
    return lax.optimization_barrier((x, first))[0]


def dot(a, b, dims=((1,), (0,))):
    return lax.dot_general(a, b, (dims, ((), ())), preferred_element_type=f32)


def dot_nt(a, b):
    return dot(a, b, ((1,), (1,)))


def dot_tn(a, b):
    return dot(a, b, ((0,), (0,)))


def rms_scale(values):
    return lax.rsqrt(jnp.mean(values * values, axis=-1, keepdims=True) + epsilon)


def pair_sum(values, axis):
    low = values.astype(bf16)
    return low.astype(f32) + swap(low, axis).astype(f32)


def norm_back(inputs, row_scale, gain_row, upstream):
    unit_rows = inputs * row_scale
    scaled_grad = upstream * gain_row
    return row_scale * (
        scaled_grad - unit_rows * jnp.mean(scaled_grad * unit_rows, axis=-1, keepdims=True)
    )


RATE = 230000000
TIMES = dict(
    route=4,
    project=5,
    attend=14,
    attend_back=23,
    second=4,
    shared=12,
    expert_rows=20,
    expert_given=9,
    expert_kept=9,
    expert_sum=4,
    expert_sums=3,
    expert_out=3,
    combine=4,
    back_two=4,
    normed_back=8,
    first=4,
    shared_weights=6,
    late_weights=8,
    early_out=5,
    turn_rows=3,
    half_sum=4,
    late_out=4,
)


def turn(values, cos, sin):
    half = HEAD_DIM // 2
    lanes = lax.broadcasted_iota(jnp.int32, values.shape, 1)
    first = (lanes // half) % 2 == 0
    size = values.shape[1]
    other = jnp.where(first, -pltpu.roll(values, size - half, 1), pltpu.roll(values, half, 1))
    return values * cos + other * sin


def whole(shape):
    return pl.BlockSpec(shape, lambda *_: (0,) * len(shape))


def call(kernel, name, args, outs, smem=(), grid=None, in_specs=None, out_specs=None, scratch=()):
    in_specs = dict(in_specs or {})
    out_specs = dict(out_specs or {})
    for i in smem:
        in_specs[i] = pl.BlockSpec(memory_space=pltpu.SMEM)
    return pl.pallas_call(
        kernel,
        **({} if grid is None else {"grid": grid}),
        in_specs=[in_specs.get(i, whole(a.shape)) for i, a in enumerate(args)],
        out_specs=[out_specs.get(i, whole(s)) for i, (s, _) in enumerate(outs)],
        out_shape=[jax.ShapeDtypeStruct(s, d) for s, d in outs],
        scratch_shapes=scratch,
        compiler_params=params,
        cost_estimate=pl.CostEstimate(flops=TIMES[name] * RATE, bytes_accessed=1 << 20, transcendentals=0),
        name=name,
    )(*args)


def lanes_of(rows=1, count=128):
    return lax.broadcasted_iota(jnp.int32, (rows, count), 1)


def route_kernel(tensor_ref, routes_ref, cot_ref, expand_ref, seat_ref, placer_ref, turned_ref, sent_ref):
    routes = routes_ref[...]
    rows, width = cot_ref.shape
    lanes = lanes_of(rows)
    member = (routes[:, 0:1] == lanes) | (routes[:, 1:2] == lanes)
    earlier = lax.broadcasted_iota(jnp.int32, (rows, rows), 0) > lanes_of(rows, rows)
    count = dot(
        jnp.where(earlier, 1.0, 0.0).astype(bf16), jnp.where(member, 1.0, 0.0).astype(bf16)
    )
    offset = (tensor_ref[0] * SLOTS).astype(f32)
    place = jnp.where(member, count - offset, -1.0).astype(bf16)
    placer = jnp.where(dot(place, expand_ref[...]) == seat_ref[...], 1.0, 0.0).astype(bf16)
    placer_ref[...] = placer
    turned = placer.T
    turned_ref[...] = turned
    sent_ref[:, :width] = dot(turned, cot_ref[...]).astype(bf16)
    sums = (routes[:, 0:1] + routes[:, 1:2]).astype(f32)
    sent_ref[:, width:] = dot(turned, jnp.where(lanes == 0, sums, 0.0).astype(bf16)).astype(bf16)


def route(tensor, routes, cotangent, experts):
    rows, width = cotangent.shape
    seats = experts * SLOTS
    columns = np.arange(seats)
    expand = jnp.asarray(np.arange(128)[:, None] == columns[None, :] // SLOTS, bf16)
    seat = jnp.asarray((columns % SLOTS)[None], f32)
    return call(
        route_kernel,
        "route",
        (tensor[None], routes, cotangent, expand, seat),
        [((rows, seats), bf16), ((seats, rows), bf16), ((seats, width + 128), bf16)],
        smem=(0,),
    )


def project_kernel(x0_ref, x1_ref, gain_ref, wk_ref, wv_ref, cos_ref, sin_ref, *rest):
    wq_ref = rest[0] if len(rest) == 5 else None
    n_ref, k_ref, v_ref = rest[-4:-1] if wq_ref is not None else rest
    for chunk, x_ref in enumerate((x0_ref, x1_ref)):
        rows = x_ref.shape[0]
        at_rows = slice(chunk * rows, (chunk + 1) * rows)
        x = x_ref[...].astype(f32)
        normed = (x * rms_scale(x) * gain_ref[...]).astype(bf16)
        n_ref[at_rows, :] = normed
        cos, sin = cos_ref[at_rows, :], sin_ref[at_rows, :]
        key = dot(normed, wk_ref[...])
        for at in range(0, key.shape[1], PAIR):
            lanes = slice(at, at + PAIR)
            k_ref[at_rows, lanes] = turn(key[:, lanes], cos, sin).astype(bf16)
        v_ref[at_rows, :] = dot(normed, wv_ref[...]).astype(bf16)
        if chunk == 0 and wq_ref is not None:
            q_ref = rest[-1]
            query = dot(normed, wq_ref[...])
            for at in range(0, query.shape[1], PAIR):
                lanes = slice(at, at + PAIR)
                turned = turn(query[:, lanes], cos, sin).astype(bf16)
                q_ref[:, lanes] = turned * (HEAD_DIM**-0.5)


def project(first, second, gain, w_key, w_value, cos, sin, w_query=None):
    rows, width = first.shape
    wide = w_key.shape[1]
    outs = [((2 * rows, width), bf16), ((2 * rows, wide), bf16), ((2 * rows, wide), bf16)]
    args = (first, second, gain, w_key, w_value, cos, sin)
    if w_query is not None:
        args += (w_query,)
        outs.append(((rows, wide), bf16))
    return call(project_kernel, "project", args, outs)


def attend_kernel(hide_ref, q_ref, ka_ref, va_ref, kb_ref, vb_ref, wo_ref, o_ref, lse_ref, part_ref, acc_ref):
    lanes = lanes_of()
    span = 2 * BLOCK
    step = pl.program_id(0)
    for half in range(2):
        rows = slice(half * BLOCK, (half + 1) * BLOCK)
        q = q_ref[rows, :]
        outs, logs = [], []
        for head in range(2):
            query = jnp.where(lanes // HEAD_DIM == head, q, jnp.zeros_like(q))
            spans = [(ka_ref, va_ref, 0, BLOCK * (half + 1), 0.0), (ka_ref, va_ref, span, span, hide_ref[1])]
            spans += [(kb_ref, vb_ref, 0, span, hide_ref[2]), (kb_ref, vb_ref, span, span, hide_ref[3])]
            scores = [dot_nt(query, k[a : a + n, :]) for k, _, a, n, _ in spans]
            tops = [jnp.max(s, axis=1, keepdims=True) - x[4] for s, x in zip(scores, spans)]
            top = functools.reduce(jnp.maximum, tops)
            total, acc = 0.0, 0.0
            for s, (_, v, a, n, off) in zip(scores, spans):
                p = jnp.exp(s - (top + off))
                total = total + jnp.sum(p, axis=1, keepdims=True)
                acc = acc + dot(p.astype(bf16), v[a : a + n, :])
            outs.append(acc / total)
            logs.append(top + jnp.log(total))
        mixed = jnp.where(lanes < HEAD_DIM, outs[0], outs[1]).astype(bf16)
        o_ref[rows, :] = mixed
        lse_ref[rows, :] = jnp.where(lanes < HEAD_DIM, logs[0], logs[1])
    part = dot(o_ref[...], wo_ref[...])

    @pl.when(step == 0)
    def _():
        acc_ref[...] = part

    @pl.when(step > 0)
    def _():
        acc_ref[...] += part

    @pl.when(step == pl.num_programs(0) - 1)
    def _():
        part_ref[...] = acc_ref[...].astype(bf16)


def attend(hide, q, ka, va, kb, vb, w_output):
    rows, keys = q.shape[0], ka.shape[0]
    width = w_output.shape[1]
    of_q = pl.BlockSpec((rows, PAIR), lambda p: (0, p))
    of_k = pl.BlockSpec((keys, PAIR), lambda p: (0, p))
    return call(
        attend_kernel,
        "attend",
        (hide, q, ka, va, kb, vb, w_output),
        [(q.shape, bf16), (q.shape, f32), ((rows, width), bf16)],
        smem=(0,),
        grid=(q.shape[1] // PAIR,),
        in_specs={1: of_q, 2: of_k, 3: of_k, 4: of_k, 5: of_k, 6: pl.BlockSpec((PAIR, width), lambda p: (p, 0))},
        out_specs={0: of_q, 1: of_q},
        scratch=[pltpu.VMEM((rows, width), f32)],
    )


def attend_back_kernel(
    hide_ref, q_ref, ka_ref, va_ref, kb_ref, vb_ref, o_ref, lse_ref, g_ref, ca_ref, sa_ref, cb_ref, sb_ref,
    dq_ref, dka_ref, dva_ref, dkb_ref, dvb_ref,
):
    lanes = lanes_of()
    q, g = q_ref[...], g_ref[...]
    rows = q.shape[0]
    deltas = (g.astype(f32) * o_ref[...].astype(f32)).T
    logs = lse_ref[...].T
    dq = 0.0
    near = (ka_ref, va_ref, ca_ref, sa_ref, dka_ref, dva_ref)
    far = (kb_ref, vb_ref, cb_ref, sb_ref, dkb_ref, dvb_ref)
    for block in range(8):
        k_ref, v_ref, cos_ref, sin_ref, dk_ref, dv_ref = near if block < 4 else far
        off = 0.0 if block < 2 else hide_ref[block // 2]
        first = BLOCK if block == 1 else 0
        keys = slice((block % 4) * BLOCK, (block % 4 + 1) * BLOCK)
        k, v = k_ref[keys, :], v_ref[keys, :]
        dk, dv = 0.0, 0.0
        for head in range(2):
            mine = lanes // HEAD_DIM == head
            low = head * HEAD_DIM
            query = jnp.where(mine, q[first:, :], jnp.zeros_like(q[first:, :]))
            grads = jnp.where(mine, g[first:, :], jnp.zeros_like(g[first:, :]))
            key = jnp.where(mine, k, jnp.zeros_like(k))
            log = logs[low : low + 1, first:] + off
            delta = jnp.sum(deltas[low : low + HEAD_DIM, first:], axis=0, keepdims=True)
            p = jnp.exp(dot_nt(k, query) - log)
            ds = (p * (dot_nt(v, grads) - delta)).astype(bf16)
            dv = dv + dot(p.astype(bf16), grads)
            dk = dk + dot(ds, query)
            part = dot_tn(ds, key)
            if first:
                part = jnp.concatenate([jnp.zeros((first, PAIR), f32), part], axis=0)
            dq = dq + part
        dv_ref[keys, :] = dv.astype(bf16)
        dk_ref[keys, :] = turn(dk, cos_ref[keys, :], -sin_ref[keys, :]).astype(bf16)
    dq = dq * (HEAD_DIM**-0.5)
    dq_ref[...] = turn(dq, ca_ref[:rows, :], -sa_ref[:rows, :]).astype(bf16)


def attend_back(hide, q, ka, va, kb, vb, o, lse, g, ca, sa, cb, sb):
    rows, keys = q.shape[0], ka.shape[0]
    of_q = pl.BlockSpec((rows, PAIR), lambda p: (0, p))
    of_k = pl.BlockSpec((keys, PAIR), lambda p: (0, p))
    return call(
        attend_back_kernel,
        "attend_back",
        (hide, q, ka, va, kb, vb, o, lse, g, ca, sa, cb, sb),
        [(q.shape, bf16)] + [(ka.shape, bf16)] * 4,
        smem=(0,),
        grid=(q.shape[1] // PAIR,),
        in_specs={1: of_q, 2: of_k, 3: of_k, 4: of_k, 5: of_k, 6: of_q, 7: of_q, 8: of_q},
        out_specs={0: of_q, 1: of_k, 2: of_k, 3: of_k, 4: of_k},
    )


def turn_rows_kernel(a_ref, b_ref, ta_ref, tb_ref):
    ta_ref[...] = a_ref[...].T
    tb_ref[...] = b_ref[...].T


def half_sum_kernel(kept_ref, taken_ref, out_ref):
    out_ref[...] = (kept_ref[...].astype(f32) + taken_ref[...].astype(f32)).astype(bf16)


def second_kernel(x_ref, mine_ref, theirs_ref, gain_ref, turned_ref, cot_ref, middle_ref, n_ref, sent_ref):
    middle = x_ref[...].astype(f32) + (mine_ref[...].astype(f32) + theirs_ref[...].astype(f32))
    middle_ref[...] = middle
    normed = (middle * rms_scale(middle) * gain_ref[...]).astype(bf16)
    n_ref[...] = normed
    width = normed.shape[1]
    sent_ref[:, :width] = dot(turned_ref[...], normed).astype(bf16)
    sent_ref[:, width:] = cot_ref[...]


def swish(gate, up, grads):
    sigmoid = jax.nn.sigmoid(gate)
    unit = gate * sigmoid
    slope = sigmoid + unit * (1.0 - sigmoid)
    return (unit * up).astype(bf16), (grads * up * slope).astype(bf16), (grads * unit).astype(bf16)


def shared_kernel(
    n_ref, cot_ref, sg_ref, su_ref, sd_ref, router_ref, routes_ref, h_ref, gg_ref, gu_ref, back_ref, out_ref, share_ref
):
    normed, cot = n_ref[...], cot_ref[...]
    sg, su, sd = sg_ref[...], su_ref[...], sd_ref[...]
    hidden, gg, gu = swish(dot(normed, sg), dot(normed, su), dot_nt(cot, sd))
    h_ref[...], gg_ref[...], gu_ref[...] = hidden, gg, gu
    back = dot_nt(gg, sg) + dot_nt(gu, su)
    out = dot(hidden, sd)

    @pl.when(pl.program_id(0) == 0)
    def _():
        back_ref[...] = back
        out_ref[...] = out
        logits = dot(normed, router_ref[...])
        routes = routes_ref[...]
        lanes = lanes_of()
        first, second = lanes == routes[:, 0:1], lanes == routes[:, 1:2]
        one = jnp.sum(jnp.where(first, logits, 0.0), axis=1, keepdims=True)
        two = jnp.sum(jnp.where(second, logits, 0.0), axis=1, keepdims=True)
        top = jnp.maximum(one, two)
        one, two = jnp.exp(one - top), jnp.exp(two - top)
        share_ref[...] = (jnp.where(first, one, 0.0) + jnp.where(second, two, 0.0)) / (one + two)

    @pl.when(pl.program_id(0) > 0)
    def _():
        back_ref[...] += back
        out_ref[...] += out


def shared(normed, cot, shared_gate, shared_up, shared_down, router, routes):
    rows, width = normed.shape
    hidden = shared_gate.shape[1]
    block = 256
    columns = pl.BlockSpec((width, block), lambda k: (0, k))
    of_hidden = pl.BlockSpec((rows, block), lambda k: (0, k))
    return call(
        shared_kernel,
        "shared",
        (normed, cot, shared_gate, shared_up, shared_down, router, routes),
        [((rows, hidden), bf16)] * 3 + [((rows, width), f32)] * 2 + [((rows, 128), f32)],
        grid=(hidden // block,),
        in_specs={2: columns, 3: columns, 4: pl.BlockSpec((block, width), lambda k: (k, 0))},
        out_specs={0: of_hidden, 1: of_hidden, 2: of_hidden},
    )


def store_half(given_ref, kept_ref, at, value):
    value = value.astype(bf16)

    @pl.when(pl.program_id(0) == 0)
    def _():
        given_ref[:, at : at + value.shape[1]] = value

    @pl.when(pl.program_id(0) == 1)
    def _():
        kept_ref[:, at : at + value.shape[1]] = value


def shared_weights_kernel(core_ref, n_ref, cot_ref, gg_ref, gu_ref, h_ref, given_ref, kept_ref):
    part = h_ref.shape[1]
    turned = n_ref[...].T
    store_half(given_ref, kept_ref, 0, dot(turned, gg_ref[...]))
    store_half(given_ref, kept_ref, part, dot(turned, gu_ref[...]))
    store_half(given_ref, kept_ref, 2 * part, dot(cot_ref[...].T, h_ref[...]))


def half_call(kernel, name, core, halved, full, columns, by_rows=()):
    half = halved[0].shape[1] // 2
    specs = [pl.BlockSpec((a.shape[0], half), lambda s, c: (0, jnp.where(s == 0, 1 - c[0], c[0]))) for a in halved]
    specs += [
        pl.BlockSpec((half, a.shape[1]), lambda s, c: (jnp.where(s == 0, 1 - c[0], c[0]), 0))
        for a in by_rows
    ]
    specs += [pl.BlockSpec(a.shape, lambda s, c: (0, 0)) for a in full]
    return pl.pallas_call(
        kernel,
        grid_spec=pltpu.PrefetchScalarGridSpec(
            num_scalar_prefetch=1,
            grid=(2,),
            in_specs=specs,
            out_specs=[pl.BlockSpec((half, c), lambda s, c: (0, 0)) for c in columns for _ in range(2)],
        ),
        out_shape=[jax.ShapeDtypeStruct((half, c), bf16) for c in columns for _ in range(2)],
        compiler_params=params,
        cost_estimate=pl.CostEstimate(flops=TIMES[name] * RATE, bytes_accessed=1 << 20, transcendentals=0),
        name=name,
    )(core[None], *halved, *by_rows, *full)


def late_weights_kernel(
    core_ref, n2_ref, low_ref, gain_ref, scale_ref, ta_ref, tb_ref, wq_ref, wk_ref, wv_ref,
    dq_ref, dka_ref, dkb_ref, dva_ref, dvb_ref, lg_ref, o_ref, given_ref, kept_ref, small_given_ref, small_kept_ref, *, experts
):
    def column(row_ref):
        return jnp.broadcast_to(row_ref[...], (128, row_ref.shape[1])).T

    wide = dq_ref.shape[1]
    rows = dq_ref.shape[0]
    ta, tb = ta_ref[...], tb_ref[...]
    grad_q = dot(ta[:, :rows], dq_ref[...])
    grad_k = dot(ta, dka_ref[...]) + dot(tb, dkb_ref[...])
    grad_v = dot(ta, dva_ref[...]) + dot(tb, dvb_ref[...])
    for i, value in enumerate((grad_q, grad_k, grad_v, dot(low_ref[...].T, o_ref[...]))):
        store_half(given_ref, kept_ref, i * wide, value)
    small = dot(n2_ref[...].T, lg_ref[...])
    terms = grad_q * wq_ref[...].astype(f32) + grad_k * wk_ref[...].astype(f32) + grad_v * wv_ref[...].astype(f32)
    gain_one = jnp.sum(terms, axis=1, keepdims=True) / column(scale_ref)
    lanes = lanes_of()
    small = jnp.where(lanes == experts, 0.5 * column(gain_ref), small)
    store_half(small_given_ref, small_kept_ref, 0, jnp.where(lanes == experts + 1, gain_one, small))


def expert_kernel(
    here_ref, sent_ref, router_ref, *refs, experts, shards
):
    w_refs = refs[:shards]
    hidden_ref, grads_ref, back_ref, scaled_ref, out_ref, share_ref, acc_ref, dots_ref, slots_ref, sems = refs[shards:]
    step = pl.program_id(0)
    width = router_ref.shape[0]

    def fetch(i, slot):
        return pltpu.make_async_copy(w_refs[i], slots_ref.at[slot], sems.at[slot])

    @pl.when(step == 0)
    def _():
        fetch(0, 0).start()

    for i in range(1, shards):
        @pl.when(step == i - 1)
        def _(i=i):
            fetch(i, i % 2).start()

    slot = lax.rem(step, 2)
    fetch(0, slot).wait()
    w = slots_ref.at[slot]
    part = w.shape[1] // 3
    half = sent_ref.shape[0] // 2
    w_in, w_down = w[:, : 2 * part], w[:, 2 * part :]
    for at in (0, half):
        these = slice(at, at + half)
        rows, cot = sent_ref[these, :width], sent_ref[these, width : 2 * width]
        both = dot(rows, w_in)
        hidden_grads = dot(cot, w_down)
        hidden, gg, gu = swish(both[:, :part], both[:, part:], hidden_grads)
        hidden_ref[0, these, :] = hidden
        grads_ref[0, these, :part] = gg
        grads_ref[0, these, part:] = gu
        product = hidden.astype(f32) * hidden_grads
        product = functools.reduce(jnp.add, [product[:, a : a + 128] for a in range(0, part, 128)])
        back = dot_nt(gg, w[:, :part]) + dot_nt(gu, w[:, part : 2 * part])
        acc_ref[these, :] = jnp.where(step == 0, 0.0, acc_ref[these, :]) + back
        dots_ref[these, :] = jnp.where(step == 0, 0.0, dots_ref[these, :]) + product

    @pl.when(step == pl.num_programs(0) - 1)
    def _():
        rows, cot = sent_ref[:, :width], sent_ref[:, width : 2 * width]
        here = here_ref[0]
        lanes = lanes_of()
        logits = dot(rows, router_ref[...])
        other = sent_ref[:, 2 * width :].astype(f32)[:, :1].astype(jnp.int32) - here
        own_logit = jnp.sum(jnp.where(lanes == here, logits, 0.0), axis=1, keepdims=True)
        other_logit = jnp.sum(jnp.where(lanes == other, logits, 0.0), axis=1, keepdims=True)
        top = jnp.maximum(own_logit, other_logit)
        own = jnp.exp(own_logit - top)
        share = own / (own + jnp.exp(other_logit - top))
        share_ref[...] = jnp.broadcast_to(share, share_ref.shape)
        scaled_ref[...] = (share * rows.astype(f32)).astype(bf16)
        out_ref[...] = (share * cot.astype(f32)).astype(bf16)
        back_ref[:, :width] = (share * acc_ref[...]).astype(bf16)
        dots = jnp.sum(dots_ref[...], axis=1, keepdims=True)
        high = dots.astype(bf16).astype(f32)
        back_ref[:, width:] = (
            jnp.where(lanes == here, high, 0.0)
            + jnp.where(lanes == experts + here, dots - high, 0.0)
        ).astype(bf16)


def expert_rows(here, sent, router, weights, experts):
    rows, width = sent.shape[0], router.shape[0]
    shards, packed = len(weights), weights[0].shape[1]
    part = packed // 3
    return call(
        functools.partial(expert_kernel, experts=experts, shards=shards),
        "expert_rows",
        (here[None], sent, router, *weights),
        [
            ((shards, rows, part), bf16),
            ((shards, rows, 2 * part), bf16),
            ((rows, width + 128), bf16),
            ((rows, width), bf16),
            ((rows, width), bf16),
            ((rows, 128), f32),
        ],
        smem=(0,),
        grid=(shards,),
        in_specs={3 + i: pl.BlockSpec(memory_space=pl.ANY) for i in range(shards)},
        out_specs={
            0: pl.BlockSpec((1, rows, part), lambda k: (k, 0, 0)),
            1: pl.BlockSpec((1, rows, 2 * part), lambda k: (k, 0, 0)),
        },
        scratch=[
            pltpu.VMEM((rows, width), f32),
            pltpu.VMEM((rows, 128), f32),
            pltpu.VMEM((2, width, packed), bf16),
            pltpu.SemaphoreType.DMA((2,)),
        ],
    )


def expert_given_kernel(scaled_ref, out_ref, hidden_ref, grads_ref, *refs, shards):
    w_refs = refs[:shards]
    d_ref, acc_ref, st_ref, ot_ref, slots_ref, sems = refs[shards:]
    step = pl.program_id(0)

    @pl.when(step == 0)
    def _():
        st_ref[...] = scaled_ref[...].T
        ot_ref[...] = out_ref[...].T

    expert_step(step, st_ref, ot_ref, hidden_ref, grads_ref, w_refs, d_ref, slots_ref, sems, acc_ref, None)


def expert_kept_kernel(st_ref, ot_ref, share_ref, first_ref, hidden_ref, grads_ref, *refs, shards):
    w_refs = refs[:shards]
    d_ref, picked_ref, acc_ref, slots_ref, sems = refs[shards:]
    step = pl.program_id(0)
    expert_step(step, st_ref, ot_ref, hidden_ref, grads_ref, w_refs, d_ref, slots_ref, sems, acc_ref, first_ref)

    @pl.when(step == pl.num_programs(0) - 1)
    def _():
        picked_ref[...] = (share_ref[:, :1] * acc_ref[...]).astype(bf16)


def expert_step(step, st_ref, ot_ref, hidden_ref, grads_ref, w_refs, d_ref, slots_ref, sems, acc_ref, first_ref):
    part = hidden_ref.shape[2]

    def fetch(i, slot):
        return pltpu.make_async_copy(w_refs[i].at[:, 2 * part :], slots_ref.at[slot], sems.at[slot])

    @pl.when(step == 0)
    def _():
        fetch(0, 0).start()
        acc_ref[...] = jnp.zeros_like(acc_ref) if first_ref is None else first_ref[...]

    for i in range(1, len(w_refs)):
        @pl.when(step == i - 1)
        def _(i=i):
            fetch(i, i % 2).start()

    slot = lax.rem(step, 2)
    fetch(0, slot).wait()
    d_ref[0, :, : 2 * part] = dot(st_ref[...], grads_ref[0]).astype(bf16)
    d_ref[0, :, 2 * part :] = dot(ot_ref[...], hidden_ref[0]).astype(bf16)
    acc_ref[...] += dot_nt(hidden_ref[0], slots_ref[slot])


def expert_half(kernel, name, args, hidden, grads, weights, at, extra):
    shards = len(weights)
    _, rows, part = hidden.shape
    width = weights[0].shape[0]
    count = len(args)
    return call(
        functools.partial(kernel, shards=shards),
        name,
        (*args, hidden, grads, *weights),
        [((shards, width, 3 * part), bf16), *extra],
        grid=(shards,),
        in_specs={
            count: pl.BlockSpec((1, rows, part), lambda k: (k + at, 0, 0)),
            count + 1: pl.BlockSpec((1, rows, 2 * part), lambda k: (k + at, 0, 0)),
            **{count + 2 + i: pl.BlockSpec(memory_space=pl.ANY) for i in range(shards)},
        },
        out_specs={0: pl.BlockSpec((1, width, 3 * part), lambda k: (k, 0, 0))},
        scratch=([pltpu.VMEM((rows, width), f32)] if at else [])
        + [pltpu.VMEM((2, width, part), bf16), pltpu.SemaphoreType.DMA((2,))],
    )


def expert_sum_kernel(kept_ref, taken_ref, high_ref, tensor_ref, keep_high_ref, keep_tensor_ref):
    shard = pl.program_id(0)
    half = kept_ref.shape[1] // 2
    total = (kept_ref[0].astype(f32) + taken_ref[0].astype(f32)).astype(bf16)
    for ref, at, here in (
        (keep_high_ref, 0, shard < 2),
        (high_ref, 0, shard >= 2),
        (keep_tensor_ref, half, shard % 2 == 0),
        (tensor_ref, half, shard % 2 == 1),
    ):
        @pl.when(here)
        def _(ref=ref, at=at):
            ref[0] = total[at : at + half]


def expert_sums_kernel(kh_ref, fh_ref, kt_ref, ft_ref, to_t_ref, to_y_ref, kept_u_ref, kept_l_ref):
    to_t_ref[...] = (kh_ref[1].astype(f32) + fh_ref[1].astype(f32)).astype(bf16)
    to_y_ref[...] = (kt_ref[1].astype(f32) + ft_ref[1].astype(f32)).astype(bf16)
    kept_u_ref[...] = (kh_ref[0].astype(f32) + fh_ref[0].astype(f32)).astype(bf16)
    kept_l_ref[...] = (kt_ref[0].astype(f32) + ft_ref[0].astype(f32)).astype(bf16)


def expert_out_kernel(ku_ref, fu_ref, kl_ref, fl_ref, gate_ref, up_ref, down_ref):
    half = ku_ref.shape[0]
    part = gate_ref.shape[2]
    for at, (kept_ref, from_ref) in ((0, (ku_ref, fu_ref)), (half, (kl_ref, fl_ref))):
        total = kept_ref[...].astype(f32) + from_ref[...].astype(f32)
        gate_ref[0, at : at + half, :] = total[:, :part]
        up_ref[0, at : at + half, :] = total[:, part : 2 * part]
        down_ref[0, :, at : at + half] = total[:, 2 * part :].T


def combine_kernel(placer_ref, back_ref, share_ref, router_ref, shared_ref, part_ref, lg_ref, *, experts):
    width = shared_ref.shape[1]
    placer = placer_ref[...]
    lanes = lanes_of()
    dots = dot(placer, back_ref[:, width:])
    dots = jnp.where(lanes < experts, dots + pltpu.roll(dots, 128 - experts, 1), 0.0)
    share = share_ref[...]
    grads = (share * (dots - jnp.sum(share * dots, axis=1, keepdims=True))).astype(bf16)
    lg_ref[...] = grads
    total = shared_ref[...] + dot_nt(grads, router_ref[...]) + dot(placer, back_ref[:, :width])
    part_ref[...] = total.astype(bf16)


def back_two_kernel(middle_ref, mine_ref, theirs_ref, cot_ref, gain_ref, wo_ref, grads_ref, low_ref, mixed_ref, sum_ref):
    middle = middle_ref[...]
    scale = rms_scale(middle)
    upstream = mine_ref[...].astype(f32) + theirs_ref[...].astype(f32)
    sum_ref[...] = jnp.sum(upstream * (middle * scale), axis=0, keepdims=True)
    grads = cot_ref[...].astype(f32) + norm_back(middle, scale, gain_ref[...], upstream)
    grads_ref[...] = grads
    low = grads.astype(bf16)
    low_ref[...] = low
    mixed_ref[...] = dot_nt(low, wo_ref[...]).astype(bf16)


def normed_back_kernel(dq_ref, dka_ref, dva_ref, dkb_ref, dvb_ref, wq_ref, wk_ref, wv_ref, core_ref, far_ref, y_ref, own_ref):
    rows = dq_ref.shape[0]
    wk, wv = wk_ref[...], wv_ref[...]

    def back(dk_ref, dv_ref, chunk):
        these = slice(chunk * rows, (chunk + 1) * rows)
        return dot_nt(dk_ref[these, :], wk) + dot_nt(dv_ref[these, :], wv)

    far_ref[...] = back(dkb_ref, dvb_ref, 1).astype(bf16)
    core_ref[...] = back(dka_ref, dva_ref, 1).astype(bf16)
    y_ref[...] = back(dkb_ref, dvb_ref, 0)
    own_ref[...] = back(dka_ref, dva_ref, 0) + dot_nt(dq_ref[...], wq_ref[...])


def first_kernel(x_ref, mine_ref, theirs_ref, grads_ref, gain_ref, out_ref):
    x = x_ref[...].astype(f32)
    upstream = mine_ref[...].astype(f32) + theirs_ref[...].astype(f32)
    out_ref[...] = grads_ref[...] + norm_back(x, rms_scale(x), gain_ref[...], upstream)


def spread(part):
    copies = jnp.broadcast_to(part[None], (16,) + part.shape)
    return exchange(copies, PLANE).reshape(-1, part.shape[1])


def late_out_kernel(core_ref, mine_ref, theirs_ref, q_ref, k_ref, v_ref, o_ref, small_ref):
    half, wide = mine_ref.shape[0], q_ref.shape[1]
    for at, ref in ((0, mine_ref), (1, theirs_ref)):
        place = core_ref[0] if at == 0 else 1 - core_ref[0]
        these = pl.ds(pl.multiple_of(place * half, 128), half)
        for i, out_ref in enumerate((q_ref, k_ref, v_ref)):
            out_ref[these, :] = ref[:, i * wide : (i + 1) * wide].astype(f32)
        o_ref[:, these] = ref[:, 3 * wide : 4 * wide].astype(f32).T
        small_ref[these, :] = ref[:, 4 * wide :].astype(f32)


def early_out_kernel(core_ref, mine_ref, theirs_ref, gate_ref, up_ref, down_ref):
    half, wide = mine_ref.shape[0], gate_ref.shape[1]
    for at, ref in ((0, mine_ref), (1, theirs_ref)):
        place = core_ref[0] if at == 0 else 1 - core_ref[0]
        these = pl.ds(pl.multiple_of(place * half, 128), half)
        for i, out_ref in enumerate((gate_ref, up_ref)):
            out_ref[these, :] = ref[:, i * wide : (i + 1) * wide].astype(f32)
        down_ref[:, these] = ref[:, 2 * wide :].astype(f32).T


def local(
    tokens,
    routes,
    gain_one,
    w_query,
    w_key,
    w_value,
    w_output,
    gain_two,
    w_router,
    shared_gate,
    shared_up,
    shared_down,
    expert_gate,
    expert_up,
    expert_down,
    cotangent,
):
    rows, width = tokens.shape
    wide = w_query.shape[1]
    experts = w_router.shape[1]
    seats = experts * SLOTS
    part = expert_gate.shape[2]
    shared_part = shared_gate.shape[1]
    tensor = lax.axis_index("t")
    core = lax.axis_index("c")
    high = lax.axis_index("yl")
    expert_here = lax.axis_index(ROUTE)
    router = jnp.pad(w_router, ((0, 0), (0, 128 - experts)))
    of_rows = ((rows, width), f32)
    of_rows_low = ((rows, width), bf16)

    tokens_y = swap(tokens, "yl")
    tokens_c = swap(tokens, "c")
    hide = jnp.stack([core < 0, core == 0, high == 0, high == 0])
    hide = jnp.where(hide, 1e30, 0.0).astype(f32)

    frequency = rope_base ** (-np.arange(HEAD_DIM // 2) * 2.0 / HEAD_DIM)
    frequency = np.tile(frequency, PAIR // (HEAD_DIM // 2))
    inner = np.arange(rows)[:, None] * frequency[None, :]
    starts = jnp.stack(
        [((high ^ my) * 2 + (core ^ mc)) * rows for my, mc in ((0, 0), (0, 1), (1, 0), (1, 1))]
    )
    outer = starts.astype(f32)[:, None, None] * frequency.astype(np.float32)[None, None, :]
    cos_in, sin_in = np.cos(inner).astype(np.float32), np.sin(inner).astype(np.float32)
    cos_out, sin_out = jnp.cos(outer), jnp.sin(outer)
    cosine = (cos_out * cos_in - sin_out * sin_in).reshape(2, 2 * rows, PAIR)
    sine = (sin_out * cos_in + cos_out * sin_in).reshape(2, 2 * rows, PAIR)

    own = jnp.concatenate([expert_gate[0], expert_up[0], expert_down[0].T], axis=1)
    placer, placer_turned, sent_cot = route(tensor, routes, cotangent, experts)
    normed_a, keys_a, values_a, query = project(
        tokens, tokens_c, gain_one[None], w_key, w_value, cosine[0], sine[0], w_query
    )
    tokens_y, keys_a, placer, placer_turned, sent_cot, own_later = lax.optimization_barrier(
        (tokens_y, keys_a, placer, placer_turned, sent_cot, own)
    )
    tokens_yc = swap(tokens_y, "c")
    own_t, own_y = swap(own, "t"), swap(own_later, "yl")
    normed_b, keys_b, values_b = project(
        tokens_y, tokens_yc, gain_one[None], w_key, w_value, cosine[1], sine[1]
    )
    mixed_heads, logs, attended = attend(
        hide, query, keys_a, values_a, keys_b, values_b, w_output
    )
    attended, own_t, own_later = lax.optimization_barrier((attended, own_t, own_later))

    own_ty = swap(own_t, "yl")
    turned_a, turned_b = call(
        turn_rows_kernel,
        "turn_rows",
        (after(normed_a, attended), normed_b),
        [((width, 2 * rows), bf16)] * 2,
    )
    theirs, own_y, turned_a, turned_b = lax.optimization_barrier(
        (swap(attended, "t"), own_y, turned_a, turned_b)
    )
    middle, normed_two, sent_rows = call(
        second_kernel,
        "second",
        (tokens, attended, theirs, gain_two[None], placer_turned, sent_cot),
        [of_rows, of_rows_low, ((seats, 2 * width + 128), bf16)],
    )

    arrived = exchange(sent_rows.reshape(experts, SLOTS, -1), ROUTE).reshape(seats, -1)
    hidden_shared, shared_gg, shared_gu, shared_back, shared_out, share = shared(
        normed_two, cotangent, shared_gate, shared_up, shared_down, router, routes
    )
    early_given, early_kept = half_call(
        shared_weights_kernel,
        "shared_weights",
        core,
        (normed_two, cotangent),
        (shared_gg, shared_gu, hidden_shared),
        (3 * shared_part,),
    )
    weights = [own_later, own_t, own_y, own_ty]
    weights = [swap(w, "c") for w in weights] + weights
    arrived, early_given, early_kept, shared_back, shared_out, share, *weights = (
        lax.optimization_barrier(
            (arrived, early_given, early_kept, shared_back, shared_out, share, *weights)
        )
    )
    early_taken = swap(early_given, "c")
    hidden_expert, expert_grads, back, scaled_rows, out_grads, row_share = expert_rows(
        expert_here, arrived, router, weights, experts
    )
    given, first_out, scaled_turned, out_turned = expert_half(
        expert_given_kernel,
        "expert_given",
        (scaled_rows, out_grads),
        hidden_expert,
        expert_grads,
        weights[:4],
        0,
        [((seats, width), f32), ((width, seats), bf16), ((width, seats), bf16)],
    )
    (early,) = call(
        half_sum_kernel, "half_sum", (after(early_kept, back), early_taken), [(early_kept.shape, bf16)]
    )
    back = exchange(back.reshape(experts, SLOTS, -1), ROUTE).reshape(seats, -1)
    back, given, first_out, scaled_turned, out_turned, early = lax.optimization_barrier(
        (back, given, first_out, scaled_turned, out_turned, early)
    )

    mine, logits_grads = call(
        functools.partial(combine_kernel, experts=experts),
        "combine",
        (placer, back, share, router, shared_back),
        [of_rows_low, ((rows, 128), bf16)],
    )
    kept, picked = expert_half(
        expert_kept_kernel,
        "expert_kept",
        (after(scaled_turned, mine), out_turned, row_share, first_out),
        hidden_expert,
        expert_grads,
        weights[4:],
        4,
        [((seats, width), bf16)],
    )
    of_shard = pl.BlockSpec((1, width, 3 * part), lambda k: (k, 0, 0))
    half_shard = (1, width // 2, 3 * part)
    to_high, to_tensor, keep_high, keep_tensor = call(
        expert_sum_kernel,
        "expert_sum",
        (kept, swap(given, "c")),
        [((2, width // 2, 3 * part), bf16)] * 4,
        grid=(4,),
        in_specs={0: of_shard, 1: of_shard},
        out_specs={
            0: pl.BlockSpec(half_shard, lambda k: (jnp.maximum(k - 2, 0), 0, 0)),
            1: pl.BlockSpec(half_shard, lambda k: (k // 2, 0, 0)),
            2: pl.BlockSpec(half_shard, lambda k: (jnp.minimum(k, 1), 0, 0)),
            3: pl.BlockSpec(half_shard, lambda k: (k // 2, 0, 0)),
        },
    )
    theirs, to_high, to_tensor, keep_high, keep_tensor, picked = lax.optimization_barrier(
        (swap(mine, "t"), to_high, to_tensor, keep_high, keep_tensor, picked)
    )
    middle_grads, middle_low, mixed_grads, gain_sum = call(
        back_two_kernel,
        "back_two",
        (middle, mine, theirs, cotangent, gain_two[None], w_output),
        [of_rows, of_rows_low, ((rows, wide), bf16), ((1, width), f32)],
    )

    dq, dka, dva, dkb, dvb = attend_back(
        hide, query, keys_a, values_a, keys_b, values_b, mixed_heads, logs, mixed_grads,
        cosine[0], sine[0], cosine[1], sine[1],
    )
    picked = exchange(picked.reshape(experts, SLOTS, width), ROUTE).reshape(seats, width)
    from_high, from_tensor = swap(to_high, "yl"), swap(to_tensor, "t")
    dq, dka, dva, dkb, dvb, picked, from_high, from_tensor = lax.optimization_barrier(
        (dq, dka, dva, dkb, dvb, picked, from_high, from_tensor)
    )
    late_given, late_kept, small_given, small_kept = half_call(
        functools.partial(late_weights_kernel, experts=experts),
        "late_weights",
        core,
        (normed_two, middle_low, gain_sum, gain_one[None]),
        (dq, dka, dkb, dva, dvb, logits_grads, mixed_heads),
        (4 * wide, 128),
        (turned_a, turned_b, w_query, w_key, w_value),
    )

    small = swap(small_kept, "t").astype(f32) + lax.ppermute(
        small_given, ("c", "t"), [(0, 3), (3, 0), (1, 2), (2, 1)]
    ).astype(f32)
    small = small_kept.astype(f32) + swap(small_given, "c").astype(f32) + small
    sums = call(
        expert_sums_kernel,
        "expert_sums",
        (keep_high, after(from_high, late_given), keep_tensor, from_tensor),
        [((width // 2, 3 * part), bf16)] * 4,
    )
    early = lax.psum_scatter(early, "x", scatter_dimension=0, tiled=True)
    early = lax.psum_scatter(early, ("yh", "yl"), scatter_dimension=0, tiled=True)
    early_zh = swap(after(early, late_given), "zh")
    late_taken, small, next_t, next_y, kept_u, kept_l, early, early_zh = lax.optimization_barrier(
        (swap(late_given, "c"), small, *sums, early, early_zh)
    )
    total = late_kept.astype(f32) + late_taken.astype(f32)
    total = jnp.concatenate([total, small], axis=1).astype(bf16)
    parts = exchange(total.reshape(16, -1, total.shape[1]), PLANE)
    parts, from_next_t, from_next_y = lax.optimization_barrier(
        (parts, swap(next_t, "t"), swap(next_y, "yl"))
    )

    to_core, to_far, to_y, own_part = call(
        normed_back_kernel,
        "normed_back",
        (after(dq, total), dka, dva, dkb, dvb, w_query, w_key, w_value),
        [of_rows_low, of_rows_low, of_rows, of_rows],
    )
    from_far = swap(to_far, "c").astype(f32)
    own_part = own_part + swap(to_core, "c").astype(f32)
    from_y = swap((to_y + from_far).astype(bf16), "yl")
    block_part = (shared_out + dot(after(placer, total), picked)).astype(bf16)
    part_sum = jnp.sum(parts.astype(f32), axis=0).astype(bf16)
    part_zh, from_y, from_block, own_part = lax.optimization_barrier(
        (swap(part_sum, "zh"), from_y, swap(block_part, "t"), own_part)
    )
    own_part = (own_part + from_y.astype(f32)).astype(bf16)
    total = (part_sum.astype(f32) + part_zh.astype(f32)).astype(bf16)
    total, from_t = lax.optimization_barrier(
        (spread(after(total, own_part)), swap(own_part, "t"))
    )
    block_out = (middle + block_part.astype(f32) + from_block.astype(f32)).astype(bf16)
    (grad_tokens,) = call(
        first_kernel,
        "first",
        (tokens, own_part, from_t, middle_grads, gain_one[None]),
        [of_rows],
    )
    square = ((width, wide), f32)
    grad_query, grad_key, grad_value, grad_output, small = call(
        late_out_kernel,
        "late_out",
        (core[None], total, swap(total, "c")),
        [square, square, square, ((wide, width), f32), ((width, 128), f32)],
        smem=(0,),
    )
    grad_expert_gate, grad_expert_up, grad_expert_down = call(
        expert_out_kernel,
        "expert_out",
        (kept_u, from_next_t, kept_l, from_next_y),
        [((1, width, part), f32), ((1, width, part), f32), ((1, part, width), f32)],
    )
    early = (early.astype(f32) + early_zh.astype(f32)).astype(bf16)
    early = lax.all_gather(early, PLANE, axis=0, tiled=True)
    early = after(early, from_t)
    hidden = (width, shared_part)
    grad_shared_gate, grad_shared_up, grad_shared_down = call(
        early_out_kernel,
        "early_out",
        (core[None], early, swap(early, "c")),
        [(hidden, f32), (hidden, f32), (hidden[::-1], f32)],
        smem=(0,),
    )
    return (
        block_out,
        grad_tokens,
        small[:, experts + 1],
        grad_query,
        grad_key,
        grad_value,
        grad_output,
        small[:, experts],
        small[:, :experts],
        grad_shared_gate,
        grad_shared_up,
        grad_shared_down,
        grad_expert_gate,
        grad_expert_up,
        grad_expert_down,
    )


def solution(mesh):
    fine = Mesh(mesh.devices.reshape(2, 4, 2, 2, 2, 2), AXES)
    placed = (
        P(EXPERT, None),
        P(EXPERT, None),
        P(),
        P(None, "t"),
        P(None, "t"),
        P(None, "t"),
        P("t", None),
        P(),
        P(),
        P(None, "t"),
        P(None, "t"),
        P("t", None),
        P(EXPERT, None, "t"),
        P(EXPERT, None, "t"),
        P(EXPERT, "t", None),
        P(EXPERT, None),
    )
    return jax.shard_map(
        local,
        mesh=fine,
        in_specs=placed,
        out_specs=(
            P(EXPERT, None),
            P(EXPERT, None),
            P(),
            P(None, "t"),
            P(None, "t"),
            P(None, "t"),
            P("t", None),
            P(),
            P(),
            P(None, "t"),
            P(None, "t"),
            P("t", None),
            P(EXPERT, None, "t"),
            P(EXPERT, None, "t"),
            P(EXPERT, "t", None),
        ),
        check_vma=False,
    )
```

```python
import functools

import jax
import jax.numpy as jnp
import numpy as np
from jax import lax
from jax.experimental import pallas as pl
from jax.experimental.pallas import tpu as pltpu
from jax.sharding import Mesh
from jax.sharding import PartitionSpec as P

HEAD_DIM = 64
BLOCK = 256
SLOTS = 40
PAIR = 128
AXES = ("zh", "x", "yh", "yl", "c", "t")
EXPERT = AXES[:5]
ROUTE = ("zh", "x", "yh")
PLANE = ("x", "yh", "yl")
CHIPS = ("zh",) + PLANE

epsilon = 1e-06
rope_base = 10000.0
bf16 = jnp.bfloat16
f32 = jnp.float32
params = pltpu.CompilerParams(vmem_limit_bytes=52 << 20)


def swap(x, axis):
    return lax.ppermute(x, axis, [(0, 1), (1, 0)])


def exchange(x, axis):
    return lax.all_to_all(x, axis, split_axis=0, concat_axis=0, tiled=True)


def after(x, first):
    return lax.optimization_barrier((x, first))[0]


def dot(a, b, dims=((1,), (0,))):
    return lax.dot_general(a, b, (dims, ((), ())), preferred_element_type=f32)


def dot_nt(a, b):
    return dot(a, b, ((1,), (1,)))


def dot_tn(a, b):
    return dot(a, b, ((0,), (0,)))


def rms_scale(values):
    return lax.rsqrt(jnp.mean(values * values, axis=-1, keepdims=True) + epsilon)


def pair_sum(values, axis):
    low = values.astype(bf16)
    return low.astype(f32) + swap(low, axis).astype(f32)


def norm_back(inputs, row_scale, gain_row, upstream):
    unit_rows = inputs * row_scale
    scaled_grad = upstream * gain_row
    return row_scale * (
        scaled_grad - unit_rows * jnp.mean(scaled_grad * unit_rows, axis=-1, keepdims=True)
    )


RATE = 230000000
TIMES = dict(
    route=4,
    project=5,
    attend=14,
    attend_back=23,
    second=4,
    shared=12,
    expert_rows=20,
    expert_given=9,
    expert_kept=9,
    expert_sum=4,
    expert_sums=3,
    expert_out=3,
    combine=4,
    back_two=4,
    normed_back=8,
    first=4,
    shared_weights=6,
    late_weights=8,
    early_out=5,
    turn_rows=3,
    half_sum=4,
    late_out=4,
)


def turn(values, cos, sin):
    half = HEAD_DIM // 2
    lanes = lax.broadcasted_iota(jnp.int32, values.shape, 1)
    first = (lanes // half) % 2 == 0
    size = values.shape[1]
    other = jnp.where(first, -pltpu.roll(values, size - half, 1), pltpu.roll(values, half, 1))
    return values * cos + other * sin


def whole(shape):
    return pl.BlockSpec(shape, lambda *_: (0,) * len(shape))


def call(kernel, name, args, outs, smem=(), grid=None, in_specs=None, out_specs=None, scratch=()):
    in_specs = dict(in_specs or {})
    out_specs = dict(out_specs or {})
    for i in smem:
        in_specs[i] = pl.BlockSpec(memory_space=pltpu.SMEM)
    return pl.pallas_call(
        kernel,
        **({} if grid is None else {"grid": grid}),
        in_specs=[in_specs.get(i, whole(a.shape)) for i, a in enumerate(args)],
        out_specs=[out_specs.get(i, whole(s)) for i, (s, _) in enumerate(outs)],
        out_shape=[jax.ShapeDtypeStruct(s, d) for s, d in outs],
        scratch_shapes=scratch,
        compiler_params=params,
        cost_estimate=pl.CostEstimate(flops=TIMES[name] * RATE, bytes_accessed=1 << 20, transcendentals=0),
        name=name,
    )(*args)


def lanes_of(rows=1, count=128):
    return lax.broadcasted_iota(jnp.int32, (rows, count), 1)


def route_kernel(tensor_ref, routes_ref, cot_ref, expand_ref, seat_ref, placer_ref, turned_ref, sent_ref):
    routes = routes_ref[...]
    rows, width = cot_ref.shape
    lanes = lanes_of(rows)
    member = (routes[:, 0:1] == lanes) | (routes[:, 1:2] == lanes)
    earlier = lax.broadcasted_iota(jnp.int32, (rows, rows), 0) > lanes_of(rows, rows)
    count = dot(
        jnp.where(earlier, 1.0, 0.0).astype(bf16), jnp.where(member, 1.0, 0.0).astype(bf16)
    )
    offset = (tensor_ref[0] * SLOTS).astype(f32)
    place = jnp.where(member, count - offset, -1.0).astype(bf16)
    placer = jnp.where(dot(place, expand_ref[...]) == seat_ref[...], 1.0, 0.0).astype(bf16)
    placer_ref[...] = placer
    turned = placer.T
    turned_ref[...] = turned
    sent_ref[:, :width] = dot(turned, cot_ref[...]).astype(bf16)
    sums = (routes[:, 0:1] + routes[:, 1:2]).astype(f32)
    sent_ref[:, width:] = dot(turned, jnp.where(lanes == 0, sums, 0.0).astype(bf16)).astype(bf16)


def route(tensor, routes, cotangent, experts):
    rows, width = cotangent.shape
    seats = experts * SLOTS
    columns = np.arange(seats)
    expand = jnp.asarray(np.arange(128)[:, None] == columns[None, :] // SLOTS, bf16)
    seat = jnp.asarray((columns % SLOTS)[None], f32)
    return call(
        route_kernel,
        "route",
        (tensor[None], routes, cotangent, expand, seat),
        [((rows, seats), bf16), ((seats, rows), bf16), ((seats, width + 128), bf16)],
        smem=(0,),
    )


def project_kernel(x0_ref, x1_ref, gain_ref, wk_ref, wv_ref, cos_ref, sin_ref, *rest):
    wq_ref = rest[0] if len(rest) == 5 else None
    n_ref, k_ref, v_ref = rest[-4:-1] if wq_ref is not None else rest
    for chunk, x_ref in enumerate((x0_ref, x1_ref)):
        rows = x_ref.shape[0]
        at_rows = slice(chunk * rows, (chunk + 1) * rows)
        x = x_ref[...].astype(f32)
        normed = (x * rms_scale(x) * gain_ref[...]).astype(bf16)
        n_ref[at_rows, :] = normed
        cos, sin = cos_ref[at_rows, :], sin_ref[at_rows, :]
        key = dot(normed, wk_ref[...])
        for at in range(0, key.shape[1], PAIR):
            lanes = slice(at, at + PAIR)
            k_ref[at_rows, lanes] = turn(key[:, lanes], cos, sin).astype(bf16)
        v_ref[at_rows, :] = dot(normed, wv_ref[...]).astype(bf16)
        if chunk == 0 and wq_ref is not None:
            q_ref = rest[-1]
            query = dot(normed, wq_ref[...])
            for at in range(0, query.shape[1], PAIR):
                lanes = slice(at, at + PAIR)
                turned = turn(query[:, lanes], cos, sin).astype(bf16)
                q_ref[:, lanes] = turned * (HEAD_DIM**-0.5)


def project(first, second, gain, w_key, w_value, cos, sin, w_query=None):
    rows, width = first.shape
    wide = w_key.shape[1]
    outs = [((2 * rows, width), bf16), ((2 * rows, wide), bf16), ((2 * rows, wide), bf16)]
    args = (first, second, gain, w_key, w_value, cos, sin)
    if w_query is not None:
        args += (w_query,)
        outs.append(((rows, wide), bf16))
    return call(project_kernel, "project", args, outs)


def attend_kernel(hide_ref, q_ref, ka_ref, va_ref, kb_ref, vb_ref, wo_ref, o_ref, lse_ref, part_ref, acc_ref):
    lanes = lanes_of()
    span = 2 * BLOCK
    step = pl.program_id(0)
    for half in range(2):
        rows = slice(half * BLOCK, (half + 1) * BLOCK)
        q = q_ref[rows, :]
        outs, logs = [], []
        for head in range(2):
            query = jnp.where(lanes // HEAD_DIM == head, q, jnp.zeros_like(q))
            spans = [(ka_ref, va_ref, 0, BLOCK * (half + 1), 0.0), (ka_ref, va_ref, span, span, hide_ref[1])]
            spans += [(kb_ref, vb_ref, 0, span, hide_ref[2]), (kb_ref, vb_ref, span, span, hide_ref[3])]
            scores = [dot_nt(query, k[a : a + n, :]) for k, _, a, n, _ in spans]
            tops = [jnp.max(s, axis=1, keepdims=True) - x[4] for s, x in zip(scores, spans)]
            top = functools.reduce(jnp.maximum, tops)
            total, acc = 0.0, 0.0
            for s, (_, v, a, n, off) in zip(scores, spans):
                p = jnp.exp(s - (top + off))
                total = total + jnp.sum(p, axis=1, keepdims=True)
                acc = acc + dot(p.astype(bf16), v[a : a + n, :])
            outs.append(acc / total)
            logs.append(top + jnp.log(total))
        mixed = jnp.where(lanes < HEAD_DIM, outs[0], outs[1]).astype(bf16)
        o_ref[rows, :] = mixed
        lse_ref[rows, :] = jnp.where(lanes < HEAD_DIM, logs[0], logs[1])
    part = dot(o_ref[...], wo_ref[...])

    @pl.when(step == 0)
    def _():
        acc_ref[...] = part

    @pl.when(step > 0)
    def _():
        acc_ref[...] += part

    @pl.when(step == pl.num_programs(0) - 1)
    def _():
        part_ref[...] = acc_ref[...].astype(bf16)


def attend(hide, q, ka, va, kb, vb, w_output):
    rows, keys = q.shape[0], ka.shape[0]
    width = w_output.shape[1]
    of_q = pl.BlockSpec((rows, PAIR), lambda p: (0, p))
    of_k = pl.BlockSpec((keys, PAIR), lambda p: (0, p))
    return call(
        attend_kernel,
        "attend",
        (hide, q, ka, va, kb, vb, w_output),
        [(q.shape, bf16), (q.shape, f32), ((rows, width), bf16)],
        smem=(0,),
        grid=(q.shape[1] // PAIR,),
        in_specs={1: of_q, 2: of_k, 3: of_k, 4: of_k, 5: of_k, 6: pl.BlockSpec((PAIR, width), lambda p: (p, 0))},
        out_specs={0: of_q, 1: of_q},
        scratch=[pltpu.VMEM((rows, width), f32)],
    )


def attend_back_kernel(
    hide_ref, q_ref, ka_ref, va_ref, kb_ref, vb_ref, o_ref, lse_ref, g_ref, ca_ref, sa_ref, cb_ref, sb_ref,
    dq_ref, dka_ref, dva_ref, dkb_ref, dvb_ref,
):
    lanes = lanes_of()
    q, g = q_ref[...], g_ref[...]
    rows = q.shape[0]
    deltas = (g.astype(f32) * o_ref[...].astype(f32)).T
    logs = lse_ref[...].T
    dq = 0.0
    near = (ka_ref, va_ref, ca_ref, sa_ref, dka_ref, dva_ref)
    far = (kb_ref, vb_ref, cb_ref, sb_ref, dkb_ref, dvb_ref)
    for block in range(8):
        k_ref, v_ref, cos_ref, sin_ref, dk_ref, dv_ref = near if block < 4 else far
        off = 0.0 if block < 2 else hide_ref[block // 2]
        first = BLOCK if block == 1 else 0
        keys = slice((block % 4) * BLOCK, (block % 4 + 1) * BLOCK)
        k, v = k_ref[keys, :], v_ref[keys, :]
        dk, dv = 0.0, 0.0
        for head in range(2):
            mine = lanes // HEAD_DIM == head
            low = head * HEAD_DIM
            query = jnp.where(mine, q[first:, :], jnp.zeros_like(q[first:, :]))
            grads = jnp.where(mine, g[first:, :], jnp.zeros_like(g[first:, :]))
            key = jnp.where(mine, k, jnp.zeros_like(k))
            log = logs[low : low + 1, first:] + off
            delta = jnp.sum(deltas[low : low + HEAD_DIM, first:], axis=0, keepdims=True)
            p = jnp.exp(dot_nt(k, query) - log)
            ds = (p * (dot_nt(v, grads) - delta)).astype(bf16)
            dv = dv + dot(p.astype(bf16), grads)
            dk = dk + dot(ds, query)
            part = dot_tn(ds, key)
            if first:
                part = jnp.concatenate([jnp.zeros((first, PAIR), f32), part], axis=0)
            dq = dq + part
        dv_ref[keys, :] = dv.astype(bf16)
        dk_ref[keys, :] = turn(dk, cos_ref[keys, :], -sin_ref[keys, :]).astype(bf16)
    dq = dq * (HEAD_DIM**-0.5)
    dq_ref[...] = turn(dq, ca_ref[:rows, :], -sa_ref[:rows, :]).astype(bf16)


def attend_back(hide, q, ka, va, kb, vb, o, lse, g, ca, sa, cb, sb):
    rows, keys = q.shape[0], ka.shape[0]
    of_q = pl.BlockSpec((rows, PAIR), lambda p: (0, p))
    of_k = pl.BlockSpec((keys, PAIR), lambda p: (0, p))
    return call(
        attend_back_kernel,
        "attend_back",
        (hide, q, ka, va, kb, vb, o, lse, g, ca, sa, cb, sb),
        [(q.shape, bf16)] + [(ka.shape, bf16)] * 4,
        smem=(0,),
        grid=(q.shape[1] // PAIR,),
        in_specs={1: of_q, 2: of_k, 3: of_k, 4: of_k, 5: of_k, 6: of_q, 7: of_q, 8: of_q},
        out_specs={0: of_q, 1: of_k, 2: of_k, 3: of_k, 4: of_k},
    )


def turn_rows_kernel(a_ref, b_ref, ta_ref, tb_ref):
    ta_ref[...] = a_ref[...].T
    tb_ref[...] = b_ref[...].T


def half_sum_kernel(kept_ref, taken_ref, out_ref):
    out_ref[...] = kept_ref[...] + taken_ref[...]


def second_kernel(x_ref, mine_ref, theirs_ref, gain_ref, turned_ref, cot_ref, middle_ref, n_ref, sent_ref):
    middle = x_ref[...].astype(f32) + (mine_ref[...].astype(f32) + theirs_ref[...].astype(f32))
    middle_ref[...] = middle
    normed = (middle * rms_scale(middle) * gain_ref[...]).astype(bf16)
    n_ref[...] = normed
    width = normed.shape[1]
    sent_ref[:, :width] = dot(turned_ref[...], normed).astype(bf16)
    sent_ref[:, width:] = cot_ref[...]


def swish(gate, up, grads):
    sigmoid = jax.nn.sigmoid(gate)
    unit = gate * sigmoid
    slope = sigmoid + unit * (1.0 - sigmoid)
    return (unit * up).astype(bf16), (grads * up * slope).astype(bf16), (grads * unit).astype(bf16)


def shared_kernel(
    n_ref, cot_ref, sg_ref, su_ref, sd_ref, router_ref, routes_ref, h_ref, gg_ref, gu_ref, back_ref, out_ref, share_ref
):
    normed, cot = n_ref[...], cot_ref[...]
    sg, su, sd = sg_ref[...], su_ref[...], sd_ref[...]
    hidden, gg, gu = swish(dot(normed, sg), dot(normed, su), dot_nt(cot, sd))
    h_ref[...], gg_ref[...], gu_ref[...] = hidden, gg, gu
    back = dot_nt(gg, sg) + dot_nt(gu, su)
    out = dot(hidden, sd)

    @pl.when(pl.program_id(0) == 0)
    def _():
        back_ref[...] = back
        out_ref[...] = out
        logits = dot(normed, router_ref[...])
        routes = routes_ref[...]
        lanes = lanes_of()
        first, second = lanes == routes[:, 0:1], lanes == routes[:, 1:2]
        one = jnp.sum(jnp.where(first, logits, 0.0), axis=1, keepdims=True)
        two = jnp.sum(jnp.where(second, logits, 0.0), axis=1, keepdims=True)
        top = jnp.maximum(one, two)
        one, two = jnp.exp(one - top), jnp.exp(two - top)
        share_ref[...] = (jnp.where(first, one, 0.0) + jnp.where(second, two, 0.0)) / (one + two)

    @pl.when(pl.program_id(0) > 0)
    def _():
        back_ref[...] += back
        out_ref[...] += out


def shared(normed, cot, shared_gate, shared_up, shared_down, router, routes):
    rows, width = normed.shape
    hidden = shared_gate.shape[1]
    block = 512
    columns = pl.BlockSpec((width, block), lambda k: (0, k))
    of_hidden = pl.BlockSpec((rows, block), lambda k: (0, k))
    return call(
        shared_kernel,
        "shared",
        (normed, cot, shared_gate, shared_up, shared_down, router, routes),
        [((rows, hidden), bf16)] * 3 + [((rows, width), f32)] * 2 + [((rows, 128), f32)],
        grid=(hidden // block,),
        in_specs={2: columns, 3: columns, 4: pl.BlockSpec((block, width), lambda k: (k, 0))},
        out_specs={0: of_hidden, 1: of_hidden, 2: of_hidden},
    )


def store_half(given_ref, kept_ref, at, value):
    value = value.astype(bf16)

    @pl.when(pl.program_id(0) == 0)
    def _():
        given_ref[:, at : at + value.shape[1]] = value

    @pl.when(pl.program_id(0) == 1)
    def _():
        kept_ref[:, at : at + value.shape[1]] = value


def shared_weights_kernel(core_ref, n_ref, cot_ref, gg_ref, gu_ref, h_ref, given_ref, kept_ref):
    part = h_ref.shape[1]
    turned = n_ref[...].T
    store_half(given_ref, kept_ref, 0, dot(turned, gg_ref[...]))
    store_half(given_ref, kept_ref, part, dot(turned, gu_ref[...]))
    store_half(given_ref, kept_ref, 2 * part, dot(cot_ref[...].T, h_ref[...]))


def half_call(kernel, name, core, halved, full, columns, by_rows=()):
    half = halved[0].shape[1] // 2
    specs = [pl.BlockSpec((a.shape[0], half), lambda s, c: (0, jnp.where(s == 0, 1 - c[0], c[0]))) for a in halved]
    specs += [
        pl.BlockSpec((half, a.shape[1]), lambda s, c: (jnp.where(s == 0, 1 - c[0], c[0]), 0))
        for a in by_rows
    ]
    specs += [pl.BlockSpec(a.shape, lambda s, c: (0, 0)) for a in full]
    return pl.pallas_call(
        kernel,
        grid_spec=pltpu.PrefetchScalarGridSpec(
            num_scalar_prefetch=1,
            grid=(2,),
            in_specs=specs,
            out_specs=[pl.BlockSpec((half, c), lambda s, c: (0, 0)) for c in columns for _ in range(2)],
        ),
        out_shape=[jax.ShapeDtypeStruct((half, c), bf16) for c in columns for _ in range(2)],
        compiler_params=params,
        cost_estimate=pl.CostEstimate(flops=TIMES[name] * RATE, bytes_accessed=1 << 20, transcendentals=0),
        name=name,
    )(core[None], *halved, *by_rows, *full)


def late_weights_kernel(
    core_ref, n2_ref, low_ref, gain_ref, scale_ref, ta_ref, tb_ref, wq_ref, wk_ref, wv_ref,
    dq_ref, dka_ref, dkb_ref, dva_ref, dvb_ref, lg_ref, o_ref, given_ref, kept_ref, small_given_ref, small_kept_ref, *, experts
):
    def column(row_ref):
        return jnp.broadcast_to(row_ref[...], (128, row_ref.shape[1])).T

    wide = dq_ref.shape[1]
    rows = dq_ref.shape[0]
    ta, tb = ta_ref[...], tb_ref[...]
    grad_q = dot(ta[:, :rows], dq_ref[...])
    grad_k = dot(ta, dka_ref[...]) + dot(tb, dkb_ref[...])
    grad_v = dot(ta, dva_ref[...]) + dot(tb, dvb_ref[...])
    for i, value in enumerate((grad_q, grad_k, grad_v, dot(low_ref[...].T, o_ref[...]))):
        store_half(given_ref, kept_ref, i * wide, value)
    small = dot(n2_ref[...].T, lg_ref[...])
    terms = grad_q * wq_ref[...].astype(f32) + grad_k * wk_ref[...].astype(f32) + grad_v * wv_ref[...].astype(f32)
    gain_one = jnp.sum(terms, axis=1, keepdims=True) / column(scale_ref)
    lanes = lanes_of()
    small = jnp.where(lanes == experts, 0.5 * column(gain_ref), small)
    store_half(small_given_ref, small_kept_ref, 0, jnp.where(lanes == experts + 1, gain_one, small))


def expert_kernel(
    here_ref, sent_ref, router_ref, *refs, experts, shards
):
    w_refs = refs[:shards]
    hidden_ref, grads_ref, back_ref, scaled_ref, out_ref, share_ref, acc_ref, dots_ref, slots_ref, sems = refs[shards:]
    step = pl.program_id(0)
    width = router_ref.shape[0]

    def fetch(i, slot):
        return pltpu.make_async_copy(w_refs[i], slots_ref.at[slot], sems.at[slot])

    @pl.when(step == 0)
    def _():
        fetch(0, 0).start()

    for i in range(1, shards):
        @pl.when(step == i - 1)
        def _(i=i):
            fetch(i, i % 2).start()

    slot = lax.rem(step, 2)
    fetch(0, slot).wait()
    w = slots_ref.at[slot]
    part = w.shape[1] // 3
    half = sent_ref.shape[0] // 2
    w_in, w_down = w[:, : 2 * part], w[:, 2 * part :]
    for at in (0, half):
        these = slice(at, at + half)
        rows, cot = sent_ref[these, :width], sent_ref[these, width : 2 * width]
        both = dot(rows, w_in)
        hidden_grads = dot(cot, w_down)
        hidden, gg, gu = swish(both[:, :part], both[:, part:], hidden_grads)
        hidden_ref[0, these, :] = hidden
        grads_ref[0, these, :part] = gg
        grads_ref[0, these, part:] = gu
        product = hidden.astype(f32) * hidden_grads
        product = functools.reduce(jnp.add, [product[:, a : a + 128] for a in range(0, part, 128)])
        back = dot_nt(gg, w[:, :part]) + dot_nt(gu, w[:, part : 2 * part])
        acc_ref[these, :] = jnp.where(step == 0, 0.0, acc_ref[these, :]) + back
        dots_ref[these, :] = jnp.where(step == 0, 0.0, dots_ref[these, :]) + product

    @pl.when(step == pl.num_programs(0) - 1)
    def _():
        rows, cot = sent_ref[:, :width], sent_ref[:, width : 2 * width]
        here = here_ref[0]
        lanes = lanes_of()
        logits = dot(rows, router_ref[...])
        other = sent_ref[:, 2 * width :].astype(f32)[:, :1].astype(jnp.int32) - here
        own_logit = jnp.sum(jnp.where(lanes == here, logits, 0.0), axis=1, keepdims=True)
        other_logit = jnp.sum(jnp.where(lanes == other, logits, 0.0), axis=1, keepdims=True)
        top = jnp.maximum(own_logit, other_logit)
        own = jnp.exp(own_logit - top)
        share = own / (own + jnp.exp(other_logit - top))
        share_ref[...] = jnp.broadcast_to(share, share_ref.shape)
        scaled_ref[...] = (share * rows.astype(f32)).astype(bf16)
        out_ref[...] = (share * cot.astype(f32)).astype(bf16)
        back_ref[:, :width] = (share * acc_ref[...]).astype(bf16)
        dots = jnp.sum(dots_ref[...], axis=1, keepdims=True)
        high = dots.astype(bf16).astype(f32)
        back_ref[:, width:] = (
            jnp.where(lanes == here, high, 0.0)
            + jnp.where(lanes == experts + here, dots - high, 0.0)
        ).astype(bf16)


def expert_rows(here, sent, router, weights, experts):
    rows, width = sent.shape[0], router.shape[0]
    shards, packed = len(weights), weights[0].shape[1]
    part = packed // 3
    return call(
        functools.partial(expert_kernel, experts=experts, shards=shards),
        "expert_rows",
        (here[None], sent, router, *weights),
        [
            ((shards, rows, part), bf16),
            ((shards, rows, 2 * part), bf16),
            ((rows, width + 128), bf16),
            ((rows, width), bf16),
            ((rows, width), bf16),
            ((rows, 128), f32),
        ],
        smem=(0,),
        grid=(shards,),
        in_specs={3 + i: pl.BlockSpec(memory_space=pl.ANY) for i in range(shards)},
        out_specs={
            0: pl.BlockSpec((1, rows, part), lambda k: (k, 0, 0)),
            1: pl.BlockSpec((1, rows, 2 * part), lambda k: (k, 0, 0)),
        },
        scratch=[
            pltpu.VMEM((rows, width), f32),
            pltpu.VMEM((rows, 128), f32),
            pltpu.VMEM((2, width, packed), bf16),
            pltpu.SemaphoreType.DMA((2,)),
        ],
    )


def expert_given_kernel(scaled_ref, out_ref, hidden_ref, grads_ref, *refs, shards):
    w_refs = refs[:shards]
    d_ref, acc_ref, st_ref, ot_ref, slots_ref, sems = refs[shards:]
    step = pl.program_id(0)

    @pl.when(step == 0)
    def _():
        st_ref[...] = scaled_ref[...].T
        ot_ref[...] = out_ref[...].T

    expert_step(step, st_ref, ot_ref, hidden_ref, grads_ref, w_refs, d_ref, slots_ref, sems, acc_ref, None)


def expert_kept_kernel(st_ref, ot_ref, share_ref, first_ref, hidden_ref, grads_ref, *refs, shards):
    w_refs = refs[:shards]
    d_ref, picked_ref, acc_ref, slots_ref, sems = refs[shards:]
    step = pl.program_id(0)
    expert_step(step, st_ref, ot_ref, hidden_ref, grads_ref, w_refs, d_ref, slots_ref, sems, acc_ref, first_ref)

    @pl.when(step == pl.num_programs(0) - 1)
    def _():
        picked_ref[...] = (share_ref[:, :1] * acc_ref[...]).astype(bf16)


def expert_step(step, st_ref, ot_ref, hidden_ref, grads_ref, w_refs, d_ref, slots_ref, sems, acc_ref, first_ref):
    part = hidden_ref.shape[2]

    def fetch(i, slot):
        return pltpu.make_async_copy(w_refs[i].at[:, 2 * part :], slots_ref.at[slot], sems.at[slot])

    @pl.when(step == 0)
    def _():
        fetch(0, 0).start()
        acc_ref[...] = jnp.zeros_like(acc_ref) if first_ref is None else first_ref[...]

    for i in range(1, len(w_refs)):
        @pl.when(step == i - 1)
        def _(i=i):
            fetch(i, i % 2).start()

    slot = lax.rem(step, 2)
    fetch(0, slot).wait()
    d_ref[0, :, : 2 * part] = dot(st_ref[...], grads_ref[0]).astype(bf16)
    d_ref[0, :, 2 * part :] = dot(ot_ref[...], hidden_ref[0]).astype(bf16)
    acc_ref[...] += dot_nt(hidden_ref[0], slots_ref[slot])


def expert_half(kernel, name, args, hidden, grads, weights, at, extra):
    shards = len(weights)
    _, rows, part = hidden.shape
    width = weights[0].shape[0]
    count = len(args)
    return call(
        functools.partial(kernel, shards=shards),
        name,
        (*args, hidden, grads, *weights),
        [((shards, width, 3 * part), bf16), *extra],
        grid=(shards,),
        in_specs={
            count: pl.BlockSpec((1, rows, part), lambda k: (k + at, 0, 0)),
            count + 1: pl.BlockSpec((1, rows, 2 * part), lambda k: (k + at, 0, 0)),
            **{count + 2 + i: pl.BlockSpec(memory_space=pl.ANY) for i in range(shards)},
        },
        out_specs={0: pl.BlockSpec((1, width, 3 * part), lambda k: (k, 0, 0))},
        scratch=([pltpu.VMEM((rows, width), f32)] if at else [])
        + [pltpu.VMEM((2, width, part), bf16), pltpu.SemaphoreType.DMA((2,))],
    )


def expert_sum_kernel(kept_ref, taken_ref, high_ref, tensor_ref, keep_high_ref, keep_tensor_ref):
    shard = pl.program_id(0)
    half = kept_ref.shape[1] // 2
    total = kept_ref[0] + taken_ref[0]
    for ref, at, here in (
        (keep_high_ref, 0, shard < 2),
        (high_ref, 0, shard >= 2),
        (keep_tensor_ref, half, shard % 2 == 0),
        (tensor_ref, half, shard % 2 == 1),
    ):
        @pl.when(here)
        def _(ref=ref, at=at):
            ref[0] = total[at : at + half]


def expert_sums_kernel(kh_ref, fh_ref, kt_ref, ft_ref, to_t_ref, to_y_ref, kept_u_ref, kept_l_ref):
    to_t_ref[...] = kh_ref[1] + fh_ref[1]
    to_y_ref[...] = kt_ref[1] + ft_ref[1]
    kept_u_ref[...] = kh_ref[0] + fh_ref[0]
    kept_l_ref[...] = kt_ref[0] + ft_ref[0]


def expert_out_kernel(ku_ref, fu_ref, kl_ref, fl_ref, gate_ref, up_ref, down_ref):
    half = ku_ref.shape[0]
    part = gate_ref.shape[2]
    for at, (kept_ref, from_ref) in ((0, (ku_ref, fu_ref)), (half, (kl_ref, fl_ref))):
        total = kept_ref[...].astype(f32) + from_ref[...].astype(f32)
        gate_ref[0, at : at + half, :] = total[:, :part]
        up_ref[0, at : at + half, :] = total[:, part : 2 * part]
        down_ref[0, :, at : at + half] = total[:, 2 * part :].T


def combine_kernel(placer_ref, back_ref, share_ref, router_ref, shared_ref, part_ref, lg_ref, *, experts):
    width = shared_ref.shape[1]
    placer = placer_ref[...]
    lanes = lanes_of()
    dots = dot(placer, back_ref[:, width:])
    dots = jnp.where(lanes < experts, dots + pltpu.roll(dots, 128 - experts, 1), 0.0)
    share = share_ref[...]
    grads = (share * (dots - jnp.sum(share * dots, axis=1, keepdims=True))).astype(bf16)
    lg_ref[...] = grads
    total = shared_ref[...] + dot_nt(grads, router_ref[...]) + dot(placer, back_ref[:, :width])
    part_ref[...] = total.astype(bf16)


def back_two_kernel(middle_ref, mine_ref, theirs_ref, cot_ref, gain_ref, wo_ref, grads_ref, low_ref, mixed_ref, sum_ref):
    middle = middle_ref[...]
    scale = rms_scale(middle)
    upstream = mine_ref[...].astype(f32) + theirs_ref[...].astype(f32)
    sum_ref[...] = jnp.sum(upstream * (middle * scale), axis=0, keepdims=True)
    grads = cot_ref[...].astype(f32) + norm_back(middle, scale, gain_ref[...], upstream)
    grads_ref[...] = grads
    low = grads.astype(bf16)
    low_ref[...] = low
    mixed_ref[...] = dot_nt(low, wo_ref[...]).astype(bf16)


def normed_back_kernel(dq_ref, dka_ref, dva_ref, dkb_ref, dvb_ref, wq_ref, wk_ref, wv_ref, core_ref, far_ref, y_ref, own_ref):
    rows = dq_ref.shape[0]
    wk, wv = wk_ref[...], wv_ref[...]

    def back(dk_ref, dv_ref, chunk):
        these = slice(chunk * rows, (chunk + 1) * rows)
        return dot_nt(dk_ref[these, :], wk) + dot_nt(dv_ref[these, :], wv)

    far_ref[...] = back(dkb_ref, dvb_ref, 1).astype(bf16)
    core_ref[...] = back(dka_ref, dva_ref, 1).astype(bf16)
    y_ref[...] = back(dkb_ref, dvb_ref, 0)
    own_ref[...] = back(dka_ref, dva_ref, 0) + dot_nt(dq_ref[...], wq_ref[...])


def first_kernel(x_ref, mine_ref, theirs_ref, grads_ref, gain_ref, out_ref):
    x = x_ref[...].astype(f32)
    upstream = mine_ref[...].astype(f32) + theirs_ref[...].astype(f32)
    out_ref[...] = grads_ref[...] + norm_back(x, rms_scale(x), gain_ref[...], upstream)


def spread(part):
    copies = jnp.broadcast_to(part[None], (16,) + part.shape)
    return exchange(copies, PLANE).reshape(-1, part.shape[1])


def late_out_kernel(core_ref, mine_ref, theirs_ref, q_ref, k_ref, v_ref, o_ref, small_ref):
    half, wide = mine_ref.shape[0], q_ref.shape[1]
    for at, ref in ((0, mine_ref), (1, theirs_ref)):
        place = core_ref[0] if at == 0 else 1 - core_ref[0]
        these = pl.ds(pl.multiple_of(place * half, 128), half)
        for i, out_ref in enumerate((q_ref, k_ref, v_ref)):
            out_ref[these, :] = ref[:, i * wide : (i + 1) * wide].astype(f32)
        o_ref[:, these] = ref[:, 3 * wide : 4 * wide].astype(f32).T
        small_ref[these, :] = ref[:, 4 * wide :].astype(f32)


def early_out_kernel(core_ref, mine_ref, theirs_ref, gate_ref, up_ref, down_ref):
    half, wide = mine_ref.shape[0], gate_ref.shape[1]
    for at, ref in ((0, mine_ref), (1, theirs_ref)):
        place = core_ref[0] if at == 0 else 1 - core_ref[0]
        these = pl.ds(pl.multiple_of(place * half, 128), half)
        for i, out_ref in enumerate((gate_ref, up_ref)):
            out_ref[these, :] = ref[:, i * wide : (i + 1) * wide].astype(f32)
        down_ref[:, these] = ref[:, 2 * wide :].astype(f32).T


def local(
    tokens,
    routes,
    gain_one,
    w_query,
    w_key,
    w_value,
    w_output,
    gain_two,
    w_router,
    shared_gate,
    shared_up,
    shared_down,
    expert_gate,
    expert_up,
    expert_down,
    cotangent,
):
    rows, width = tokens.shape
    wide = w_query.shape[1]
    experts = w_router.shape[1]
    seats = experts * SLOTS
    part = expert_gate.shape[2]
    shared_part = shared_gate.shape[1]
    tensor = lax.axis_index("t")
    core = lax.axis_index("c")
    high = lax.axis_index("yl")
    expert_here = lax.axis_index(ROUTE)
    router = jnp.pad(w_router, ((0, 0), (0, 128 - experts)))
    of_rows = ((rows, width), f32)
    of_rows_low = ((rows, width), bf16)

    tokens_y = swap(tokens, "yl")
    tokens_c = swap(tokens, "c")
    hide = jnp.stack([core < 0, core == 0, high == 0, high == 0])
    hide = jnp.where(hide, 1e30, 0.0).astype(f32)

    frequency = rope_base ** (-np.arange(HEAD_DIM // 2) * 2.0 / HEAD_DIM)
    frequency = np.tile(frequency, PAIR // (HEAD_DIM // 2))
    inner = np.arange(rows)[:, None] * frequency[None, :]
    starts = jnp.stack(
        [((high ^ my) * 2 + (core ^ mc)) * rows for my, mc in ((0, 0), (0, 1), (1, 0), (1, 1))]
    )
    outer = starts.astype(f32)[:, None, None] * frequency.astype(np.float32)[None, None, :]
    cos_in, sin_in = np.cos(inner).astype(np.float32), np.sin(inner).astype(np.float32)
    cos_out, sin_out = jnp.cos(outer), jnp.sin(outer)
    cosine = (cos_out * cos_in - sin_out * sin_in).reshape(2, 2 * rows, PAIR)
    sine = (sin_out * cos_in + cos_out * sin_in).reshape(2, 2 * rows, PAIR)

    own = jnp.concatenate([expert_gate[0], expert_up[0], expert_down[0].T], axis=1)
    placer, placer_turned, sent_cot = route(tensor, routes, cotangent, experts)
    normed_a, keys_a, values_a, query = project(
        tokens, tokens_c, gain_one[None], w_key, w_value, cosine[0], sine[0], w_query
    )
    tokens_y, keys_a, placer, placer_turned, sent_cot, own_later = lax.optimization_barrier(
        (tokens_y, keys_a, placer, placer_turned, sent_cot, own)
    )
    tokens_yc = swap(tokens_y, "c")
    own_t, own_y = swap(own, "t"), swap(own_later, "yl")
    normed_b, keys_b, values_b = project(
        tokens_y, tokens_yc, gain_one[None], w_key, w_value, cosine[1], sine[1]
    )
    mixed_heads, logs, attended = attend(
        hide, query, keys_a, values_a, keys_b, values_b, w_output
    )
    attended, own_t, own_later = lax.optimization_barrier((attended, own_t, own_later))

    own_ty = swap(own_t, "yl")
    turned_a, turned_b = call(
        turn_rows_kernel,
        "turn_rows",
        (after(normed_a, attended), normed_b),
        [((width, 2 * rows), bf16)] * 2,
    )
    theirs, own_y, turned_a, turned_b = lax.optimization_barrier(
        (swap(attended, "t"), own_y, turned_a, turned_b)
    )
    middle, normed_two, sent_rows = call(
        second_kernel,
        "second",
        (tokens, attended, theirs, gain_two[None], placer_turned, sent_cot),
        [of_rows, of_rows_low, ((seats, 2 * width + 128), bf16)],
    )

    arrived = exchange(sent_rows.reshape(experts, SLOTS, -1), ROUTE).reshape(seats, -1)
    hidden_shared, shared_gg, shared_gu, shared_back, shared_out, share = shared(
        normed_two, cotangent, shared_gate, shared_up, shared_down, router, routes
    )
    early_given, early_kept = half_call(
        shared_weights_kernel,
        "shared_weights",
        core,
        (normed_two, cotangent),
        (shared_gg, shared_gu, hidden_shared),
        (3 * shared_part,),
    )
    weights = [own_later, own_t, own_y, own_ty]
    weights = [swap(w, "c") for w in weights] + weights
    arrived, early_given, early_kept, shared_back, shared_out, share, *weights = (
        lax.optimization_barrier(
            (arrived, early_given, early_kept, shared_back, shared_out, share, *weights)
        )
    )
    early_taken = swap(early_given, "c")
    hidden_expert, expert_grads, back, scaled_rows, out_grads, row_share = expert_rows(
        expert_here, arrived, router, weights, experts
    )
    given, first_out, scaled_turned, out_turned = expert_half(
        expert_given_kernel,
        "expert_given",
        (scaled_rows, out_grads),
        hidden_expert,
        expert_grads,
        weights[:4],
        0,
        [((seats, width), f32), ((width, seats), bf16), ((width, seats), bf16)],
    )
    (early,) = call(
        half_sum_kernel, "half_sum", (after(early_kept, back), early_taken), [(early_kept.shape, bf16)]
    )
    back = exchange(back.reshape(experts, SLOTS, -1), ROUTE).reshape(seats, -1)
    back, given, first_out, scaled_turned, out_turned, early = lax.optimization_barrier(
        (back, given, first_out, scaled_turned, out_turned, early)
    )

    mine, logits_grads = call(
        functools.partial(combine_kernel, experts=experts),
        "combine",
        (placer, back, share, router, shared_back),
        [of_rows_low, ((rows, 128), bf16)],
    )
    kept, picked = expert_half(
        expert_kept_kernel,
        "expert_kept",
        (after(scaled_turned, mine), out_turned, row_share, first_out),
        hidden_expert,
        expert_grads,
        weights[4:],
        4,
        [((seats, width), bf16)],
    )
    of_shard = pl.BlockSpec((1, width, 3 * part), lambda k: (k, 0, 0))
    half_shard = (1, width // 2, 3 * part)
    to_high, to_tensor, keep_high, keep_tensor = call(
        expert_sum_kernel,
        "expert_sum",
        (kept, swap(given, "c")),
        [((2, width // 2, 3 * part), bf16)] * 4,
        grid=(4,),
        in_specs={0: of_shard, 1: of_shard},
        out_specs={
            0: pl.BlockSpec(half_shard, lambda k: (jnp.maximum(k - 2, 0), 0, 0)),
            1: pl.BlockSpec(half_shard, lambda k: (k // 2, 0, 0)),
            2: pl.BlockSpec(half_shard, lambda k: (jnp.minimum(k, 1), 0, 0)),
            3: pl.BlockSpec(half_shard, lambda k: (k // 2, 0, 0)),
        },
    )
    theirs, to_high, to_tensor, keep_high, keep_tensor, picked = lax.optimization_barrier(
        (swap(mine, "t"), to_high, to_tensor, keep_high, keep_tensor, picked)
    )
    middle_grads, middle_low, mixed_grads, gain_sum = call(
        back_two_kernel,
        "back_two",
        (middle, mine, theirs, cotangent, gain_two[None], w_output),
        [of_rows, of_rows_low, ((rows, wide), bf16), ((1, width), f32)],
    )

    dq, dka, dva, dkb, dvb = attend_back(
        hide, query, keys_a, values_a, keys_b, values_b, mixed_heads, logs, mixed_grads,
        cosine[0], sine[0], cosine[1], sine[1],
    )
    picked = exchange(picked.reshape(experts, SLOTS, width), ROUTE).reshape(seats, width)
    from_high, from_tensor = swap(to_high, "yl"), swap(to_tensor, "t")
    early = lax.psum_scatter(early, "x", scatter_dimension=0, tiled=True)
    early = lax.psum_scatter(early, ("yh", "yl"), scatter_dimension=0, tiled=True)
    dq, dka, dva, dkb, dvb, picked, from_high, from_tensor, early = lax.optimization_barrier(
        (dq, dka, dva, dkb, dvb, picked, from_high, from_tensor, early)
    )
    early_zh = swap(early, "zh")
    late_given, late_kept, small_given, small_kept = half_call(
        functools.partial(late_weights_kernel, experts=experts),
        "late_weights",
        core,
        (normed_two, middle_low, gain_sum, gain_one[None]),
        (dq, dka, dkb, dva, dvb, logits_grads, mixed_heads),
        (4 * wide, 128),
        (turned_a, turned_b, w_query, w_key, w_value),
    )

    small = swap(small_kept, "t").astype(f32) + lax.ppermute(
        small_given, ("c", "t"), [(0, 3), (3, 0), (1, 2), (2, 1)]
    ).astype(f32)
    small = small_kept.astype(f32) + swap(small_given, "c").astype(f32) + small
    sums = call(
        expert_sums_kernel,
        "expert_sums",
        (keep_high, after(from_high, late_given), keep_tensor, from_tensor),
        [((width // 2, 3 * part), bf16)] * 4,
    )
    early = early.astype(f32) + after(early_zh, late_given).astype(f32)
    early = lax.all_gather(early.astype(bf16), PLANE, axis=0, tiled=True)
    late_taken, small, next_t, next_y, kept_u, kept_l = lax.optimization_barrier(
        (swap(late_given, "c"), small, *sums)
    )
    total = late_kept.astype(f32) + late_taken.astype(f32)
    total = jnp.concatenate([total, small], axis=1).astype(bf16)
    parts = exchange(total.reshape(16, -1, total.shape[1]), PLANE)
    parts, from_next_t = lax.optimization_barrier((parts, swap(next_t, "t")))

    to_core, to_far, to_y, own_part = call(
        normed_back_kernel,
        "normed_back",
        (after(dq, total), dka, dva, dkb, dvb, w_query, w_key, w_value),
        [of_rows_low, of_rows_low, of_rows, of_rows],
    )
    from_far = swap(to_far, "c").astype(f32)
    own_part = own_part + swap(to_core, "c").astype(f32)
    from_y = swap((to_y + from_far).astype(bf16), "yl")
    block_part = (shared_out + dot(after(placer, total), picked)).astype(bf16)
    part_sum = jnp.sum(parts.astype(f32), axis=0).astype(bf16)
    part_zh, from_block, own_part = lax.optimization_barrier(
        (swap(part_sum, "zh"), swap(block_part, "t"), own_part)
    )
    total = (part_sum.astype(f32) + part_zh.astype(f32)).astype(bf16)
    own_part = (own_part + after(from_y, total).astype(f32)).astype(bf16)
    block_out = (middle + block_part.astype(f32) + after(from_block, own_part).astype(f32)).astype(bf16)
    hidden = (width, shared_part)
    early = after(early, own_part)
    shared_grads = call(
        early_out_kernel,
        "early_out",
        (core[None], early, swap(early, "c")),
        [(hidden, f32), (hidden, f32), (hidden[::-1], f32)],
        smem=(0,),
    )
    from_next_y = swap(after(next_y, own_part), "yl")
    total, from_t, block_out, *shared_grads = lax.optimization_barrier(
        (spread(total), swap(own_part, "t"), block_out, *shared_grads)
    )
    grad_shared_gate, grad_shared_up, grad_shared_down = shared_grads
    (grad_tokens,) = call(
        first_kernel,
        "first",
        (tokens, own_part, from_t, middle_grads, gain_one[None]),
        [of_rows],
    )
    square = ((width, wide), f32)
    grad_query, grad_key, grad_value, grad_output, small = call(
        late_out_kernel,
        "late_out",
        (core[None], total, swap(total, "c")),
        [square, square, square, ((wide, width), f32), ((width, 128), f32)],
        smem=(0,),
    )
    grad_expert_gate, grad_expert_up, grad_expert_down = call(
        expert_out_kernel,
        "expert_out",
        (kept_u, from_next_t, kept_l, after(from_next_y, grad_query)),
        [((1, width, part), f32), ((1, width, part), f32), ((1, part, width), f32)],
    )
    return (
        block_out,
        grad_tokens,
        small[:, experts + 1],
        grad_query,
        grad_key,
        grad_value,
        grad_output,
        small[:, experts],
        small[:, :experts],
        grad_shared_gate,
        grad_shared_up,
        grad_shared_down,
        grad_expert_gate,
        grad_expert_up,
        grad_expert_down,
    )


def solution(mesh):
    fine = Mesh(mesh.devices.reshape(2, 4, 2, 2, 2, 2), AXES)
    placed = (
        P(EXPERT, None),
        P(EXPERT, None),
        P(),
        P(None, "t"),
        P(None, "t"),
        P(None, "t"),
        P("t", None),
        P(),
        P(),
        P(None, "t"),
        P(None, "t"),
        P("t", None),
        P(EXPERT, None, "t"),
        P(EXPERT, None, "t"),
        P(EXPERT, "t", None),
        P(EXPERT, None),
    )
    return jax.shard_map(
        local,
        mesh=fine,
        in_specs=placed,
        out_specs=(
            P(EXPERT, None),
            P(EXPERT, None),
            P(),
            P(None, "t"),
            P(None, "t"),
            P(None, "t"),
            P("t", None),
            P(),
            P(),
            P(None, "t"),
            P(None, "t"),
            P("t", None),
            P(EXPERT, None, "t"),
            P(EXPERT, None, "t"),
            P(EXPERT, "t", None),
        ),
        check_vma=False,
    )
```

```python
import functools

import jax
import jax.numpy as jnp
import numpy as np
from jax import lax
from jax.experimental import pallas as pl
from jax.experimental.pallas import tpu as pltpu
from jax.sharding import Mesh
from jax.sharding import PartitionSpec as P

HEAD_DIM = 64
BLOCK = 256
SLOTS = 40
PAIR = 128
AXES = ("zh", "x", "yh", "yl", "c", "t")
EXPERT = AXES[:5]
ROUTE = ("zh", "x", "yh")
PLANE = ("x", "yh", "yl")
CHIPS = ("zh",) + PLANE

epsilon = 1e-06
rope_base = 10000.0
bf16 = jnp.bfloat16
f32 = jnp.float32
params = pltpu.CompilerParams(vmem_limit_bytes=52 << 20)


def swap(x, axis):
    return lax.ppermute(x, axis, [(0, 1), (1, 0)])


def exchange(x, axis):
    return lax.all_to_all(x, axis, split_axis=0, concat_axis=0, tiled=True)


def after(x, first):
    return lax.optimization_barrier((x, first))[0]


def dot(a, b, dims=((1,), (0,))):
    return lax.dot_general(a, b, (dims, ((), ())), preferred_element_type=f32)


def dot_nt(a, b):
    return dot(a, b, ((1,), (1,)))


def dot_tn(a, b):
    return dot(a, b, ((0,), (0,)))


def rms_scale(values):
    return lax.rsqrt(jnp.mean(values * values, axis=-1, keepdims=True) + epsilon)


def pair_sum(values, axis):
    low = values.astype(bf16)
    return low.astype(f32) + swap(low, axis).astype(f32)


def norm_back(inputs, row_scale, gain_row, upstream):
    unit_rows = inputs * row_scale
    scaled_grad = upstream * gain_row
    return row_scale * (
        scaled_grad - unit_rows * jnp.mean(scaled_grad * unit_rows, axis=-1, keepdims=True)
    )


RATE = 57500000
TIMES = dict(
    route=4,
    project=5,
    attend=14,
    attend_back=23,
    second=4,
    shared=12,
    expert_rows=20,
    expert_given=9,
    expert_kept=9,
    expert_sum=4,
    expert_sums=3,
    expert_out=3,
    combine=4,
    back_two=4,
    normed_back=8,
    first=4,
    shared_weights=6,
    late_weights=8,
    early_out=5,
    turn_rows=3,
    half_sum=4,
    late_out=4,
)


def turn(values, cos, sin):
    half = HEAD_DIM // 2
    lanes = lax.broadcasted_iota(jnp.int32, values.shape, 1)
    first = (lanes // half) % 2 == 0
    size = values.shape[1]
    other = jnp.where(first, -pltpu.roll(values, size - half, 1), pltpu.roll(values, half, 1))
    return values * cos + other * sin


def whole(shape):
    return pl.BlockSpec(shape, lambda *_: (0,) * len(shape))


def call(kernel, name, args, outs, smem=(), grid=None, in_specs=None, out_specs=None, scratch=()):
    in_specs = dict(in_specs or {})
    out_specs = dict(out_specs or {})
    for i in smem:
        in_specs[i] = pl.BlockSpec(memory_space=pltpu.SMEM)
    return pl.pallas_call(
        kernel,
        **({} if grid is None else {"grid": grid}),
        in_specs=[in_specs.get(i, whole(a.shape)) for i, a in enumerate(args)],
        out_specs=[out_specs.get(i, whole(s)) for i, (s, _) in enumerate(outs)],
        out_shape=[jax.ShapeDtypeStruct(s, d) for s, d in outs],
        scratch_shapes=scratch,
        compiler_params=params,
        cost_estimate=pl.CostEstimate(flops=TIMES[name] * RATE, bytes_accessed=1 << 20, transcendentals=0),
        name=name,
    )(*args)


def lanes_of(rows=1, count=128):
    return lax.broadcasted_iota(jnp.int32, (rows, count), 1)


def route_kernel(tensor_ref, routes_ref, cot_ref, expand_ref, seat_ref, placer_ref, turned_ref, sent_ref):
    routes = routes_ref[...]
    rows, width = cot_ref.shape
    lanes = lanes_of(rows)
    member = (routes[:, 0:1] == lanes) | (routes[:, 1:2] == lanes)
    earlier = lax.broadcasted_iota(jnp.int32, (rows, rows), 0) > lanes_of(rows, rows)
    count = dot(
        jnp.where(earlier, 1.0, 0.0).astype(bf16), jnp.where(member, 1.0, 0.0).astype(bf16)
    )
    offset = (tensor_ref[0] * SLOTS).astype(f32)
    place = jnp.where(member, count - offset, -1.0).astype(bf16)
    placer = jnp.where(dot(place, expand_ref[...]) == seat_ref[...], 1.0, 0.0).astype(bf16)
    placer_ref[...] = placer
    turned = placer.T
    turned_ref[...] = turned
    sent_ref[:, :width] = dot(turned, cot_ref[...]).astype(bf16)
    sums = (routes[:, 0:1] + routes[:, 1:2]).astype(f32)
    sent_ref[:, width:] = dot(turned, jnp.where(lanes == 0, sums, 0.0).astype(bf16)).astype(bf16)


def route(tensor, routes, cotangent, experts):
    rows, width = cotangent.shape
    seats = experts * SLOTS
    columns = np.arange(seats)
    expand = jnp.asarray(np.arange(128)[:, None] == columns[None, :] // SLOTS, bf16)
    seat = jnp.asarray((columns % SLOTS)[None], f32)
    return call(
        route_kernel,
        "route",
        (tensor[None], routes, cotangent, expand, seat),
        [((rows, seats), bf16), ((seats, rows), bf16), ((seats, width + 128), bf16)],
        smem=(0,),
    )


def project_kernel(x0_ref, x1_ref, gain_ref, wk_ref, wv_ref, cos_ref, sin_ref, *rest):
    wq_ref = rest[0] if len(rest) == 5 else None
    n_ref, k_ref, v_ref = rest[-4:-1] if wq_ref is not None else rest
    for chunk, x_ref in enumerate((x0_ref, x1_ref)):
        rows = x_ref.shape[0]
        at_rows = slice(chunk * rows, (chunk + 1) * rows)
        x = x_ref[...].astype(f32)
        normed = (x * rms_scale(x) * gain_ref[...]).astype(bf16)
        n_ref[at_rows, :] = normed
        cos, sin = cos_ref[at_rows, :], sin_ref[at_rows, :]
        key = dot(normed, wk_ref[...])
        for at in range(0, key.shape[1], PAIR):
            lanes = slice(at, at + PAIR)
            k_ref[at_rows, lanes] = turn(key[:, lanes], cos, sin).astype(bf16)
        v_ref[at_rows, :] = dot(normed, wv_ref[...]).astype(bf16)
        if chunk == 0 and wq_ref is not None:
            q_ref = rest[-1]
            query = dot(normed, wq_ref[...])
            for at in range(0, query.shape[1], PAIR):
                lanes = slice(at, at + PAIR)
                turned = turn(query[:, lanes], cos, sin).astype(bf16)
                q_ref[:, lanes] = turned * (HEAD_DIM**-0.5)


def project(first, second, gain, w_key, w_value, cos, sin, w_query=None):
    rows, width = first.shape
    wide = w_key.shape[1]
    outs = [((2 * rows, width), bf16), ((2 * rows, wide), bf16), ((2 * rows, wide), bf16)]
    args = (first, second, gain, w_key, w_value, cos, sin)
    if w_query is not None:
        args += (w_query,)
        outs.append(((rows, wide), bf16))
    return call(project_kernel, "project", args, outs)


def attend_kernel(hide_ref, q_ref, ka_ref, va_ref, kb_ref, vb_ref, wo_ref, o_ref, lse_ref, part_ref, acc_ref):
    lanes = lanes_of()
    span = 2 * BLOCK
    step = pl.program_id(0)
    for half in range(2):
        rows = slice(half * BLOCK, (half + 1) * BLOCK)
        q = q_ref[rows, :]
        outs, logs = [], []
        for head in range(2):
            query = jnp.where(lanes // HEAD_DIM == head, q, jnp.zeros_like(q))
            spans = [(ka_ref, va_ref, 0, BLOCK * (half + 1), 0.0), (ka_ref, va_ref, span, span, hide_ref[1])]
            spans += [(kb_ref, vb_ref, 0, span, hide_ref[2]), (kb_ref, vb_ref, span, span, hide_ref[3])]
            scores = [dot_nt(query, k[a : a + n, :]) for k, _, a, n, _ in spans]
            tops = [jnp.max(s, axis=1, keepdims=True) - x[4] for s, x in zip(scores, spans)]
            top = functools.reduce(jnp.maximum, tops)
            total, acc = 0.0, 0.0
            for s, (_, v, a, n, off) in zip(scores, spans):
                p = jnp.exp(s - (top + off))
                total = total + jnp.sum(p, axis=1, keepdims=True)
                acc = acc + dot(p.astype(bf16), v[a : a + n, :])
            outs.append(acc / total)
            logs.append(top + jnp.log(total))
        mixed = jnp.where(lanes < HEAD_DIM, outs[0], outs[1]).astype(bf16)
        o_ref[rows, :] = mixed
        lse_ref[rows, :] = jnp.where(lanes < HEAD_DIM, logs[0], logs[1])
    part = dot(o_ref[...], wo_ref[...])

    @pl.when(step == 0)
    def _():
        acc_ref[...] = part

    @pl.when(step > 0)
    def _():
        acc_ref[...] += part

    @pl.when(step == pl.num_programs(0) - 1)
    def _():
        part_ref[...] = acc_ref[...].astype(bf16)


def attend(hide, q, ka, va, kb, vb, w_output):
    rows, keys = q.shape[0], ka.shape[0]
    width = w_output.shape[1]
    of_q = pl.BlockSpec((rows, PAIR), lambda p: (0, p))
    of_k = pl.BlockSpec((keys, PAIR), lambda p: (0, p))
    return call(
        attend_kernel,
        "attend",
        (hide, q, ka, va, kb, vb, w_output),
        [(q.shape, bf16), (q.shape, f32), ((rows, width), bf16)],
        smem=(0,),
        grid=(q.shape[1] // PAIR,),
        in_specs={1: of_q, 2: of_k, 3: of_k, 4: of_k, 5: of_k, 6: pl.BlockSpec((PAIR, width), lambda p: (p, 0))},
        out_specs={0: of_q, 1: of_q},
        scratch=[pltpu.VMEM((rows, width), f32)],
    )


def attend_back_kernel(
    hide_ref, q_ref, ka_ref, va_ref, kb_ref, vb_ref, o_ref, lse_ref, g_ref, ca_ref, sa_ref, cb_ref, sb_ref,
    dq_ref, dka_ref, dva_ref, dkb_ref, dvb_ref,
):
    lanes = lanes_of()
    q, g = q_ref[...], g_ref[...]
    rows = q.shape[0]
    deltas = (g.astype(f32) * o_ref[...].astype(f32)).T
    logs = lse_ref[...].T
    dq = 0.0
    near = (ka_ref, va_ref, ca_ref, sa_ref, dka_ref, dva_ref)
    far = (kb_ref, vb_ref, cb_ref, sb_ref, dkb_ref, dvb_ref)
    for block in range(8):
        k_ref, v_ref, cos_ref, sin_ref, dk_ref, dv_ref = near if block < 4 else far
        off = 0.0 if block < 2 else hide_ref[block // 2]
        first = BLOCK if block == 1 else 0
        keys = slice((block % 4) * BLOCK, (block % 4 + 1) * BLOCK)
        k, v = k_ref[keys, :], v_ref[keys, :]
        dk, dv = 0.0, 0.0
        for head in range(2):
            mine = lanes // HEAD_DIM == head
            low = head * HEAD_DIM
            query = jnp.where(mine, q[first:, :], jnp.zeros_like(q[first:, :]))
            grads = jnp.where(mine, g[first:, :], jnp.zeros_like(g[first:, :]))
            key = jnp.where(mine, k, jnp.zeros_like(k))
            log = logs[low : low + 1, first:] + off
            delta = jnp.sum(deltas[low : low + HEAD_DIM, first:], axis=0, keepdims=True)
            p = jnp.exp(dot_nt(k, query) - log)
            ds = (p * (dot_nt(v, grads) - delta)).astype(bf16)
            dv = dv + dot(p.astype(bf16), grads)
            dk = dk + dot(ds, query)
            part = dot_tn(ds, key)
            if first:
                part = jnp.concatenate([jnp.zeros((first, PAIR), f32), part], axis=0)
            dq = dq + part
        dv_ref[keys, :] = dv.astype(bf16)
        dk_ref[keys, :] = turn(dk, cos_ref[keys, :], -sin_ref[keys, :]).astype(bf16)
    dq = dq * (HEAD_DIM**-0.5)
    dq_ref[...] = turn(dq, ca_ref[:rows, :], -sa_ref[:rows, :]).astype(bf16)


def attend_back(hide, q, ka, va, kb, vb, o, lse, g, ca, sa, cb, sb):
    rows, keys = q.shape[0], ka.shape[0]
    of_q = pl.BlockSpec((rows, PAIR), lambda p: (0, p))
    of_k = pl.BlockSpec((keys, PAIR), lambda p: (0, p))
    return call(
        attend_back_kernel,
        "attend_back",
        (hide, q, ka, va, kb, vb, o, lse, g, ca, sa, cb, sb),
        [(q.shape, bf16)] + [(ka.shape, bf16)] * 4,
        smem=(0,),
        grid=(q.shape[1] // PAIR,),
        in_specs={1: of_q, 2: of_k, 3: of_k, 4: of_k, 5: of_k, 6: of_q, 7: of_q, 8: of_q},
        out_specs={0: of_q, 1: of_k, 2: of_k, 3: of_k, 4: of_k},
    )


def turn_rows_kernel(a_ref, b_ref, ta_ref, tb_ref):
    ta_ref[...] = a_ref[...].T
    tb_ref[...] = b_ref[...].T


def half_sum_kernel(kept_ref, taken_ref, out_ref):
    out_ref[...] = kept_ref[...] + taken_ref[...]


def second_kernel(x_ref, mine_ref, theirs_ref, gain_ref, turned_ref, cot_ref, middle_ref, n_ref, sent_ref):
    middle = x_ref[...].astype(f32) + (mine_ref[...].astype(f32) + theirs_ref[...].astype(f32))
    middle_ref[...] = middle
    normed = (middle * rms_scale(middle) * gain_ref[...]).astype(bf16)
    n_ref[...] = normed
    width = normed.shape[1]
    sent_ref[:, :width] = dot(turned_ref[...], normed).astype(bf16)
    sent_ref[:, width:] = cot_ref[...]


def swish(gate, up, grads):
    sigmoid = jax.nn.sigmoid(gate)
    unit = gate * sigmoid
    slope = sigmoid + unit * (1.0 - sigmoid)
    return (unit * up).astype(bf16), (grads * up * slope).astype(bf16), (grads * unit).astype(bf16)


def shared_kernel(
    n_ref, cot_ref, sg_ref, su_ref, sd_ref, router_ref, routes_ref, h_ref, gg_ref, gu_ref, back_ref, out_ref, share_ref
):
    normed, cot = n_ref[...], cot_ref[...]
    sg, su, sd = sg_ref[...], su_ref[...], sd_ref[...]
    hidden, gg, gu = swish(dot(normed, sg), dot(normed, su), dot_nt(cot, sd))
    h_ref[...], gg_ref[...], gu_ref[...] = hidden, gg, gu
    back = dot_nt(gg, sg) + dot_nt(gu, su)
    out = dot(hidden, sd)

    @pl.when(pl.program_id(0) == 0)
    def _():
        back_ref[...] = back
        out_ref[...] = out
        logits = dot(normed, router_ref[...])
        routes = routes_ref[...]
        lanes = lanes_of()
        first, second = lanes == routes[:, 0:1], lanes == routes[:, 1:2]
        one = jnp.sum(jnp.where(first, logits, 0.0), axis=1, keepdims=True)
        two = jnp.sum(jnp.where(second, logits, 0.0), axis=1, keepdims=True)
        top = jnp.maximum(one, two)
        one, two = jnp.exp(one - top), jnp.exp(two - top)
        share_ref[...] = (jnp.where(first, one, 0.0) + jnp.where(second, two, 0.0)) / (one + two)

    @pl.when(pl.program_id(0) > 0)
    def _():
        back_ref[...] += back
        out_ref[...] += out


def shared(normed, cot, shared_gate, shared_up, shared_down, router, routes):
    rows, width = normed.shape
    hidden = shared_gate.shape[1]
    block = 512
    columns = pl.BlockSpec((width, block), lambda k: (0, k))
    of_hidden = pl.BlockSpec((rows, block), lambda k: (0, k))
    return call(
        shared_kernel,
        "shared",
        (normed, cot, shared_gate, shared_up, shared_down, router, routes),
        [((rows, hidden), bf16)] * 3 + [((rows, width), f32)] * 2 + [((rows, 128), f32)],
        grid=(hidden // block,),
        in_specs={2: columns, 3: columns, 4: pl.BlockSpec((block, width), lambda k: (k, 0))},
        out_specs={0: of_hidden, 1: of_hidden, 2: of_hidden},
    )


def store_half(given_ref, kept_ref, at, value):
    value = value.astype(bf16)

    @pl.when(pl.program_id(0) == 0)
    def _():
        given_ref[:, at : at + value.shape[1]] = value

    @pl.when(pl.program_id(0) == 1)
    def _():
        kept_ref[:, at : at + value.shape[1]] = value


def shared_weights_kernel(core_ref, n_ref, cot_ref, gg_ref, gu_ref, h_ref, given_ref, kept_ref):
    part = h_ref.shape[1]
    turned = n_ref[...].T
    store_half(given_ref, kept_ref, 0, dot(turned, gg_ref[...]))
    store_half(given_ref, kept_ref, part, dot(turned, gu_ref[...]))
    store_half(given_ref, kept_ref, 2 * part, dot(cot_ref[...].T, h_ref[...]))


def half_call(kernel, name, core, halved, full, columns, by_rows=()):
    half = halved[0].shape[1] // 2
    specs = [pl.BlockSpec((a.shape[0], half), lambda s, c: (0, jnp.where(s == 0, 1 - c[0], c[0]))) for a in halved]
    specs += [
        pl.BlockSpec((half, a.shape[1]), lambda s, c: (jnp.where(s == 0, 1 - c[0], c[0]), 0))
        for a in by_rows
    ]
    specs += [pl.BlockSpec(a.shape, lambda s, c: (0, 0)) for a in full]
    return pl.pallas_call(
        kernel,
        grid_spec=pltpu.PrefetchScalarGridSpec(
            num_scalar_prefetch=1,
            grid=(2,),
            in_specs=specs,
            out_specs=[pl.BlockSpec((half, c), lambda s, c: (0, 0)) for c in columns for _ in range(2)],
        ),
        out_shape=[jax.ShapeDtypeStruct((half, c), bf16) for c in columns for _ in range(2)],
        compiler_params=params,
        cost_estimate=pl.CostEstimate(flops=TIMES[name] * RATE, bytes_accessed=1 << 20, transcendentals=0),
        name=name,
    )(core[None], *halved, *by_rows, *full)


def late_weights_kernel(
    core_ref, n2_ref, low_ref, gain_ref, scale_ref, ta_ref, tb_ref, wq_ref, wk_ref, wv_ref,
    dq_ref, dka_ref, dkb_ref, dva_ref, dvb_ref, lg_ref, o_ref, given_ref, kept_ref, small_given_ref, small_kept_ref, *, experts
):
    def column(row_ref):
        return jnp.broadcast_to(row_ref[...], (128, row_ref.shape[1])).T

    wide = dq_ref.shape[1]
    rows = dq_ref.shape[0]
    ta, tb = ta_ref[...], tb_ref[...]
    grad_q = dot(ta[:, :rows], dq_ref[...])
    grad_k = dot(ta, dka_ref[...]) + dot(tb, dkb_ref[...])
    grad_v = dot(ta, dva_ref[...]) + dot(tb, dvb_ref[...])
    for i, value in enumerate((grad_q, grad_k, grad_v, dot(low_ref[...].T, o_ref[...]))):
        store_half(given_ref, kept_ref, i * wide, value)
    small = dot(n2_ref[...].T, lg_ref[...])
    terms = grad_q * wq_ref[...].astype(f32) + grad_k * wk_ref[...].astype(f32) + grad_v * wv_ref[...].astype(f32)
    gain_one = jnp.sum(terms, axis=1, keepdims=True) / column(scale_ref)
    lanes = lanes_of()
    small = jnp.where(lanes == experts, 0.5 * column(gain_ref), small)
    store_half(small_given_ref, small_kept_ref, 0, jnp.where(lanes == experts + 1, gain_one, small))


def expert_kernel(
    here_ref, sent_ref, router_ref, *refs, experts, shards
):
    w_refs = refs[:shards]
    hidden_ref, grads_ref, back_ref, scaled_ref, out_ref, share_ref, acc_ref, dots_ref, slots_ref, sems = refs[shards:]
    step = pl.program_id(0)
    width = router_ref.shape[0]

    def fetch(i, slot):
        return pltpu.make_async_copy(w_refs[i], slots_ref.at[slot], sems.at[slot])

    @pl.when(step == 0)
    def _():
        fetch(0, 0).start()

    for i in range(1, shards):
        @pl.when(step == i - 1)
        def _(i=i):
            fetch(i, i % 2).start()

    slot = lax.rem(step, 2)
    fetch(0, slot).wait()
    w = slots_ref.at[slot]
    part = w.shape[1] // 3
    half = sent_ref.shape[0] // 2
    w_in, w_down = w[:, : 2 * part], w[:, 2 * part :]
    for at in (0, half):
        these = slice(at, at + half)
        rows, cot = sent_ref[these, :width], sent_ref[these, width : 2 * width]
        both = dot(rows, w_in)
        hidden_grads = dot(cot, w_down)
        hidden, gg, gu = swish(both[:, :part], both[:, part:], hidden_grads)
        hidden_ref[0, these, :] = hidden
        grads_ref[0, these, :part] = gg
        grads_ref[0, these, part:] = gu
        product = hidden.astype(f32) * hidden_grads
        product = functools.reduce(jnp.add, [product[:, a : a + 128] for a in range(0, part, 128)])
        back = dot_nt(gg, w[:, :part]) + dot_nt(gu, w[:, part : 2 * part])
        acc_ref[these, :] = jnp.where(step == 0, 0.0, acc_ref[these, :]) + back
        dots_ref[these, :] = jnp.where(step == 0, 0.0, dots_ref[these, :]) + product

    @pl.when(step == pl.num_programs(0) - 1)
    def _():
        rows, cot = sent_ref[:, :width], sent_ref[:, width : 2 * width]
        here = here_ref[0]
        lanes = lanes_of()
        logits = dot(rows, router_ref[...])
        other = sent_ref[:, 2 * width :].astype(f32)[:, :1].astype(jnp.int32) - here
        own_logit = jnp.sum(jnp.where(lanes == here, logits, 0.0), axis=1, keepdims=True)
        other_logit = jnp.sum(jnp.where(lanes == other, logits, 0.0), axis=1, keepdims=True)
        top = jnp.maximum(own_logit, other_logit)
        own = jnp.exp(own_logit - top)
        share = own / (own + jnp.exp(other_logit - top))
        share_ref[...] = jnp.broadcast_to(share, share_ref.shape)
        scaled_ref[...] = (share * rows.astype(f32)).astype(bf16)
        out_ref[...] = (share * cot.astype(f32)).astype(bf16)
        back_ref[:, :width] = (share * acc_ref[...]).astype(bf16)
        dots = jnp.sum(dots_ref[...], axis=1, keepdims=True)
        high = dots.astype(bf16).astype(f32)
        back_ref[:, width:] = (
            jnp.where(lanes == here, high, 0.0)
            + jnp.where(lanes == experts + here, dots - high, 0.0)
        ).astype(bf16)


def expert_rows(here, sent, router, weights, experts):
    rows, width = sent.shape[0], router.shape[0]
    shards, packed = len(weights), weights[0].shape[1]
    part = packed // 3
    return call(
        functools.partial(expert_kernel, experts=experts, shards=shards),
        "expert_rows",
        (here[None], sent, router, *weights),
        [
            ((shards, rows, part), bf16),
            ((shards, rows, 2 * part), bf16),
            ((rows, width + 128), bf16),
            ((rows, width), bf16),
            ((rows, width), bf16),
            ((rows, 128), f32),
        ],
        smem=(0,),
        grid=(shards,),
        in_specs={3 + i: pl.BlockSpec(memory_space=pl.ANY) for i in range(shards)},
        out_specs={
            0: pl.BlockSpec((1, rows, part), lambda k: (k, 0, 0)),
            1: pl.BlockSpec((1, rows, 2 * part), lambda k: (k, 0, 0)),
        },
        scratch=[
            pltpu.VMEM((rows, width), f32),
            pltpu.VMEM((rows, 128), f32),
            pltpu.VMEM((2, width, packed), bf16),
            pltpu.SemaphoreType.DMA((2,)),
        ],
    )


def expert_given_kernel(scaled_ref, out_ref, hidden_ref, grads_ref, *refs, shards):
    w_refs = refs[:shards]
    d_ref, acc_ref, st_ref, ot_ref, slots_ref, sems = refs[shards:]
    step = pl.program_id(0)

    @pl.when(step == 0)
    def _():
        st_ref[...] = scaled_ref[...].T
        ot_ref[...] = out_ref[...].T

    expert_step(step, st_ref, ot_ref, hidden_ref, grads_ref, w_refs, d_ref, slots_ref, sems, acc_ref, None)


def expert_kept_kernel(st_ref, ot_ref, share_ref, first_ref, hidden_ref, grads_ref, *refs, shards):
    w_refs = refs[:shards]
    d_ref, picked_ref, acc_ref, slots_ref, sems = refs[shards:]
    step = pl.program_id(0)
    expert_step(step, st_ref, ot_ref, hidden_ref, grads_ref, w_refs, d_ref, slots_ref, sems, acc_ref, first_ref)

    @pl.when(step == pl.num_programs(0) - 1)
    def _():
        picked_ref[...] = (share_ref[:, :1] * acc_ref[...]).astype(bf16)


def expert_step(step, st_ref, ot_ref, hidden_ref, grads_ref, w_refs, d_ref, slots_ref, sems, acc_ref, first_ref):
    part = hidden_ref.shape[2]

    def fetch(i, slot):
        return pltpu.make_async_copy(w_refs[i].at[:, 2 * part :], slots_ref.at[slot], sems.at[slot])

    @pl.when(step == 0)
    def _():
        fetch(0, 0).start()
        acc_ref[...] = jnp.zeros_like(acc_ref) if first_ref is None else first_ref[...]

    for i in range(1, len(w_refs)):
        @pl.when(step == i - 1)
        def _(i=i):
            fetch(i, i % 2).start()

    slot = lax.rem(step, 2)
    fetch(0, slot).wait()
    d_ref[0, :, : 2 * part] = dot(st_ref[...], grads_ref[0]).astype(bf16)
    d_ref[0, :, 2 * part :] = dot(ot_ref[...], hidden_ref[0]).astype(bf16)
    acc_ref[...] += dot_nt(hidden_ref[0], slots_ref[slot])


def expert_half(kernel, name, args, hidden, grads, weights, at, extra):
    shards = len(weights)
    _, rows, part = hidden.shape
    width = weights[0].shape[0]
    count = len(args)
    return call(
        functools.partial(kernel, shards=shards),
        name,
        (*args, hidden, grads, *weights),
        [((shards, width, 3 * part), bf16), *extra],
        grid=(shards,),
        in_specs={
            count: pl.BlockSpec((1, rows, part), lambda k: (k + at, 0, 0)),
            count + 1: pl.BlockSpec((1, rows, 2 * part), lambda k: (k + at, 0, 0)),
            **{count + 2 + i: pl.BlockSpec(memory_space=pl.ANY) for i in range(shards)},
        },
        out_specs={0: pl.BlockSpec((1, width, 3 * part), lambda k: (k, 0, 0))},
        scratch=([pltpu.VMEM((rows, width), f32)] if at else [])
        + [pltpu.VMEM((2, width, part), bf16), pltpu.SemaphoreType.DMA((2,))],
    )


def expert_sum_kernel(kept_ref, taken_ref, high_ref, tensor_ref, keep_high_ref, keep_tensor_ref):
    shard = pl.program_id(0)
    half = kept_ref.shape[1] // 2
    total = kept_ref[0] + taken_ref[0]
    for ref, at, here in (
        (keep_high_ref, 0, shard < 2),
        (high_ref, 0, shard >= 2),
        (keep_tensor_ref, half, shard % 2 == 0),
        (tensor_ref, half, shard % 2 == 1),
    ):
        @pl.when(here)
        def _(ref=ref, at=at):
            ref[0] = total[at : at + half]


def expert_sums_kernel(kh_ref, fh_ref, kt_ref, ft_ref, to_t_ref, to_y_ref, kept_u_ref, kept_l_ref):
    to_t_ref[...] = kh_ref[1] + fh_ref[1]
    to_y_ref[...] = kt_ref[1] + ft_ref[1]
    kept_u_ref[...] = kh_ref[0] + fh_ref[0]
    kept_l_ref[...] = kt_ref[0] + ft_ref[0]


def expert_out_kernel(ku_ref, fu_ref, kl_ref, fl_ref, gate_ref, up_ref, down_ref):
    half = ku_ref.shape[0]
    part = gate_ref.shape[2]
    for at, (kept_ref, from_ref) in ((0, (ku_ref, fu_ref)), (half, (kl_ref, fl_ref))):
        total = kept_ref[...].astype(f32) + from_ref[...].astype(f32)
        gate_ref[0, at : at + half, :] = total[:, :part]
        up_ref[0, at : at + half, :] = total[:, part : 2 * part]
        down_ref[0, :, at : at + half] = total[:, 2 * part :].T


def combine_kernel(placer_ref, back_ref, share_ref, router_ref, shared_ref, part_ref, lg_ref, *, experts):
    width = shared_ref.shape[1]
    placer = placer_ref[...]
    lanes = lanes_of()
    dots = dot(placer, back_ref[:, width:])
    dots = jnp.where(lanes < experts, dots + pltpu.roll(dots, 128 - experts, 1), 0.0)
    share = share_ref[...]
    grads = (share * (dots - jnp.sum(share * dots, axis=1, keepdims=True))).astype(bf16)
    lg_ref[...] = grads
    total = shared_ref[...] + dot_nt(grads, router_ref[...]) + dot(placer, back_ref[:, :width])
    part_ref[...] = total.astype(bf16)


def back_two_kernel(middle_ref, mine_ref, theirs_ref, cot_ref, gain_ref, wo_ref, grads_ref, low_ref, mixed_ref, sum_ref):
    middle = middle_ref[...]
    scale = rms_scale(middle)
    upstream = mine_ref[...].astype(f32) + theirs_ref[...].astype(f32)
    sum_ref[...] = jnp.sum(upstream * (middle * scale), axis=0, keepdims=True)
    grads = cot_ref[...].astype(f32) + norm_back(middle, scale, gain_ref[...], upstream)
    grads_ref[...] = grads
    low = grads.astype(bf16)
    low_ref[...] = low
    mixed_ref[...] = dot_nt(low, wo_ref[...]).astype(bf16)


def normed_back_kernel(dq_ref, dka_ref, dva_ref, dkb_ref, dvb_ref, wq_ref, wk_ref, wv_ref, core_ref, far_ref, y_ref, own_ref):
    rows = dq_ref.shape[0]
    wk, wv = wk_ref[...], wv_ref[...]

    def back(dk_ref, dv_ref, chunk):
        these = slice(chunk * rows, (chunk + 1) * rows)
        return dot_nt(dk_ref[these, :], wk) + dot_nt(dv_ref[these, :], wv)

    far_ref[...] = back(dkb_ref, dvb_ref, 1).astype(bf16)
    core_ref[...] = back(dka_ref, dva_ref, 1).astype(bf16)
    y_ref[...] = back(dkb_ref, dvb_ref, 0)
    own_ref[...] = back(dka_ref, dva_ref, 0) + dot_nt(dq_ref[...], wq_ref[...])


def first_kernel(x_ref, mine_ref, theirs_ref, grads_ref, gain_ref, out_ref):
    x = x_ref[...].astype(f32)
    upstream = mine_ref[...].astype(f32) + theirs_ref[...].astype(f32)
    out_ref[...] = grads_ref[...] + norm_back(x, rms_scale(x), gain_ref[...], upstream)


def spread(part):
    copies = jnp.broadcast_to(part[None], (16,) + part.shape)
    return exchange(copies, PLANE).reshape(-1, part.shape[1])


def late_out_kernel(core_ref, mine_ref, theirs_ref, q_ref, k_ref, v_ref, o_ref, small_ref):
    half, wide = mine_ref.shape[0], q_ref.shape[1]
    for at, ref in ((0, mine_ref), (1, theirs_ref)):
        place = core_ref[0] if at == 0 else 1 - core_ref[0]
        these = pl.ds(pl.multiple_of(place * half, 128), half)
        for i, out_ref in enumerate((q_ref, k_ref, v_ref)):
            out_ref[these, :] = ref[:, i * wide : (i + 1) * wide].astype(f32)
        o_ref[:, these] = ref[:, 3 * wide : 4 * wide].astype(f32).T
        small_ref[these, :] = ref[:, 4 * wide :].astype(f32)


def early_out_kernel(core_ref, mine_ref, theirs_ref, gate_ref, up_ref, down_ref):
    half, wide = mine_ref.shape[0], gate_ref.shape[1]
    for at, ref in ((0, mine_ref), (1, theirs_ref)):
        place = core_ref[0] if at == 0 else 1 - core_ref[0]
        these = pl.ds(pl.multiple_of(place * half, 128), half)
        for i, out_ref in enumerate((gate_ref, up_ref)):
            out_ref[these, :] = ref[:, i * wide : (i + 1) * wide].astype(f32)
        down_ref[:, these] = ref[:, 2 * wide :].astype(f32).T


def local(
    tokens,
    routes,
    gain_one,
    w_query,
    w_key,
    w_value,
    w_output,
    gain_two,
    w_router,
    shared_gate,
    shared_up,
    shared_down,
    expert_gate,
    expert_up,
    expert_down,
    cotangent,
):
    rows, width = tokens.shape
    wide = w_query.shape[1]
    experts = w_router.shape[1]
    seats = experts * SLOTS
    part = expert_gate.shape[2]
    shared_part = shared_gate.shape[1]
    tensor = lax.axis_index("t")
    core = lax.axis_index("c")
    high = lax.axis_index("yl")
    expert_here = lax.axis_index(ROUTE)
    router = jnp.pad(w_router, ((0, 0), (0, 128 - experts)))
    of_rows = ((rows, width), f32)
    of_rows_low = ((rows, width), bf16)

    tokens_y = swap(tokens, "yl")
    tokens_c = swap(tokens, "c")
    hide = jnp.stack([core < 0, core == 0, high == 0, high == 0])
    hide = jnp.where(hide, 1e30, 0.0).astype(f32)

    frequency = rope_base ** (-np.arange(HEAD_DIM // 2) * 2.0 / HEAD_DIM)
    frequency = np.tile(frequency, PAIR // (HEAD_DIM // 2))
    inner = np.arange(rows)[:, None] * frequency[None, :]
    starts = jnp.stack(
        [((high ^ my) * 2 + (core ^ mc)) * rows for my, mc in ((0, 0), (0, 1), (1, 0), (1, 1))]
    )
    outer = starts.astype(f32)[:, None, None] * frequency.astype(np.float32)[None, None, :]
    cos_in, sin_in = np.cos(inner).astype(np.float32), np.sin(inner).astype(np.float32)
    cos_out, sin_out = jnp.cos(outer), jnp.sin(outer)
    cosine = (cos_out * cos_in - sin_out * sin_in).reshape(2, 2 * rows, PAIR)
    sine = (sin_out * cos_in + cos_out * sin_in).reshape(2, 2 * rows, PAIR)

    own = jnp.concatenate([expert_gate[0], expert_up[0], expert_down[0].T], axis=1)
    placer, placer_turned, sent_cot = route(tensor, routes, cotangent, experts)
    normed_a, keys_a, values_a, query = project(
        tokens, tokens_c, gain_one[None], w_key, w_value, cosine[0], sine[0], w_query
    )
    tokens_y, keys_a, placer, placer_turned, sent_cot, own_later = lax.optimization_barrier(
        (tokens_y, keys_a, placer, placer_turned, sent_cot, own)
    )
    tokens_yc = swap(tokens_y, "c")
    own_t, own_y = swap(own, "t"), swap(own_later, "yl")
    normed_b, keys_b, values_b = project(
        tokens_y, tokens_yc, gain_one[None], w_key, w_value, cosine[1], sine[1]
    )
    mixed_heads, logs, attended = attend(
        hide, query, keys_a, values_a, keys_b, values_b, w_output
    )
    attended, own_t, own_later = lax.optimization_barrier((attended, own_t, own_later))

    own_ty = swap(own_t, "yl")
    turned_a, turned_b = call(
        turn_rows_kernel,
        "turn_rows",
        (after(normed_a, attended), normed_b),
        [((width, 2 * rows), bf16)] * 2,
    )
    theirs, own_y, turned_a, turned_b = lax.optimization_barrier(
        (swap(attended, "t"), own_y, turned_a, turned_b)
    )
    middle, normed_two, sent_rows = call(
        second_kernel,
        "second",
        (tokens, attended, theirs, gain_two[None], placer_turned, sent_cot),
        [of_rows, of_rows_low, ((seats, 2 * width + 128), bf16)],
    )

    arrived = exchange(sent_rows.reshape(experts, SLOTS, -1), ROUTE).reshape(seats, -1)
    hidden_shared, shared_gg, shared_gu, shared_back, shared_out, share = shared(
        normed_two, cotangent, shared_gate, shared_up, shared_down, router, routes
    )
    early_given, early_kept = half_call(
        shared_weights_kernel,
        "shared_weights",
        core,
        (normed_two, cotangent),
        (shared_gg, shared_gu, hidden_shared),
        (3 * shared_part,),
    )
    weights = [own_later, own_t, own_y, own_ty]
    weights = [swap(w, "c") for w in weights] + weights
    arrived, early_given, early_kept, shared_back, shared_out, share, *weights = (
        lax.optimization_barrier(
            (arrived, early_given, early_kept, shared_back, shared_out, share, *weights)
        )
    )
    early_taken = swap(early_given, "c")
    hidden_expert, expert_grads, back, scaled_rows, out_grads, row_share = expert_rows(
        expert_here, arrived, router, weights, experts
    )
    given, first_out, scaled_turned, out_turned = expert_half(
        expert_given_kernel,
        "expert_given",
        (scaled_rows, out_grads),
        hidden_expert,
        expert_grads,
        weights[:4],
        0,
        [((seats, width), f32), ((width, seats), bf16), ((width, seats), bf16)],
    )
    (early,) = call(
        half_sum_kernel, "half_sum", (after(early_kept, back), early_taken), [(early_kept.shape, bf16)]
    )
    back = exchange(back.reshape(experts, SLOTS, -1), ROUTE).reshape(seats, -1)
    back, given, first_out, scaled_turned, out_turned, early = lax.optimization_barrier(
        (back, given, first_out, scaled_turned, out_turned, early)
    )

    mine, logits_grads = call(
        functools.partial(combine_kernel, experts=experts),
        "combine",
        (placer, back, share, router, shared_back),
        [of_rows_low, ((rows, 128), bf16)],
    )
    kept, picked = expert_half(
        expert_kept_kernel,
        "expert_kept",
        (after(scaled_turned, mine), out_turned, row_share, first_out),
        hidden_expert,
        expert_grads,
        weights[4:],
        4,
        [((seats, width), bf16)],
    )
    of_shard = pl.BlockSpec((1, width, 3 * part), lambda k: (k, 0, 0))
    half_shard = (1, width // 2, 3 * part)
    to_high, to_tensor, keep_high, keep_tensor = call(
        expert_sum_kernel,
        "expert_sum",
        (kept, swap(given, "c")),
        [((2, width // 2, 3 * part), bf16)] * 4,
        grid=(4,),
        in_specs={0: of_shard, 1: of_shard},
        out_specs={
            0: pl.BlockSpec(half_shard, lambda k: (jnp.maximum(k - 2, 0), 0, 0)),
            1: pl.BlockSpec(half_shard, lambda k: (k // 2, 0, 0)),
            2: pl.BlockSpec(half_shard, lambda k: (jnp.minimum(k, 1), 0, 0)),
            3: pl.BlockSpec(half_shard, lambda k: (k // 2, 0, 0)),
        },
    )
    theirs, to_high, to_tensor, keep_high, keep_tensor, picked = lax.optimization_barrier(
        (swap(mine, "t"), to_high, to_tensor, keep_high, keep_tensor, picked)
    )
    middle_grads, middle_low, mixed_grads, gain_sum = call(
        back_two_kernel,
        "back_two",
        (middle, mine, theirs, cotangent, gain_two[None], w_output),
        [of_rows, of_rows_low, ((rows, wide), bf16), ((1, width), f32)],
    )

    dq, dka, dva, dkb, dvb = attend_back(
        hide, query, keys_a, values_a, keys_b, values_b, mixed_heads, logs, mixed_grads,
        cosine[0], sine[0], cosine[1], sine[1],
    )
    picked = exchange(picked.reshape(experts, SLOTS, width), ROUTE).reshape(seats, width)
    from_high, from_tensor = swap(to_high, "yl"), swap(to_tensor, "t")
    early = lax.psum_scatter(early, "x", scatter_dimension=0, tiled=True)
    early = lax.psum_scatter(early, ("yh", "yl"), scatter_dimension=0, tiled=True)
    dq, dka, dva, dkb, dvb, picked, from_high, from_tensor, early = lax.optimization_barrier(
        (dq, dka, dva, dkb, dvb, picked, from_high, from_tensor, early)
    )
    early_zh = swap(early, "zh")
    late_given, late_kept, small_given, small_kept = half_call(
        functools.partial(late_weights_kernel, experts=experts),
        "late_weights",
        core,
        (normed_two, middle_low, gain_sum, gain_one[None]),
        (dq, dka, dkb, dva, dvb, logits_grads, mixed_heads),
        (4 * wide, 128),
        (turned_a, turned_b, w_query, w_key, w_value),
    )

    small = swap(small_kept, "t").astype(f32) + lax.ppermute(
        small_given, ("c", "t"), [(0, 3), (3, 0), (1, 2), (2, 1)]
    ).astype(f32)
    small = small_kept.astype(f32) + swap(small_given, "c").astype(f32) + small
    sums = call(
        expert_sums_kernel,
        "expert_sums",
        (keep_high, after(from_high, late_given), keep_tensor, from_tensor),
        [((width // 2, 3 * part), bf16)] * 4,
    )
    early = early.astype(f32) + after(early_zh, late_given).astype(f32)
    early = lax.all_gather(early.astype(bf16), PLANE, axis=0, tiled=True)
    late_taken, small, next_t, next_y, kept_u, kept_l = lax.optimization_barrier(
        (swap(late_given, "c"), small, *sums)
    )
    total = late_kept.astype(f32) + late_taken.astype(f32)
    total = jnp.concatenate([total, small], axis=1).astype(bf16)
    parts = exchange(total.reshape(16, -1, total.shape[1]), PLANE)
    parts, from_next_t = lax.optimization_barrier((parts, swap(next_t, "t")))

    to_core, to_far, to_y, own_part = call(
        normed_back_kernel,
        "normed_back",
        (after(dq, total), dka, dva, dkb, dvb, w_query, w_key, w_value),
        [of_rows_low, of_rows_low, of_rows, of_rows],
    )
    from_far = swap(to_far, "c").astype(f32)
    own_part = own_part + swap(to_core, "c").astype(f32)
    from_y = swap((to_y + from_far).astype(bf16), "yl")
    block_part = (shared_out + dot(after(placer, total), picked)).astype(bf16)
    part_sum = jnp.sum(parts.astype(f32), axis=0).astype(bf16)
    part_zh, from_block, own_part = lax.optimization_barrier(
        (swap(part_sum, "zh"), swap(block_part, "t"), own_part)
    )
    total = (part_sum.astype(f32) + part_zh.astype(f32)).astype(bf16)
    own_part = (own_part + after(from_y, total).astype(f32)).astype(bf16)
    block_out = (middle + block_part.astype(f32) + after(from_block, own_part).astype(f32)).astype(bf16)
    hidden = (width, shared_part)
    early = after(early, own_part)
    shared_grads = call(
        early_out_kernel,
        "early_out",
        (core[None], early, swap(early, "c")),
        [(hidden, f32), (hidden, f32), (hidden[::-1], f32)],
        smem=(0,),
    )
    from_next_y = swap(after(next_y, own_part), "yl")
    total, from_t, block_out, *shared_grads = lax.optimization_barrier(
        (spread(total), swap(own_part, "t"), block_out, *shared_grads)
    )
    grad_shared_gate, grad_shared_up, grad_shared_down = shared_grads
    (grad_tokens,) = call(
        first_kernel,
        "first",
        (tokens, own_part, from_t, middle_grads, gain_one[None]),
        [of_rows],
    )
    square = ((width, wide), f32)
    grad_query, grad_key, grad_value, grad_output, small = call(
        late_out_kernel,
        "late_out",
        (core[None], total, swap(total, "c")),
        [square, square, square, ((wide, width), f32), ((width, 128), f32)],
        smem=(0,),
    )
    grad_expert_gate, grad_expert_up, grad_expert_down = call(
        expert_out_kernel,
        "expert_out",
        (kept_u, from_next_t, kept_l, after(from_next_y, grad_query)),
        [((1, width, part), f32), ((1, width, part), f32), ((1, part, width), f32)],
    )
    return (
        block_out,
        grad_tokens,
        small[:, experts + 1],
        grad_query,
        grad_key,
        grad_value,
        grad_output,
        small[:, experts],
        small[:, :experts],
        grad_shared_gate,
        grad_shared_up,
        grad_shared_down,
        grad_expert_gate,
        grad_expert_up,
        grad_expert_down,
    )


def solution(mesh):
    fine = Mesh(mesh.devices.reshape(2, 4, 2, 2, 2, 2), AXES)
    placed = (
        P(EXPERT, None),
        P(EXPERT, None),
        P(),
        P(None, "t"),
        P(None, "t"),
        P(None, "t"),
        P("t", None),
        P(),
        P(),
        P(None, "t"),
        P(None, "t"),
        P("t", None),
        P(EXPERT, None, "t"),
        P(EXPERT, None, "t"),
        P(EXPERT, "t", None),
        P(EXPERT, None),
    )
    return jax.shard_map(
        local,
        mesh=fine,
        in_specs=placed,
        out_specs=(
            P(EXPERT, None),
            P(EXPERT, None),
            P(),
            P(None, "t"),
            P(None, "t"),
            P(None, "t"),
            P("t", None),
            P(),
            P(),
            P(None, "t"),
            P(None, "t"),
            P("t", None),
            P(EXPERT, None, "t"),
            P(EXPERT, None, "t"),
            P(EXPERT, "t", None),
        ),
        check_vma=False,
    )
```

```python
import functools

import jax
import jax.numpy as jnp
import numpy as np
from jax import lax
from jax.experimental import pallas as pl
from jax.experimental.pallas import tpu as pltpu
from jax.sharding import Mesh
from jax.sharding import PartitionSpec as P

HEAD_DIM = 64
BLOCK = 256
SLOTS = 40
PAIR = 128
AXES = ("zh", "x", "yh", "yl", "c", "t")
EXPERT = AXES[:5]
ROUTE = ("zh", "x", "yh")
PLANE = ("x", "yh", "yl")
CHIPS = ("zh",) + PLANE

epsilon = 1e-06
rope_base = 10000.0
bf16 = jnp.bfloat16
f32 = jnp.float32
params = pltpu.CompilerParams(vmem_limit_bytes=52 << 20)


def swap(x, axis):
    return lax.ppermute(x, axis, [(0, 1), (1, 0)])


def exchange(x, axis):
    return lax.all_to_all(x, axis, split_axis=0, concat_axis=0, tiled=True)


def after(x, first):
    return lax.optimization_barrier((x, first))[0]


def dot(a, b, dims=((1,), (0,))):
    return lax.dot_general(a, b, (dims, ((), ())), preferred_element_type=f32)


def dot_nt(a, b):
    return dot(a, b, ((1,), (1,)))


def dot_tn(a, b):
    return dot(a, b, ((0,), (0,)))


def rms_scale(values):
    return lax.rsqrt(jnp.mean(values * values, axis=-1, keepdims=True) + epsilon)


def pair_sum(values, axis):
    low = values.astype(bf16)
    return low.astype(f32) + swap(low, axis).astype(f32)


def norm_back(inputs, row_scale, gain_row, upstream):
    unit_rows = inputs * row_scale
    scaled_grad = upstream * gain_row
    return row_scale * (
        scaled_grad - unit_rows * jnp.mean(scaled_grad * unit_rows, axis=-1, keepdims=True)
    )


RATE = 57500000
TIMES = dict(
    route=4,
    project=5,
    attend=14,
    attend_back=23,
    second=4,
    shared=12,
    expert_rows=20,
    expert_given=9,
    expert_kept=9,
    expert_sum=4,
    expert_sums=3,
    expert_out=3,
    combine=4,
    back_two=4,
    normed_back=8,
    first=4,
    shared_weights=6,
    late_weights=8,
    early_out=5,
    turn_rows=3,
    half_sum=4,
    late_out=4,
)


def turn(values, cos, sin):
    half = HEAD_DIM // 2
    lanes = lax.broadcasted_iota(jnp.int32, values.shape, 1)
    first = (lanes // half) % 2 == 0
    size = values.shape[1]
    other = jnp.where(first, -pltpu.roll(values, size - half, 1), pltpu.roll(values, half, 1))
    return values * cos + other * sin


def whole(shape):
    return pl.BlockSpec(shape, lambda *_: (0,) * len(shape))


def call(kernel, name, args, outs, smem=(), grid=None, in_specs=None, out_specs=None, scratch=()):
    in_specs = dict(in_specs or {})
    out_specs = dict(out_specs or {})
    for i in smem:
        in_specs[i] = pl.BlockSpec(memory_space=pltpu.SMEM)
    return pl.pallas_call(
        kernel,
        **({} if grid is None else {"grid": grid}),
        in_specs=[in_specs.get(i, whole(a.shape)) for i, a in enumerate(args)],
        out_specs=[out_specs.get(i, whole(s)) for i, (s, _) in enumerate(outs)],
        out_shape=[jax.ShapeDtypeStruct(s, d) for s, d in outs],
        scratch_shapes=scratch,
        compiler_params=params,
        cost_estimate=pl.CostEstimate(flops=TIMES[name] * RATE, bytes_accessed=1 << 20, transcendentals=0),
        name=name,
    )(*args)


def lanes_of(rows=1, count=128):
    return lax.broadcasted_iota(jnp.int32, (rows, count), 1)


def route_kernel(tensor_ref, routes_ref, cot_ref, expand_ref, seat_ref, placer_ref, turned_ref, sent_ref):
    routes = routes_ref[...]
    rows, width = cot_ref.shape
    lanes = lanes_of(rows)
    member = (routes[:, 0:1] == lanes) | (routes[:, 1:2] == lanes)
    earlier = lax.broadcasted_iota(jnp.int32, (rows, rows), 0) > lanes_of(rows, rows)
    count = dot(
        jnp.where(earlier, 1.0, 0.0).astype(bf16), jnp.where(member, 1.0, 0.0).astype(bf16)
    )
    offset = (tensor_ref[0] * SLOTS).astype(f32)
    place = jnp.where(member, count - offset, -1.0).astype(bf16)
    placer = jnp.where(dot(place, expand_ref[...]) == seat_ref[...], 1.0, 0.0).astype(bf16)
    placer_ref[...] = placer
    turned = placer.T
    turned_ref[...] = turned
    sent_ref[:, :width] = dot(turned, cot_ref[...]).astype(bf16)
    sums = (routes[:, 0:1] + routes[:, 1:2]).astype(f32)
    sent_ref[:, width:] = dot(turned, jnp.where(lanes == 0, sums, 0.0).astype(bf16)).astype(bf16)


def route(tensor, routes, cotangent, experts):
    rows, width = cotangent.shape
    seats = experts * SLOTS
    columns = np.arange(seats)
    expand = jnp.asarray(np.arange(128)[:, None] == columns[None, :] // SLOTS, bf16)
    seat = jnp.asarray((columns % SLOTS)[None], f32)
    return call(
        route_kernel,
        "route",
        (tensor[None], routes, cotangent, expand, seat),
        [((rows, seats), bf16), ((seats, rows), bf16), ((seats, width + 128), bf16)],
        smem=(0,),
    )


def project_kernel(x0_ref, x1_ref, gain_ref, wk_ref, wv_ref, cos_ref, sin_ref, *rest):
    wq_ref = rest[0] if len(rest) == 5 else None
    n_ref, k_ref, v_ref = rest[-4:-1] if wq_ref is not None else rest
    for chunk, x_ref in enumerate((x0_ref, x1_ref)):
        rows = x_ref.shape[0]
        at_rows = slice(chunk * rows, (chunk + 1) * rows)
        x = x_ref[...].astype(f32)
        normed = (x * rms_scale(x) * gain_ref[...]).astype(bf16)
        n_ref[at_rows, :] = normed
        cos, sin = cos_ref[at_rows, :], sin_ref[at_rows, :]
        key = dot(normed, wk_ref[...])
        for at in range(0, key.shape[1], PAIR):
            lanes = slice(at, at + PAIR)
            k_ref[at_rows, lanes] = turn(key[:, lanes], cos, sin).astype(bf16)
        v_ref[at_rows, :] = dot(normed, wv_ref[...]).astype(bf16)
        if chunk == 0 and wq_ref is not None:
            q_ref = rest[-1]
            query = dot(normed, wq_ref[...])
            for at in range(0, query.shape[1], PAIR):
                lanes = slice(at, at + PAIR)
                turned = turn(query[:, lanes], cos, sin).astype(bf16)
                q_ref[:, lanes] = turned * (HEAD_DIM**-0.5)


def project(first, second, gain, w_key, w_value, cos, sin, w_query=None):
    rows, width = first.shape
    wide = w_key.shape[1]
    outs = [((2 * rows, width), bf16), ((2 * rows, wide), bf16), ((2 * rows, wide), bf16)]
    args = (first, second, gain, w_key, w_value, cos, sin)
    if w_query is not None:
        args += (w_query,)
        outs.append(((rows, wide), bf16))
    return call(project_kernel, "project", args, outs)


def attend_kernel(hide_ref, q_ref, ka_ref, va_ref, kb_ref, vb_ref, wo_ref, o_ref, lse_ref, part_ref, acc_ref):
    lanes = lanes_of()
    span = 2 * BLOCK
    step = pl.program_id(0)
    for half in range(2):
        rows = slice(half * BLOCK, (half + 1) * BLOCK)
        q = q_ref[rows, :]
        outs, logs = [], []
        for head in range(2):
            query = jnp.where(lanes // HEAD_DIM == head, q, jnp.zeros_like(q))
            spans = [(ka_ref, va_ref, 0, BLOCK * (half + 1), 0.0), (ka_ref, va_ref, span, span, hide_ref[1])]
            spans += [(kb_ref, vb_ref, 0, span, hide_ref[2]), (kb_ref, vb_ref, span, span, hide_ref[3])]
            scores = [dot_nt(query, k[a : a + n, :]) for k, _, a, n, _ in spans]
            tops = [jnp.max(s, axis=1, keepdims=True) - x[4] for s, x in zip(scores, spans)]
            top = functools.reduce(jnp.maximum, tops)
            total, acc = 0.0, 0.0
            for s, (_, v, a, n, off) in zip(scores, spans):
                p = jnp.exp(s - (top + off))
                total = total + jnp.sum(p, axis=1, keepdims=True)
                acc = acc + dot(p.astype(bf16), v[a : a + n, :])
            outs.append(acc / total)
            logs.append(top + jnp.log(total))
        mixed = jnp.where(lanes < HEAD_DIM, outs[0], outs[1]).astype(bf16)
        o_ref[rows, :] = mixed
        lse_ref[rows, :] = jnp.where(lanes < HEAD_DIM, logs[0], logs[1])
    part = dot(o_ref[...], wo_ref[...])

    @pl.when(step == 0)
    def _():
        acc_ref[...] = part

    @pl.when(step > 0)
    def _():
        acc_ref[...] += part

    @pl.when(step == pl.num_programs(0) - 1)
    def _():
        part_ref[...] = acc_ref[...].astype(bf16)


def attend(hide, q, ka, va, kb, vb, w_output):
    rows, keys = q.shape[0], ka.shape[0]
    width = w_output.shape[1]
    of_q = pl.BlockSpec((rows, PAIR), lambda p: (0, p))
    of_k = pl.BlockSpec((keys, PAIR), lambda p: (0, p))
    return call(
        attend_kernel,
        "attend",
        (hide, q, ka, va, kb, vb, w_output),
        [(q.shape, bf16), (q.shape, f32), ((rows, width), bf16)],
        smem=(0,),
        grid=(q.shape[1] // PAIR,),
        in_specs={1: of_q, 2: of_k, 3: of_k, 4: of_k, 5: of_k, 6: pl.BlockSpec((PAIR, width), lambda p: (p, 0))},
        out_specs={0: of_q, 1: of_q},
        scratch=[pltpu.VMEM((rows, width), f32)],
    )


def attend_back_kernel(
    hide_ref, q_ref, ka_ref, va_ref, kb_ref, vb_ref, o_ref, lse_ref, g_ref, ca_ref, sa_ref, cb_ref, sb_ref,
    dq_ref, dka_ref, dva_ref, dkb_ref, dvb_ref,
):
    lanes = lanes_of()
    q, g = q_ref[...], g_ref[...]
    rows = q.shape[0]
    deltas = (g.astype(f32) * o_ref[...].astype(f32)).T
    logs = lse_ref[...].T
    dq = 0.0
    near = (ka_ref, va_ref, ca_ref, sa_ref, dka_ref, dva_ref)
    far = (kb_ref, vb_ref, cb_ref, sb_ref, dkb_ref, dvb_ref)
    for block in range(8):
        k_ref, v_ref, cos_ref, sin_ref, dk_ref, dv_ref = near if block < 4 else far
        off = 0.0 if block < 2 else hide_ref[block // 2]
        first = BLOCK if block == 1 else 0
        keys = slice((block % 4) * BLOCK, (block % 4 + 1) * BLOCK)
        k, v = k_ref[keys, :], v_ref[keys, :]
        dk, dv = 0.0, 0.0
        for head in range(2):
            mine = lanes // HEAD_DIM == head
            low = head * HEAD_DIM
            query = jnp.where(mine, q[first:, :], jnp.zeros_like(q[first:, :]))
            grads = jnp.where(mine, g[first:, :], jnp.zeros_like(g[first:, :]))
            key = jnp.where(mine, k, jnp.zeros_like(k))
            log = logs[low : low + 1, first:] + off
            delta = jnp.sum(deltas[low : low + HEAD_DIM, first:], axis=0, keepdims=True)
            p = jnp.exp(dot_nt(k, query) - log)
            ds = (p * (dot_nt(v, grads) - delta)).astype(bf16)
            dv = dv + dot(p.astype(bf16), grads)
            dk = dk + dot(ds, query)
            part = dot_tn(ds, key)
            if first:
                part = jnp.concatenate([jnp.zeros((first, PAIR), f32), part], axis=0)
            dq = dq + part
        dv_ref[keys, :] = dv.astype(bf16)
        dk_ref[keys, :] = turn(dk, cos_ref[keys, :], -sin_ref[keys, :]).astype(bf16)
    dq = dq * (HEAD_DIM**-0.5)
    dq_ref[...] = turn(dq, ca_ref[:rows, :], -sa_ref[:rows, :]).astype(bf16)


def attend_back(hide, q, ka, va, kb, vb, o, lse, g, ca, sa, cb, sb):
    rows, keys = q.shape[0], ka.shape[0]
    of_q = pl.BlockSpec((rows, PAIR), lambda p: (0, p))
    of_k = pl.BlockSpec((keys, PAIR), lambda p: (0, p))
    return call(
        attend_back_kernel,
        "attend_back",
        (hide, q, ka, va, kb, vb, o, lse, g, ca, sa, cb, sb),
        [(q.shape, bf16)] + [(ka.shape, bf16)] * 4,
        smem=(0,),
        grid=(q.shape[1] // PAIR,),
        in_specs={1: of_q, 2: of_k, 3: of_k, 4: of_k, 5: of_k, 6: of_q, 7: of_q, 8: of_q},
        out_specs={0: of_q, 1: of_k, 2: of_k, 3: of_k, 4: of_k},
    )


def turn_rows_kernel(a_ref, b_ref, ta_ref, tb_ref):
    ta_ref[...] = a_ref[...].T
    tb_ref[...] = b_ref[...].T


def half_sum_kernel(kept_ref, taken_ref, out_ref):
    out_ref[...] = kept_ref[...] + taken_ref[...]


def second_kernel(x_ref, mine_ref, theirs_ref, gain_ref, turned_ref, cot_ref, middle_ref, n_ref, sent_ref):
    middle = x_ref[...].astype(f32) + (mine_ref[...].astype(f32) + theirs_ref[...].astype(f32))
    middle_ref[...] = middle
    normed = (middle * rms_scale(middle) * gain_ref[...]).astype(bf16)
    n_ref[...] = normed
    width = normed.shape[1]
    sent_ref[:, :width] = dot(turned_ref[...], normed).astype(bf16)
    sent_ref[:, width:] = cot_ref[...]


def swish(gate, up, grads):
    sigmoid = jax.nn.sigmoid(gate)
    unit = gate * sigmoid
    slope = sigmoid + unit * (1.0 - sigmoid)
    return (unit * up).astype(bf16), (grads * up * slope).astype(bf16), (grads * unit).astype(bf16)


def shared_kernel(
    n_ref, cot_ref, sg_ref, su_ref, sd_ref, router_ref, routes_ref, h_ref, gg_ref, gu_ref, back_ref, out_ref, share_ref
):
    normed, cot = n_ref[...], cot_ref[...]
    sg, su, sd = sg_ref[...], su_ref[...], sd_ref[...]
    hidden, gg, gu = swish(dot(normed, sg), dot(normed, su), dot_nt(cot, sd))
    h_ref[...], gg_ref[...], gu_ref[...] = hidden, gg, gu
    back = dot_nt(gg, sg) + dot_nt(gu, su)
    out = dot(hidden, sd)

    @pl.when(pl.program_id(0) == 0)
    def _():
        back_ref[...] = back
        out_ref[...] = out
        logits = dot(normed, router_ref[...])
        routes = routes_ref[...]
        lanes = lanes_of()
        first, second = lanes == routes[:, 0:1], lanes == routes[:, 1:2]
        one = jnp.sum(jnp.where(first, logits, 0.0), axis=1, keepdims=True)
        two = jnp.sum(jnp.where(second, logits, 0.0), axis=1, keepdims=True)
        top = jnp.maximum(one, two)
        one, two = jnp.exp(one - top), jnp.exp(two - top)
        share_ref[...] = (jnp.where(first, one, 0.0) + jnp.where(second, two, 0.0)) / (one + two)

    @pl.when(pl.program_id(0) > 0)
    def _():
        back_ref[...] += back
        out_ref[...] += out


def shared(normed, cot, shared_gate, shared_up, shared_down, router, routes):
    rows, width = normed.shape
    hidden = shared_gate.shape[1]
    block = 512
    columns = pl.BlockSpec((width, block), lambda k: (0, k))
    of_hidden = pl.BlockSpec((rows, block), lambda k: (0, k))
    return call(
        shared_kernel,
        "shared",
        (normed, cot, shared_gate, shared_up, shared_down, router, routes),
        [((rows, hidden), bf16)] * 3 + [((rows, width), f32)] * 2 + [((rows, 128), f32)],
        grid=(hidden // block,),
        in_specs={2: columns, 3: columns, 4: pl.BlockSpec((block, width), lambda k: (k, 0))},
        out_specs={0: of_hidden, 1: of_hidden, 2: of_hidden},
    )


def store_half(given_ref, kept_ref, at, value):
    value = value.astype(bf16)

    @pl.when(pl.program_id(0) == 0)
    def _():
        given_ref[:, at : at + value.shape[1]] = value

    @pl.when(pl.program_id(0) == 1)
    def _():
        kept_ref[:, at : at + value.shape[1]] = value


def shared_weights_kernel(core_ref, n_ref, cot_ref, gg_ref, gu_ref, h_ref, given_ref, kept_ref):
    part = h_ref.shape[1]
    turned = n_ref[...].T
    store_half(given_ref, kept_ref, 0, dot(turned, gg_ref[...]))
    store_half(given_ref, kept_ref, part, dot(turned, gu_ref[...]))
    store_half(given_ref, kept_ref, 2 * part, dot(cot_ref[...].T, h_ref[...]))


def half_call(kernel, name, core, halved, full, columns, by_rows=()):
    half = halved[0].shape[1] // 2
    specs = [pl.BlockSpec((a.shape[0], half), lambda s, c: (0, jnp.where(s == 0, 1 - c[0], c[0]))) for a in halved]
    specs += [
        pl.BlockSpec((half, a.shape[1]), lambda s, c: (jnp.where(s == 0, 1 - c[0], c[0]), 0))
        for a in by_rows
    ]
    specs += [pl.BlockSpec(a.shape, lambda s, c: (0, 0)) for a in full]
    return pl.pallas_call(
        kernel,
        grid_spec=pltpu.PrefetchScalarGridSpec(
            num_scalar_prefetch=1,
            grid=(2,),
            in_specs=specs,
            out_specs=[pl.BlockSpec((half, c), lambda s, c: (0, 0)) for c in columns for _ in range(2)],
        ),
        out_shape=[jax.ShapeDtypeStruct((half, c), bf16) for c in columns for _ in range(2)],
        compiler_params=params,
        cost_estimate=pl.CostEstimate(flops=TIMES[name] * RATE, bytes_accessed=1 << 20, transcendentals=0),
        name=name,
    )(core[None], *halved, *by_rows, *full)


def late_weights_kernel(
    core_ref, n2_ref, low_ref, gain_ref, scale_ref, ta_ref, tb_ref, wq_ref, wk_ref, wv_ref,
    dq_ref, dka_ref, dkb_ref, dva_ref, dvb_ref, lg_ref, o_ref, given_ref, kept_ref, small_given_ref, small_kept_ref, *, experts
):
    def column(row_ref):
        return jnp.broadcast_to(row_ref[...], (128, row_ref.shape[1])).T

    wide = dq_ref.shape[1]
    rows = dq_ref.shape[0]
    ta, tb = ta_ref[...], tb_ref[...]
    grad_q = dot(ta[:, :rows], dq_ref[...])
    grad_k = dot(ta, dka_ref[...]) + dot(tb, dkb_ref[...])
    grad_v = dot(ta, dva_ref[...]) + dot(tb, dvb_ref[...])
    for i, value in enumerate((grad_q, grad_k, grad_v, dot(low_ref[...].T, o_ref[...]))):
        store_half(given_ref, kept_ref, i * wide, value)
    small = dot(n2_ref[...].T, lg_ref[...])
    terms = grad_q * wq_ref[...].astype(f32) + grad_k * wk_ref[...].astype(f32) + grad_v * wv_ref[...].astype(f32)
    gain_one = jnp.sum(terms, axis=1, keepdims=True) / column(scale_ref)
    lanes = lanes_of()
    small = jnp.where(lanes == experts, 0.5 * column(gain_ref), small)
    store_half(small_given_ref, small_kept_ref, 0, jnp.where(lanes == experts + 1, gain_one, small))


def expert_kernel(
    here_ref, sent_ref, router_ref, *refs, experts, shards
):
    w_refs = refs[:shards]
    hidden_ref, grads_ref, back_ref, scaled_ref, out_ref, share_ref, acc_ref, dots_ref, slots_ref, sems = refs[shards:]
    step = pl.program_id(0)
    width = router_ref.shape[0]

    def fetch(i, slot):
        return pltpu.make_async_copy(w_refs[i], slots_ref.at[slot], sems.at[slot])

    @pl.when(step == 0)
    def _():
        fetch(0, 0).start()

    for i in range(1, shards):
        @pl.when(step == i - 1)
        def _(i=i):
            fetch(i, i % 2).start()

    slot = lax.rem(step, 2)
    fetch(0, slot).wait()
    w = slots_ref.at[slot]
    part = w.shape[1] // 3
    half = sent_ref.shape[0] // 2
    w_in, w_down = w[:, : 2 * part], w[:, 2 * part :]
    for at in (0, half):
        these = slice(at, at + half)
        rows, cot = sent_ref[these, :width], sent_ref[these, width : 2 * width]
        both = dot(rows, w_in)
        hidden_grads = dot(cot, w_down)
        hidden, gg, gu = swish(both[:, :part], both[:, part:], hidden_grads)
        hidden_ref[0, these, :] = hidden
        grads_ref[0, these, :part] = gg
        grads_ref[0, these, part:] = gu
        product = hidden.astype(f32) * hidden_grads
        product = functools.reduce(jnp.add, [product[:, a : a + 128] for a in range(0, part, 128)])
        back = dot_nt(gg, w[:, :part]) + dot_nt(gu, w[:, part : 2 * part])
        acc_ref[these, :] = jnp.where(step == 0, 0.0, acc_ref[these, :]) + back
        dots_ref[these, :] = jnp.where(step == 0, 0.0, dots_ref[these, :]) + product

    @pl.when(step == pl.num_programs(0) - 1)
    def _():
        rows, cot = sent_ref[:, :width], sent_ref[:, width : 2 * width]
        here = here_ref[0]
        lanes = lanes_of()
        logits = dot(rows, router_ref[...])
        other = sent_ref[:, 2 * width :].astype(f32)[:, :1].astype(jnp.int32) - here
        own_logit = jnp.sum(jnp.where(lanes == here, logits, 0.0), axis=1, keepdims=True)
        other_logit = jnp.sum(jnp.where(lanes == other, logits, 0.0), axis=1, keepdims=True)
        top = jnp.maximum(own_logit, other_logit)
        own = jnp.exp(own_logit - top)
        share = own / (own + jnp.exp(other_logit - top))
        share_ref[...] = jnp.broadcast_to(share, share_ref.shape)
        scaled_ref[...] = (share * rows.astype(f32)).astype(bf16)
        out_ref[...] = (share * cot.astype(f32)).astype(bf16)
        back_ref[:, :width] = (share * acc_ref[...]).astype(bf16)
        dots = jnp.sum(dots_ref[...], axis=1, keepdims=True)
        high = dots.astype(bf16).astype(f32)
        back_ref[:, width:] = (
            jnp.where(lanes == here, high, 0.0)
            + jnp.where(lanes == experts + here, dots - high, 0.0)
        ).astype(bf16)


def expert_rows(here, sent, router, weights, experts):
    rows, width = sent.shape[0], router.shape[0]
    shards, packed = len(weights), weights[0].shape[1]
    part = packed // 3
    return call(
        functools.partial(expert_kernel, experts=experts, shards=shards),
        "expert_rows",
        (here[None], sent, router, *weights),
        [
            ((shards, rows, part), bf16),
            ((shards, rows, 2 * part), bf16),
            ((rows, width + 128), bf16),
            ((rows, width), bf16),
            ((rows, width), bf16),
            ((rows, 128), f32),
        ],
        smem=(0,),
        grid=(shards,),
        in_specs={3 + i: pl.BlockSpec(memory_space=pl.ANY) for i in range(shards)},
        out_specs={
            0: pl.BlockSpec((1, rows, part), lambda k: (k, 0, 0)),
            1: pl.BlockSpec((1, rows, 2 * part), lambda k: (k, 0, 0)),
        },
        scratch=[
            pltpu.VMEM((rows, width), f32),
            pltpu.VMEM((rows, 128), f32),
            pltpu.VMEM((2, width, packed), bf16),
            pltpu.SemaphoreType.DMA((2,)),
        ],
    )


def expert_given_kernel(scaled_ref, out_ref, hidden_ref, grads_ref, *refs, shards):
    w_refs = refs[:shards]
    d_ref, acc_ref, st_ref, ot_ref, slots_ref, sems = refs[shards:]
    step = pl.program_id(0)

    @pl.when(step == 0)
    def _():
        st_ref[...] = scaled_ref[...].T
        ot_ref[...] = out_ref[...].T

    expert_step(step, st_ref, ot_ref, hidden_ref, grads_ref, w_refs, d_ref, slots_ref, sems, acc_ref, None)


def expert_kept_kernel(st_ref, ot_ref, share_ref, first_ref, hidden_ref, grads_ref, *refs, shards):
    w_refs = refs[:shards]
    d_ref, picked_ref, acc_ref, slots_ref, sems = refs[shards:]
    step = pl.program_id(0)
    expert_step(step, st_ref, ot_ref, hidden_ref, grads_ref, w_refs, d_ref, slots_ref, sems, acc_ref, first_ref)

    @pl.when(step == pl.num_programs(0) - 1)
    def _():
        picked_ref[...] = (share_ref[:, :1] * acc_ref[...]).astype(bf16)


def expert_step(step, st_ref, ot_ref, hidden_ref, grads_ref, w_refs, d_ref, slots_ref, sems, acc_ref, first_ref):
    part = hidden_ref.shape[2]

    def fetch(i, slot):
        return pltpu.make_async_copy(w_refs[i].at[:, 2 * part :], slots_ref.at[slot], sems.at[slot])

    @pl.when(step == 0)
    def _():
        fetch(0, 0).start()
        acc_ref[...] = jnp.zeros_like(acc_ref) if first_ref is None else first_ref[...]

    for i in range(1, len(w_refs)):
        @pl.when(step == i - 1)
        def _(i=i):
            fetch(i, i % 2).start()

    slot = lax.rem(step, 2)
    fetch(0, slot).wait()
    d_ref[0, :, : 2 * part] = dot(st_ref[...], grads_ref[0]).astype(bf16)
    d_ref[0, :, 2 * part :] = dot(ot_ref[...], hidden_ref[0]).astype(bf16)
    acc_ref[...] += dot_nt(hidden_ref[0], slots_ref[slot])


def expert_half(kernel, name, args, hidden, grads, weights, at, extra):
    shards = len(weights)
    _, rows, part = hidden.shape
    width = weights[0].shape[0]
    count = len(args)
    return call(
        functools.partial(kernel, shards=shards),
        name,
        (*args, hidden, grads, *weights),
        [((shards, width, 3 * part), bf16), *extra],
        grid=(shards,),
        in_specs={
            count: pl.BlockSpec((1, rows, part), lambda k: (k + at, 0, 0)),
            count + 1: pl.BlockSpec((1, rows, 2 * part), lambda k: (k + at, 0, 0)),
            **{count + 2 + i: pl.BlockSpec(memory_space=pl.ANY) for i in range(shards)},
        },
        out_specs={0: pl.BlockSpec((1, width, 3 * part), lambda k: (k, 0, 0))},
        scratch=([pltpu.VMEM((rows, width), f32)] if at else [])
        + [pltpu.VMEM((2, width, part), bf16), pltpu.SemaphoreType.DMA((2,))],
    )


def expert_sum_kernel(kept_ref, taken_ref, high_ref, tensor_ref, keep_high_ref, keep_tensor_ref):
    shard = pl.program_id(0)
    half = high_ref.shape[1]
    total = kept_ref[0] + taken_ref[0]
    for ref, at, here in (
        (keep_high_ref, 0, shard < 2),
        (high_ref, 0, shard >= 2),
        (keep_tensor_ref, half, shard % 2 == 0),
        (tensor_ref, half, shard % 2 == 1),
    ):
        @pl.when(here)
        def _(ref=ref, at=at):
            ref[0] = total[at : at + ref.shape[1]]


def expert_sums_kernel(kh_ref, fh_ref, kt_ref, ft_ref, to_t_ref, to_y_ref, kept_u_ref, kept_l_ref):
    to_t_ref[...] = kh_ref[1] + fh_ref[1]
    to_y_ref[...] = kt_ref[1] + ft_ref[1]
    kept_u_ref[...] = kh_ref[0] + fh_ref[0]
    kept_l_ref[...] = kt_ref[0] + ft_ref[0]


def expert_out_kernel(ku_ref, fu_ref, kl_ref, fl_ref, gate_ref, up_ref, down_ref):
    half = ku_ref.shape[0]
    part = gate_ref.shape[2]
    for at, (kept_ref, from_ref) in ((0, (ku_ref, fu_ref)), (half, (kl_ref, fl_ref))):
        total = kept_ref[...].astype(f32) + from_ref[...].astype(f32)
        rows = slice(at, at + kept_ref.shape[0])
        gate_ref[0, rows, :] = total[:, :part]
        up_ref[0, rows, :] = total[:, part : 2 * part]
        down_ref[0, :, rows] = total[:, 2 * part :].T


def combine_kernel(placer_ref, back_ref, share_ref, router_ref, shared_ref, part_ref, lg_ref, *, experts):
    width = shared_ref.shape[1]
    placer = placer_ref[...]
    lanes = lanes_of()
    dots = dot(placer, back_ref[:, width:])
    dots = jnp.where(lanes < experts, dots + pltpu.roll(dots, 128 - experts, 1), 0.0)
    share = share_ref[...]
    grads = (share * (dots - jnp.sum(share * dots, axis=1, keepdims=True))).astype(bf16)
    lg_ref[...] = grads
    total = shared_ref[...] + dot_nt(grads, router_ref[...]) + dot(placer, back_ref[:, :width])
    part_ref[...] = total.astype(bf16)


def back_two_kernel(middle_ref, mine_ref, theirs_ref, cot_ref, gain_ref, wo_ref, grads_ref, low_ref, mixed_ref, sum_ref):
    middle = middle_ref[...]
    scale = rms_scale(middle)
    upstream = mine_ref[...].astype(f32) + theirs_ref[...].astype(f32)
    sum_ref[...] = jnp.sum(upstream * (middle * scale), axis=0, keepdims=True)
    grads = cot_ref[...].astype(f32) + norm_back(middle, scale, gain_ref[...], upstream)
    grads_ref[...] = grads
    low = grads.astype(bf16)
    low_ref[...] = low
    mixed_ref[...] = dot_nt(low, wo_ref[...]).astype(bf16)


def normed_back_kernel(dq_ref, dka_ref, dva_ref, dkb_ref, dvb_ref, wq_ref, wk_ref, wv_ref, core_ref, far_ref, y_ref, own_ref):
    rows = dq_ref.shape[0]
    wk, wv = wk_ref[...], wv_ref[...]

    def back(dk_ref, dv_ref, chunk):
        these = slice(chunk * rows, (chunk + 1) * rows)
        return dot_nt(dk_ref[these, :], wk) + dot_nt(dv_ref[these, :], wv)

    far_ref[...] = back(dkb_ref, dvb_ref, 1).astype(bf16)
    core_ref[...] = back(dka_ref, dva_ref, 1).astype(bf16)
    y_ref[...] = back(dkb_ref, dvb_ref, 0)
    own_ref[...] = back(dka_ref, dva_ref, 0) + dot_nt(dq_ref[...], wq_ref[...])


def first_kernel(x_ref, mine_ref, theirs_ref, grads_ref, gain_ref, out_ref):
    x = x_ref[...].astype(f32)
    upstream = mine_ref[...].astype(f32) + theirs_ref[...].astype(f32)
    out_ref[...] = grads_ref[...] + norm_back(x, rms_scale(x), gain_ref[...], upstream)


def spread(part):
    copies = jnp.broadcast_to(part[None], (16,) + part.shape)
    return exchange(copies, PLANE).reshape(-1, part.shape[1])


def late_out_kernel(core_ref, mine_ref, theirs_ref, q_ref, k_ref, v_ref, o_ref, small_ref):
    half, wide = mine_ref.shape[0], q_ref.shape[1]
    for at, ref in ((0, mine_ref), (1, theirs_ref)):
        place = core_ref[0] if at == 0 else 1 - core_ref[0]
        these = pl.ds(pl.multiple_of(place * half, 128), half)
        for i, out_ref in enumerate((q_ref, k_ref, v_ref)):
            out_ref[these, :] = ref[:, i * wide : (i + 1) * wide].astype(f32)
        o_ref[:, these] = ref[:, 3 * wide : 4 * wide].astype(f32).T
        small_ref[these, :] = ref[:, 4 * wide :].astype(f32)


def early_out_kernel(core_ref, mine_ref, theirs_ref, gate_ref, up_ref, down_ref):
    half, wide = mine_ref.shape[0], gate_ref.shape[1]
    for at, ref in ((0, mine_ref), (1, theirs_ref)):
        place = core_ref[0] if at == 0 else 1 - core_ref[0]
        these = pl.ds(pl.multiple_of(place * half, 128), half)
        for i, out_ref in enumerate((gate_ref, up_ref)):
            out_ref[these, :] = ref[:, i * wide : (i + 1) * wide].astype(f32)
        down_ref[:, these] = ref[:, 2 * wide :].astype(f32).T


def local(
    tokens,
    routes,
    gain_one,
    w_query,
    w_key,
    w_value,
    w_output,
    gain_two,
    w_router,
    shared_gate,
    shared_up,
    shared_down,
    expert_gate,
    expert_up,
    expert_down,
    cotangent,
):
    rows, width = tokens.shape
    wide = w_query.shape[1]
    experts = w_router.shape[1]
    seats = experts * SLOTS
    part = expert_gate.shape[2]
    shared_part = shared_gate.shape[1]
    tensor = lax.axis_index("t")
    core = lax.axis_index("c")
    high = lax.axis_index("yl")
    expert_here = lax.axis_index(ROUTE)
    router = jnp.pad(w_router, ((0, 0), (0, 128 - experts)))
    of_rows = ((rows, width), f32)
    of_rows_low = ((rows, width), bf16)

    tokens_y = swap(tokens, "yl")
    tokens_c = swap(tokens, "c")
    hide = jnp.stack([core < 0, core == 0, high == 0, high == 0])
    hide = jnp.where(hide, 1e30, 0.0).astype(f32)

    frequency = rope_base ** (-np.arange(HEAD_DIM // 2) * 2.0 / HEAD_DIM)
    frequency = np.tile(frequency, PAIR // (HEAD_DIM // 2))
    inner = np.arange(rows)[:, None] * frequency[None, :]
    starts = jnp.stack(
        [((high ^ my) * 2 + (core ^ mc)) * rows for my, mc in ((0, 0), (0, 1), (1, 0), (1, 1))]
    )
    outer = starts.astype(f32)[:, None, None] * frequency.astype(np.float32)[None, None, :]
    cos_in, sin_in = np.cos(inner).astype(np.float32), np.sin(inner).astype(np.float32)
    cos_out, sin_out = jnp.cos(outer), jnp.sin(outer)
    cosine = (cos_out * cos_in - sin_out * sin_in).reshape(2, 2 * rows, PAIR)
    sine = (sin_out * cos_in + cos_out * sin_in).reshape(2, 2 * rows, PAIR)

    own = jnp.concatenate([expert_gate[0], expert_up[0], expert_down[0].T], axis=1)
    placer, placer_turned, sent_cot = route(tensor, routes, cotangent, experts)
    normed_a, keys_a, values_a, query = project(
        tokens, tokens_c, gain_one[None], w_key, w_value, cosine[0], sine[0], w_query
    )
    tokens_y, keys_a, placer, placer_turned, sent_cot, own_later = lax.optimization_barrier(
        (tokens_y, keys_a, placer, placer_turned, sent_cot, own)
    )
    tokens_yc = swap(tokens_y, "c")
    own_t, own_y = swap(own, "t"), swap(own_later, "yl")
    normed_b, keys_b, values_b = project(
        tokens_y, tokens_yc, gain_one[None], w_key, w_value, cosine[1], sine[1]
    )
    mixed_heads, logs, attended = attend(
        hide, query, keys_a, values_a, keys_b, values_b, w_output
    )
    attended, own_t, own_later = lax.optimization_barrier((attended, own_t, own_later))

    own_ty = swap(own_t, "yl")
    turned_a, turned_b = call(
        turn_rows_kernel,
        "turn_rows",
        (after(normed_a, attended), normed_b),
        [((width, 2 * rows), bf16)] * 2,
    )
    theirs, own_y, turned_a, turned_b = lax.optimization_barrier(
        (swap(attended, "t"), own_y, turned_a, turned_b)
    )
    middle, normed_two, sent_rows = call(
        second_kernel,
        "second",
        (tokens, attended, theirs, gain_two[None], placer_turned, sent_cot),
        [of_rows, of_rows_low, ((seats, 2 * width + 128), bf16)],
    )

    arrived = exchange(sent_rows.reshape(experts, SLOTS, -1), ROUTE).reshape(seats, -1)
    hidden_shared, shared_gg, shared_gu, shared_back, shared_out, share = shared(
        normed_two, cotangent, shared_gate, shared_up, shared_down, router, routes
    )
    early_given, early_kept = half_call(
        shared_weights_kernel,
        "shared_weights",
        core,
        (normed_two, cotangent),
        (shared_gg, shared_gu, hidden_shared),
        (3 * shared_part,),
    )
    weights = [own_later, own_t, own_y, own_ty]
    weights = [swap(w, "c") for w in weights] + weights
    arrived, early_given, early_kept, shared_back, shared_out, share, *weights = (
        lax.optimization_barrier(
            (arrived, early_given, early_kept, shared_back, shared_out, share, *weights)
        )
    )
    early_taken = swap(early_given, "c")
    hidden_expert, expert_grads, back, scaled_rows, out_grads, row_share = expert_rows(
        expert_here, arrived, router, weights, experts
    )
    given, first_out, scaled_turned, out_turned = expert_half(
        expert_given_kernel,
        "expert_given",
        (scaled_rows, out_grads),
        hidden_expert,
        expert_grads,
        weights[:4],
        0,
        [((seats, width), f32), ((width, seats), bf16), ((width, seats), bf16)],
    )
    (early,) = call(
        half_sum_kernel, "half_sum", (after(early_kept, back), early_taken), [(early_kept.shape, bf16)]
    )
    back = exchange(back.reshape(experts, SLOTS, -1), ROUTE).reshape(seats, -1)
    back, given, first_out, scaled_turned, out_turned, early = lax.optimization_barrier(
        (back, given, first_out, scaled_turned, out_turned, early)
    )

    mine, logits_grads = call(
        functools.partial(combine_kernel, experts=experts),
        "combine",
        (placer, back, share, router, shared_back),
        [of_rows_low, ((rows, 128), bf16)],
    )
    kept, picked = expert_half(
        expert_kept_kernel,
        "expert_kept",
        (after(scaled_turned, mine), out_turned, row_share, first_out),
        hidden_expert,
        expert_grads,
        weights[4:],
        4,
        [((seats, width), bf16)],
    )
    of_shard = pl.BlockSpec((1, width, 3 * part), lambda k: (k, 0, 0))
    upper, lower = (2 * width // 3, 3 * part), (width // 3, 3 * part)
    to_high, to_tensor, keep_high, keep_tensor = call(
        expert_sum_kernel,
        "expert_sum",
        (kept, swap(given, "c")),
        [((2, *upper), bf16), ((2, *lower), bf16)] * 2,
        grid=(4,),
        in_specs={0: of_shard, 1: of_shard},
        out_specs={
            0: pl.BlockSpec((1, *upper), lambda k: (jnp.maximum(k - 2, 0), 0, 0)),
            1: pl.BlockSpec((1, *lower), lambda k: (k // 2, 0, 0)),
            2: pl.BlockSpec((1, *upper), lambda k: (jnp.minimum(k, 1), 0, 0)),
            3: pl.BlockSpec((1, *lower), lambda k: (k // 2, 0, 0)),
        },
    )
    theirs, to_high, to_tensor, keep_high, keep_tensor, picked = lax.optimization_barrier(
        (swap(mine, "t"), to_high, to_tensor, keep_high, keep_tensor, picked)
    )
    middle_grads, middle_low, mixed_grads, gain_sum = call(
        back_two_kernel,
        "back_two",
        (middle, mine, theirs, cotangent, gain_two[None], w_output),
        [of_rows, of_rows_low, ((rows, wide), bf16), ((1, width), f32)],
    )

    dq, dka, dva, dkb, dvb = attend_back(
        hide, query, keys_a, values_a, keys_b, values_b, mixed_heads, logs, mixed_grads,
        cosine[0], sine[0], cosine[1], sine[1],
    )
    picked = exchange(picked.reshape(experts, SLOTS, width), ROUTE).reshape(seats, width)
    from_high, from_tensor = swap(to_high, "yl"), swap(to_tensor, "t")
    early = lax.psum_scatter(early, "x", scatter_dimension=0, tiled=True)
    early = lax.psum_scatter(early, ("yh", "yl"), scatter_dimension=0, tiled=True)
    dq, dka, dva, dkb, dvb, picked, from_high, from_tensor, early = lax.optimization_barrier(
        (dq, dka, dva, dkb, dvb, picked, from_high, from_tensor, early)
    )
    early_zh = swap(early, "zh")
    late_given, late_kept, small_given, small_kept = half_call(
        functools.partial(late_weights_kernel, experts=experts),
        "late_weights",
        core,
        (normed_two, middle_low, gain_sum, gain_one[None]),
        (dq, dka, dkb, dva, dvb, logits_grads, mixed_heads),
        (4 * wide, 128),
        (turned_a, turned_b, w_query, w_key, w_value),
    )

    small = swap(small_kept, "t").astype(f32) + lax.ppermute(
        small_given, ("c", "t"), [(0, 3), (3, 0), (1, 2), (2, 1)]
    ).astype(f32)
    small = small_kept.astype(f32) + swap(small_given, "c").astype(f32) + small
    sums = call(
        expert_sums_kernel,
        "expert_sums",
        (keep_high, after(from_high, late_given), keep_tensor, from_tensor),
        [(upper, bf16), (lower, bf16)] * 2,
    )
    early = early.astype(f32) + after(early_zh, late_given).astype(f32)
    early = lax.all_gather(early.astype(bf16), PLANE, axis=0, tiled=True)
    late_taken, small, next_t, next_y, kept_u, kept_l = lax.optimization_barrier(
        (swap(late_given, "c"), small, *sums)
    )
    total = late_kept.astype(f32) + late_taken.astype(f32)
    total = jnp.concatenate([total, small], axis=1).astype(bf16)
    parts = exchange(total.reshape(16, -1, total.shape[1]), PLANE)
    parts, from_next_t = lax.optimization_barrier((parts, swap(next_t, "t")))

    to_core, to_far, to_y, own_part = call(
        normed_back_kernel,
        "normed_back",
        (after(dq, total), dka, dva, dkb, dvb, w_query, w_key, w_value),
        [of_rows_low, of_rows_low, of_rows, of_rows],
    )
    from_far = swap(to_far, "c").astype(f32)
    own_part = own_part + swap(to_core, "c").astype(f32)
    from_y = swap((to_y + from_far).astype(bf16), "yl")
    block_part = (shared_out + dot(after(placer, total), picked)).astype(bf16)
    part_sum = jnp.sum(parts.astype(f32), axis=0).astype(bf16)
    part_zh, from_block, own_part = lax.optimization_barrier(
        (swap(part_sum, "zh"), swap(block_part, "t"), own_part)
    )
    total = (part_sum.astype(f32) + part_zh.astype(f32)).astype(bf16)
    own_part = (own_part + after(from_y, total).astype(f32)).astype(bf16)
    block_out = (middle + block_part.astype(f32) + after(from_block, own_part).astype(f32)).astype(bf16)
    hidden = (width, shared_part)
    early = after(early, own_part)
    shared_grads = call(
        early_out_kernel,
        "early_out",
        (core[None], early, swap(early, "c")),
        [(hidden, f32), (hidden, f32), (hidden[::-1], f32)],
        smem=(0,),
    )
    from_next_y = swap(after(next_y, own_part), "yl")
    total, from_t, block_out, *shared_grads = lax.optimization_barrier(
        (spread(total), swap(own_part, "t"), block_out, *shared_grads)
    )
    grad_shared_gate, grad_shared_up, grad_shared_down = shared_grads
    (grad_tokens,) = call(
        first_kernel,
        "first",
        (tokens, own_part, from_t, middle_grads, gain_one[None]),
        [of_rows],
    )
    square = ((width, wide), f32)
    grad_query, grad_key, grad_value, grad_output, small = call(
        late_out_kernel,
        "late_out",
        (core[None], total, swap(total, "c")),
        [square, square, square, ((wide, width), f32), ((width, 128), f32)],
        smem=(0,),
    )
    grad_expert_gate, grad_expert_up, grad_expert_down = call(
        expert_out_kernel,
        "expert_out",
        (kept_u, from_next_t, kept_l, after(from_next_y, grad_query)),
        [((1, width, part), f32), ((1, width, part), f32), ((1, part, width), f32)],
    )
    return (
        block_out,
        grad_tokens,
        small[:, experts + 1],
        grad_query,
        grad_key,
        grad_value,
        grad_output,
        small[:, experts],
        small[:, :experts],
        grad_shared_gate,
        grad_shared_up,
        grad_shared_down,
        grad_expert_gate,
        grad_expert_up,
        grad_expert_down,
    )


def solution(mesh):
    fine = Mesh(mesh.devices.reshape(2, 4, 2, 2, 2, 2), AXES)
    placed = (
        P(EXPERT, None),
        P(EXPERT, None),
        P(),
        P(None, "t"),
        P(None, "t"),
        P(None, "t"),
        P("t", None),
        P(),
        P(),
        P(None, "t"),
        P(None, "t"),
        P("t", None),
        P(EXPERT, None, "t"),
        P(EXPERT, None, "t"),
        P(EXPERT, "t", None),
        P(EXPERT, None),
    )
    return jax.shard_map(
        local,
        mesh=fine,
        in_specs=placed,
        out_specs=(
            P(EXPERT, None),
            P(EXPERT, None),
            P(),
            P(None, "t"),
            P(None, "t"),
            P(None, "t"),
            P("t", None),
            P(),
            P(),
            P(None, "t"),
            P(None, "t"),
            P("t", None),
            P(EXPERT, None, "t"),
            P(EXPERT, None, "t"),
            P(EXPERT, "t", None),
        ),
        check_vma=False,
    )
```
